32 devices in a mesh: rows: 8 (over z, y), heads: 4 (over x, core).
Axes of the slice: x: 2, y: 2, z: 4, core: 2. Of those that a mesh axis runs over, the one named last changes fastest.
Arguments:
- tokens: bfloat16 [32768, 768], P('rows')
- cotangent: bfloat16 [32768, 768], P(('rows', 'heads')), may hold values from -6 to 6
- bucket: int32 [64], P('rows'), may hold values from 0 to 2, as said below
- lengths: int32 [64, 8], P('rows'), may hold values from 0 to 512, as said below
- in_weight: float32 [3, 768, 768], P(None, 'rows', 'heads'), may hold values from -0.21875 to 0.21875
- in_first: float32 [3, 768, 768], P(None, 'rows', 'heads'), may hold values from -0.00061035156 to 0.00061035156
- in_second: float32 [3, 768, 768], P(None, 'rows', 'heads'), may hold values from 1e-09 to 4e-09
- in_average: float32 [3, 768, 768], P(None, 'rows', 'heads'), may hold values from -0.21875 to 0.21875
- in_bias: float32 [2, 12, 64], P(None, 'heads', 'rows'), may hold values from -1.75 to 1.75
- bias_first: float32 [2, 12, 64], P(None, 'heads', 'rows'), may hold values from -0.0017089844 to 0.0017089844
- bias_second: float32 [2, 12, 64], P(None, 'heads', 'rows'), may hold values from 1e-08 to 4e-08
- bias_average: float32 [2, 12, 64], P(None, 'heads', 'rows'), may hold values from -1.75 to 1.75
- out_weight: float32 [768, 768], P(('rows', 'heads')), may hold values from -0.875 to 0.875
- out_first: float32 [768, 768], P(('rows', 'heads')), may hold values from -0.00061035156 to 0.00061035156
- out_second: float32 [768, 768], P(('rows', 'heads')), may hold values from 1e-09 to 4e-09
- out_average: float32 [768, 768], P(('rows', 'heads')), may hold values from -0.875 to 0.875
- up_weight: float32 [768, 3072], P(('rows', 'heads')), may hold values from -0.21875 to 0.21875
- up_first: float32 [768, 3072], P(('rows', 'heads')), may hold values from -0.00061035156 to 0.00061035156
- up_second: float32 [768, 3072], P(('rows', 'heads')), may hold values from 1e-09 to 4e-09
- up_average: float32 [768, 3072], P(('rows', 'heads')), may hold values from -0.21875 to 0.21875
- down_weight: float32 [3072, 768], P(('rows', 'heads')), may hold values from -0.109375 to 0.109375
- down_first: float32 [3072, 768], P(('rows', 'heads')), may hold values from -0.00061035156 to 0.00061035156
- down_second: float32 [3072, 768], P(('rows', 'heads')), may hold values from 1e-09 to 4e-09
- down_average: float32 [3072, 768], P(('rows', 'heads')), may hold values from -0.109375 to 0.109375
- vectors: float32 [7680], P(('rows', 'heads'))
- vec_first: float32 [7680], P(('rows', 'heads')), may hold values from -0.0017089844 to 0.0017089844
- vec_second: float32 [7680], P(('rows', 'heads')), may hold values from 1e-08 to 4e-08
- vec_average: float32 [7680], P(('rows', 'heads'))
Outputs:
- layer_out: bfloat16 [32768, 768], P(('rows', 'heads'))
- token_grad: float32 [32768, 768], P(('rows', 'heads'))
- grad_norm: float32 [], replicated
- in_weight_new: float32 [3, 768, 768], P(None, 'rows', 'heads')
- in_first_new: float32 [3, 768, 768], P(None, 'rows', 'heads')
- in_second_new: float32 [3, 768, 768], P(None, 'rows', 'heads')
- in_average_new: float32 [3, 768, 768], P(None, 'rows', 'heads')
- in_bias_new: float32 [2, 12, 64], P(None, 'heads', 'rows')
- bias_first_new: float32 [2, 12, 64], P(None, 'heads', 'rows')
- bias_second_new: float32 [2, 12, 64], P(None, 'heads', 'rows')
- bias_average_new: float32 [2, 12, 64], P(None, 'heads', 'rows')
- out_weight_new: float32 [768, 768], P(('rows', 'heads'))
- out_first_new: float32 [768, 768], P(('rows', 'heads'))
- out_second_new: float32 [768, 768], P(('rows', 'heads'))
- out_average_new: float32 [768, 768], P(('rows', 'heads'))
- up_weight_new: float32 [768, 3072], P(('rows', 'heads'))
- up_first_new: float32 [768, 3072], P(('rows', 'heads'))
- up_second_new: float32 [768, 3072], P(('rows', 'heads'))
- up_average_new: float32 [768, 3072], P(('rows', 'heads'))
- down_weight_new: float32 [3072, 768], P(('rows', 'heads'))
- down_first_new: float32 [3072, 768], P(('rows', 'heads'))
- down_second_new: float32 [3072, 768], P(('rows', 'heads'))
- down_average_new: float32 [3072, 768], P(('rows', 'heads'))
- vectors_new: float32 [7680], P(('rows', 'heads'))
- vec_first_new: float32 [7680], P(('rows', 'heads'))
- vec_second_new: float32 [7680], P(('rows', 'heads'))
- vec_average_new: float32 [7680], P(('rows', 'heads'))
The draws below stay inside these ranges and needn't reach their ends.
Inputs may be any that keep to these rules, and one draw needn't show every extreme that they name: Block b of 512 slots holds one slot row of 512 slots when bucket[b] is 0, rows of 128 slots filling it when 1, rows of 64 slots filling it when 2. Among the 8 blocks of each index of rows there is at least one of kind 0. lengths[b, r] is the number of live tokens at the start of slot row r of block b, 1 to that row's capacity for the rows that the block's kind has, and 0 for the entries beyond them. Among the blocks of each index of rows, one of kind 0 has its row full.
All inputs are finite; a program needn't handle non-finite values.
Results may differ from the reference program's by a relative error of at most 0.013.
The reference program's roundings to bfloat16 on the way count: a program that leaves them out, or rounds other values in their place, can miss the bound.
Values may be sent and summed in bfloat16 or wider, within the bound.
No kernel may reach another device: no remote copies, remote signals or barrier semaphores. Data moves between devices by JAX's collectives and lax.ppermute only.
A program may use at most 192 MiB of HBM per device.

```python
import math
import jax
import jax.numpy as jnp
from jax import lax

D = 768
H = 12
HD = 64
FF = 3072
CAP_L = 512
CAP_M = 128
CAP_S = 64
BLK_DEV = 8
STEP = 10
ROWS_BLK = 8
TOKENS = 32768
BLOCKS = 64
VEC = 7680
PARAMS = 7087104
N_ROWS = 8


def bucket_layout(key):
    kind_key, full_key, first_key, second_key = jax.random.split(key, 4)
    coarse = jax.random.randint(kind_key, (BLOCKS,), 0, 8)
    kinds = jnp.where(coarse == 0, 0, jnp.where(coarse < 3, 1, 2))
    chosen = jax.random.randint(full_key, (N_ROWS,), 0, BLK_DEV)
    block_place = jnp.arange(BLOCKS) % BLK_DEV
    owner_row = jnp.arange(BLOCKS) // BLK_DEV
    forced = block_place == chosen[owner_row]
    kinds = jnp.where(forced, 0, kinds).astype(jnp.int32)
    capacity = jnp.where(kinds == 0, CAP_L, jnp.where(kinds == 1, CAP_M, CAP_S))
    filled = jnp.where(kinds == 0, 1, jnp.where(kinds == 1, CAP_L // CAP_M, ROWS_BLK))
    first_draw = jax.random.randint(first_key, (BLOCKS, ROWS_BLK), 0, CAP_L)
    second_draw = jax.random.randint(second_key, (BLOCKS, ROWS_BLK), 0, CAP_L)
    shortfall = jnp.minimum(first_draw % capacity[:, None], second_draw % capacity[:, None])
    row_lengths = capacity[:, None] - shortfall
    slot_index = jnp.arange(ROWS_BLK)[None, :]
    row_lengths = jnp.where(slot_index < filled[:, None], row_lengths, 0)
    row_lengths = jnp.where((slot_index == 0) & forced[:, None], CAP_L, row_lengths)
    return (kinds, row_lengths.astype(jnp.int32))


def draw_bucket(key, part):
    kinds, row_lengths = bucket_layout(key)
    return kinds


def draw_lengths(key, part):
    kinds, row_lengths = bucket_layout(key)
    return row_lengths


def draw_tokens(key, part):
    key = jax.random.fold_in(key, 11)
    ramp = jnp.arange(D, dtype=jnp.float32) / (D - 1)
    base = jax.random.normal(key, (TOKENS, D), jnp.float32)
    scale_row = 0.55 * 3.0 ** ramp
    return (base * scale_row[None, :]).astype(jnp.bfloat16)


def vector_values(key, low_end, shift_scale):
    gain_key, shift_key = jax.random.split(key, 2)
    ramp = jnp.arange(D, dtype=jnp.float32) / (D - 1)
    gains = (low_end + ramp)[None, :] * jax.random.uniform(gain_key, (2, D), jnp.float32, 0.8, 1.2)
    shifts = jax.random.normal(shift_key, (4 * D + FF,), jnp.float32) * shift_scale
    return jnp.concatenate([shifts[:2 * D + FF], gains[0], shifts[2 * D + FF:3 * D + FF], gains[1], shifts[3 * D + FF:]])


def draw_vectors(key, part):
    key = jax.random.fold_in(key, 21)
    return vector_values(key, 0.5, 0.3)


def draw_vec_average(key, part):
    key = jax.random.fold_in(key, 22)
    return vector_values(key, 0.5, 0.3)


def block_scale(stream_key, dims, cuts, least, top_value):
    gain, own = 1.0, jax.random.fold_in(stream_key, 6)
    for dim, parts in cuts:
        steps = jnp.exp(jax.random.uniform(jax.random.fold_in(own, dim), (parts,), jnp.float32, least / len(cuts), top_value / len(cuts)))
        gain = gain * jnp.repeat(steps, dims[dim] // parts).reshape([-1 if axis == dim else 1 for axis in range(len(dims))])
    return gain


def gaussian(own_key, dims, width, bound, cuts=(), held_as=jnp.bfloat16):
    values = width * jax.random.normal(own_key, dims, jnp.float32)
    if cuts:
        values = values * block_scale(own_key, dims, cuts, -0.22, 0.18)
    return jnp.clip(values, -bound, bound).astype(held_as)


def setup_inputs(seed: int = 0) -> dict:
    key_of = jax.random.split(jax.random.key(seed), 29)
    tokens = draw_tokens(jax.random.fold_in(key_of[28], 71), 0)
    cotangent = gaussian(key_of[1], (TOKENS, D), 1.0, 6.0, ((0, 32),))
    bucket = draw_bucket(jax.random.fold_in(key_of[28], 71), 0)
    lengths = draw_lengths(jax.random.fold_in(key_of[28], 71), 0)
    in_weight = gaussian(key_of[4], (3, D, D), D ** -0.5, 0.21875, ((1, 8), (2, 4)), jnp.float32)
    in_first = gaussian(key_of[5], (3, D, D), 0.0001, 0.00061035156, ((1, 8), (2, 4)), jnp.float32)
    in_second = jnp.clip(jnp.exp(math.log(3.999999886872274e-09) - 1.3862944 * jax.random.uniform(key_of[6], (3, D, D), jnp.float32) ** block_scale(key_of[6], (3, D, D), ((1, 8), (2, 4)), -0.2, 0.2)), 9.999999717180685e-10, 3.999999886872274e-09)
    in_average = gaussian(key_of[7], (3, D, D), D ** -0.5, 0.21875, ((1, 8), (2, 4)), jnp.float32)
    in_bias = gaussian(key_of[8], (2, H, HD), 0.3, 1.75, ((1, 4), (2, 8)), jnp.float32)
    bias_first = gaussian(key_of[9], (2, H, HD), 0.0003, 0.0017089844, ((1, 4), (2, 8)), jnp.float32)
    bias_second = jnp.clip(jnp.exp(math.log(3.999999975690116e-08) - 1.3862944 * jax.random.uniform(key_of[10], (2, H, HD), jnp.float32) ** block_scale(key_of[10], (2, H, HD), ((1, 4), (2, 8)), -0.2, 0.2)), 9.99999993922529e-09, 3.999999975690116e-08)
    bias_average = gaussian(key_of[11], (2, H, HD), 0.3, 1.75, ((1, 4), (2, 8)), jnp.float32)
    out_weight = gaussian(key_of[12], (D, D), (D // 16) ** -0.5, 0.875, ((0, 32),), jnp.float32)
    out_first = gaussian(key_of[13], (D, D), 0.0001, 0.00061035156, ((0, 32),), jnp.float32)
    out_second = jnp.clip(jnp.exp(math.log(3.999999886872274e-09) - 1.3862944 * jax.random.uniform(key_of[14], (D, D), jnp.float32) ** block_scale(key_of[14], (D, D), ((0, 32),), -0.2, 0.2)), 9.999999717180685e-10, 3.999999886872274e-09)
    out_average = gaussian(key_of[15], (D, D), (D // 16) ** -0.5, 0.875, ((0, 32),), jnp.float32)
    up_weight = gaussian(key_of[16], (D, FF), D ** -0.5, 0.21875, ((0, 32),), jnp.float32)
    up_first = gaussian(key_of[17], (D, FF), 0.0001, 0.00061035156, ((0, 32),), jnp.float32)
    up_second = jnp.clip(jnp.exp(math.log(3.999999886872274e-09) - 1.3862944 * jax.random.uniform(key_of[18], (D, FF), jnp.float32) ** block_scale(key_of[18], (D, FF), ((0, 32),), -0.2, 0.2)), 9.999999717180685e-10, 3.999999886872274e-09)
    up_average = gaussian(key_of[19], (D, FF), D ** -0.5, 0.21875, ((0, 32),), jnp.float32)
    down_weight = gaussian(key_of[20], (FF, D), FF ** -0.5, 0.109375, ((0, 32),), jnp.float32)
    down_first = gaussian(key_of[21], (FF, D), 0.0001, 0.00061035156, ((0, 32),), jnp.float32)
    down_second = jnp.clip(jnp.exp(math.log(3.999999886872274e-09) - 1.3862944 * jax.random.uniform(key_of[22], (FF, D), jnp.float32) ** block_scale(key_of[22], (FF, D), ((0, 32),), -0.2, 0.2)), 9.999999717180685e-10, 3.999999886872274e-09)
    down_average = gaussian(key_of[23], (FF, D), FF ** -0.5, 0.109375, ((0, 32),), jnp.float32)
    vectors = draw_vectors(jax.random.fold_in(key_of[28], 71), 0)
    vec_first = gaussian(key_of[25], (VEC,), 0.0003, 0.0017089844, ((0, 32),), jnp.float32)
    vec_second = jnp.clip(jnp.exp(math.log(3.999999975690116e-08) - 1.3862944 * jax.random.uniform(key_of[26], (VEC,), jnp.float32) ** block_scale(key_of[26], (VEC,), ((0, 32),), -0.2, 0.2)), 9.99999993922529e-09, 3.999999975690116e-08)
    vec_average = draw_vec_average(jax.random.fold_in(key_of[28], 71), 0)
    return dict(tokens=tokens, cotangent=cotangent, bucket=bucket, lengths=lengths, in_weight=in_weight, in_first=in_first, in_second=in_second, in_average=in_average, in_bias=in_bias, bias_first=bias_first, bias_second=bias_second, bias_average=bias_average, out_weight=out_weight, out_first=out_first, out_second=out_second, out_average=out_average, up_weight=up_weight, up_first=up_first, up_second=up_second, up_average=up_average, down_weight=down_weight, down_first=down_first, down_second=down_second, down_average=down_average, vectors=vectors, vec_first=vec_first, vec_second=vec_second, vec_average=vec_average)


@jax.custom_vjp
def low(v):
    return lax.optimization_barrier(v.astype(jnp.bfloat16)).astype(jnp.float32)

@jax.custom_vjp
def low_back(v):
    return v

def low_keep(v):
    return (low(v), None)

def low_pass(kept, grad):
    return (grad,)

def back_keep(v):
    return (v, None)

def back_low(kept, grad):
    return (low(grad),)
low.defvjp(low_keep, low_pass)
low_back.defvjp(back_keep, back_low)
LN_EPS = 1e-05
LEARN_RATE = 0.1
VECTOR_RATE = 0.3
BETA_ONE = 0.9
BETA_TWO = 0.999
ADAM_EPS = 1e-08
WEIGHT_DECAY = 0.01
AVERAGE_KEEP = 0.75
CLIP_RMS = 0.001

def hmul(left, right):
    return jnp.dot(left, right, precision=lax.Precision.HIGHEST)

def layer_norm(values, scale_gain, shift_add):
    center = values - lax.optimization_barrier(jnp.mean(values, axis=-1, keepdims=True))
    spread = lax.optimization_barrier(jnp.mean(center * center, axis=-1, keepdims=True))
    return center * lax.rsqrt(spread + LN_EPS) * scale_gain + shift_add

def block_mask(block_kind, row_lengths):
    capacity = jnp.where(block_kind == 0, CAP_L, jnp.where(block_kind == 1, CAP_M, CAP_S)).astype(jnp.int32)
    position = jnp.arange(CAP_L, dtype=jnp.int32)
    row_index = position // capacity
    within = position - row_index * capacity
    slot_index = jnp.arange(ROWS_BLK, dtype=jnp.int32)
    live_length = lax.optimization_barrier(jnp.sum(jnp.where(row_index[:, None] == slot_index[None, :], row_lengths[None, :], 0), axis=1))
    is_valid = within < live_length
    return (row_index[:, None] == row_index[None, :]) & is_valid[None, :]

def split_vector(vec_values):
    split_points = [D, D + FF, 2 * D + FF, 3 * D + FF, 4 * D + FF, 5 * D + FF]
    return jnp.split(vec_values, split_points)

def group_forward(inputs, kinds, row_lengths, w_in, b_in, w_out, w_up, w_down, pieces):
    bias_out, bias_up, bias_down, gain_one, shift_one, gain_two, shift_two = pieces
    block_count = kinds.shape[0]
    queries = low(low_back(hmul(inputs, w_in[0]) + b_in[0]))
    key_rows = low(low_back(hmul(inputs, w_in[1])))
    values = low(low_back(hmul(inputs, w_in[2]) + b_in[1]))
    shape_four = (block_count, CAP_L, H, HD)
    scores = jnp.einsum('bqhd,bkhd->bhqk', queries.reshape(shape_four), key_rows.reshape(shape_four), precision=lax.Precision.HIGHEST) * HD ** (-0.5)
    scores = low_back(scores)
    key_masks = jax.vmap(block_mask)(kinds, row_lengths)
    scores = jnp.where(key_masks[:, None], scores, -1e+30)
    attention = low(jax.nn.softmax(scores, axis=-1))
    head_rows = jnp.einsum('bhqk,bkhd->bqhd', attention, values.reshape(shape_four), precision=lax.Precision.HIGHEST).reshape(block_count * CAP_L, D)
    head_rows = low(low_back(head_rows))
    branch = low_back(hmul(head_rows, w_out) + bias_out)
    first_out = layer_norm(inputs + branch, gain_one, shift_one)
    hidden_pre = low_back(hmul(low(first_out), w_up) + bias_up)
    hidden = low(jax.nn.gelu(hidden_pre, approximate=False))
    ffn_out = low_back(hmul(hidden, w_down) + bias_down)
    return layer_norm(first_out + ffn_out, gain_two, shift_two)

def forward(inputs, bucket, lengths, w_in, b_in, w_out, w_up, w_down, w_vec):
    w_in = low(w_in)
    b_in = low(b_in).reshape(2, D)
    w_out = low(w_out)
    w_up = low(w_up)
    w_down = low(w_down)
    pieces = split_vector(low(w_vec))
    group_blocks = 8
    group_count = BLOCKS // group_blocks

    def one_group(group_items):
        return group_forward(group_items[0], group_items[1], group_items[2], w_in, b_in, w_out, w_up, w_down, pieces)
    outputs = lax.map(jax.checkpoint(one_group), (inputs.reshape(group_count, group_blocks * CAP_L, D), bucket.reshape(group_count, group_blocks), lengths.reshape(group_count, group_blocks, ROWS_BLK)))
    return outputs.reshape(TOKENS, D)

def adam_update(weight, first, second, average, gradient, rate):
    first_new = BETA_ONE * first + (1.0 - BETA_ONE) * gradient
    second_new = BETA_TWO * second + (1.0 - BETA_TWO) * gradient * gradient
    first_hat = first_new / (1.0 - BETA_ONE ** STEP)
    second_hat = second_new / (1.0 - BETA_TWO ** STEP)
    weight_new = weight - rate * (first_hat / (jnp.sqrt(second_hat) + ADAM_EPS) + WEIGHT_DECAY * weight)
    average_new = AVERAGE_KEEP * average + (1.0 - AVERAGE_KEEP) * weight_new
    return (weight_new, first_new, second_new, average_new)

def reference(tokens, cotangent, bucket, lengths, in_weight, in_first, in_second, in_average, in_bias, bias_first, bias_second, bias_average, out_weight, out_first, out_second, out_average, up_weight, up_first, up_second, up_average, down_weight, down_first, down_second, down_average, vectors, vec_first, vec_second, vec_average):
    inputs = tokens.astype(jnp.float32)

    def layer(inputs_f, w_in, b_in, w_out, w_up, w_down, w_vec):
        return forward(inputs_f, bucket, lengths, w_in, b_in, w_out, w_up, w_down, w_vec)
    outputs, pullback = jax.vjp(layer, inputs, in_weight, in_bias, out_weight, up_weight, down_weight, vectors)
    gradients = pullback(cotangent.astype(jnp.float32))
    token_grad = gradients[0]
    square_sum = jnp.zeros((), jnp.float32)
    for gradient in gradients[1:]:
        square_sum = square_sum + jnp.sum(gradient * gradient)
    grad_norm = jnp.sqrt(square_sum)
    clip_limit = CLIP_RMS * math.sqrt(PARAMS)
    factor = clip_limit / jnp.maximum(grad_norm, clip_limit)
    in_new = adam_update(in_weight, in_first, in_second, in_average, gradients[1] * factor, LEARN_RATE)
    bias_new = adam_update(in_bias, bias_first, bias_second, bias_average, gradients[2] * factor, LEARN_RATE)
    out_new = adam_update(out_weight, out_first, out_second, out_average, gradients[3] * factor, LEARN_RATE)
    up_new = adam_update(up_weight, up_first, up_second, up_average, gradients[4] * factor, LEARN_RATE)
    down_new = adam_update(down_weight, down_first, down_second, down_average, gradients[5] * factor, LEARN_RATE)
    vec_new = adam_update(vectors, vec_first, vec_second, vec_average, gradients[6] * factor, VECTOR_RATE)
    return (outputs.astype(jnp.bfloat16), token_grad, grad_norm, in_new[0], in_new[1], in_new[2], in_new[3], bias_new[0], bias_new[1], bias_new[2], bias_new[3], out_new[0], out_new[1], out_new[2], out_new[3], up_new[0], up_new[1], up_new[2], up_new[3], down_new[0], down_new[1], down_new[2], down_new[3], vec_new[0], vec_new[1], vec_new[2], vec_new[3])
```

```python
from functools import partial
import math

import jax
import jax.numpy as jnp
from jax import lax
from jax.experimental import pallas as pl
from jax.experimental.pallas import tpu as pltpu
from jax.sharding import PartitionSpec as P

D = 768
HD = 64
FF = 3072
CAP_L = 512
CAP_M = 128
CAP_S = 64
STEP = 10
ROWS_BLK = 8
PARAMS = 7087104

LN_EPS = 1e-05
LEARN_RATE = 0.1
VECTOR_RATE = 0.3
BETA_ONE = 0.9
BETA_TWO = 0.999
ADAM_EPS = 1e-08
WEIGHT_DECAY = 0.01
AVERAGE_KEEP = 0.75
CLIP_RMS = 0.001

AXES = ("rows", "heads")
BF = jnp.bfloat16
F32 = jnp.float32
VMEM_BYTES = 58 * 1024 * 1024
GROUP = 256
HALF = D // 2
PACK_VEC = 16


def dot_nn(left, right):
    return lax.dot_general(left, right, (((1,), (0,)), ((), ())), preferred_element_type=F32)


def dot_nt(left, right):
    return lax.dot_general(left, right, (((1,), (1,)), ((), ())), preferred_element_type=F32)


def dot_tn(left, right):
    return lax.dot_general(left, right, (((0,), (0,)), ((), ())), preferred_element_type=F32)


def kernel_params(steps=1):
    return pltpu.CompilerParams(
        vmem_limit_bytes=VMEM_BYTES, dimension_semantics=("arbitrary",) * steps
    )


def whole(shape):
    return pl.BlockSpec(shape, lambda *_: (0,) * len(shape))


ANY = pl.BlockSpec(memory_space=pl.ANY)


class Place:
    def __init__(self):
        self.n_rows = lax.axis_size("rows")
        self.n_heads = lax.axis_size("heads")
        self.total = self.n_rows * self.n_heads
        self.sizes = {"z": self.n_rows // 2, "y": 2, "x": self.n_heads // 2, "c": 2}
        self.strides = {"c": 1, "x": 2, "y": self.n_heads, "z": 2 * self.n_heads}
        row, head = lax.axis_index("rows"), lax.axis_index("heads")
        self.z, self.y = row // 2, row % 2
        self.x, self.c = head // 2, head % 2

    def send(self, value, digit, shift=1):
        size, stride = self.sizes[digit], self.strides[digit]
        pairs = []
        for device in range(self.total):
            own = (device // stride) % size
            pairs.append((device, device + ((own + shift) % size - own) * stride))
        return lax.ppermute(value, AXES, pairs)


def gather_pieces(place, piece):
    z_size = place.sizes["z"]
    column = jnp.stack([piece] + [place.send(piece, "z", shift) for shift in range(1, z_size)])
    from_x = place.send(column, "x")
    from_y = place.send(column, "y")
    cut = z_size // 2
    diag_low = place.send(from_x[:cut], "y")
    diag_high = place.send(from_y[cut:], "x")
    shifts = tuple(range(z_size))
    near = [
        (column, shifts, 0, 0, 0),
        (from_x, shifts, 0, 1, 0),
        (from_y, shifts, 1, 0, 0),
        (diag_low, shifts[:cut], 1, 1, 0),
        (diag_high, shifts[cut:], 1, 1, 0),
    ]
    far = [(place.send(buffer, "c"), s, y, x, 1) for buffer, s, y, x, _ in near]
    return near + far


def pick(value, index, axis):
    return lax.dynamic_index_in_dim(value, index, axis, keepdims=False)


def add_low(left, right):
    return (left.astype(F32) + right.astype(F32)).astype(BF)


def scatter_pair(place, value, digit, axis):
    own = getattr(place, digit)
    received = place.send(pick(value, 1 - own, axis), digit)
    return add_low(pick(value, own, axis), received)


def scatter_column(place, value):
    size = place.sizes["z"]
    total = pick(value, place.z, 0).astype(F32)
    for shift in range(1, size):
        part = place.send(pick(value, (place.z + shift) % size, 0), "z", shift)
        total = total + part.astype(F32)
    return total


def scatter_chip(place, value, x_first):
    if x_first:
        value = scatter_pair(place, value, "x", 2)
        value = scatter_pair(place, value, "y", 1)
    else:
        value = scatter_pair(place, value, "y", 1)
        value = scatter_pair(place, value, "x", 1)
    return scatter_column(place, value)


def swap_halves(place, value, cut_axis, join_axis):
    size = value.shape[cut_axis] // 2
    keep = lax.dynamic_slice_in_dim(value, place.c * size, size, cut_axis)
    give = lax.dynamic_slice_in_dim(value, (1 - place.c) * size, size, cut_axis)
    got = place.send(give, "c")
    first = jnp.where(place.c == 0, keep, got)
    second = jnp.where(place.c == 0, got, keep)
    return jnp.concatenate([first, second], axis=join_axis)


def sum_all(place, value):
    for digit in ("c", "x", "y"):
        value = value + place.send(value, digit)
    own = value
    for shift in range(1, place.sizes["z"]):
        value = value + place.send(own, "z", shift)
    return value


def run_copies(copies):
    for copy in copies:
        copy.start()
    return copies


def finish_copies(copies):
    for copy in copies:
        copy.wait()


def piece_origin(place_ref, z_size, entry, index):
    _, shifts, y, x, c = entry
    shift = shifts[index]
    z_at = lax.rem(place_ref[0] + (z_size - shift), z_size)
    return z_at, place_ref[1] ^ y, place_ref[2] ^ x, place_ref[3] ^ c


def lane_half(rows):
    return lax.broadcasted_iota(jnp.int32, (rows, 2 * HD), 1) < HD


def attend_kernel(layout, place_ref, x_ref, bias_ref, keys_ref, ones_ref, *rest):
    entries, z_size = layout
    n_in = len(entries) if entries else 1
    sources = rest[:n_in]
    q_ref, k_ref, v_ref, o_ref, lse_ref, weight, sems = rest[n_in:]
    group = pl.program_id(0)

    @pl.when(group == 0)
    def _():
        copies = []
        if entries:
            for entry, source in zip(entries, sources):
                for index in range(len(entry[1])):
                    z_at, y_at, x_at, c_at = piece_origin(place_ref, z_size, entry, index)
                    row = pl.multiple_of((z_at * 2 + y_at) * 96 + c_at * 48, 16)
                    col = pl.multiple_of(x_at * HALF, 128)
                    for j in range(3):
                        copies.append(
                            pltpu.make_async_copy(
                                source.at[index, pl.ds(j * 48, 48), :],
                                weight.at[j, pl.ds(row, 48), pl.ds(col, HALF)],
                                sems.at[len(copies)],
                            )
                        )
        else:
            copies.append(pltpu.make_async_copy(sources[0], weight, sems.at[0]))
        finish_copies(run_copies(copies))

    x = x_ref[...]
    at = pl.multiple_of(group * GROUP, GROUP)
    for j, out in enumerate((q_ref, k_ref, v_ref)):
        out[...] = (dot_nn(x, weight[j, :, pl.ds(at, GROUP)]) + bias_ref[j]).astype(BF)
    low = lane_half(CAP_L)
    for block in range(x_ref.shape[0] // CAP_L):
        rows = slice(block * CAP_L, (block + 1) * CAP_L)
        key_mask, query_row = keys_ref[rows, :], ones_ref[rows, :]
        for pair in range(GROUP // 128):
            cols = slice(pair * 128, (pair + 1) * 128)
            q2, k2 = q_ref[rows, cols] * BF(HD ** -0.5), k_ref[rows, cols]
            v2t = v_ref[rows, cols].T
            outs = []
            for side in range(2):
                here = low if side == 0 else ~low
                s = dot_nt(jnp.where(here, k2, key_mask), jnp.where(here, q2, query_row))
                peak = jnp.max(s, axis=0, keepdims=True)
                e = jnp.exp(s - peak)
                total = jnp.sum(e, axis=0, keepdims=True)
                o = dot_nn(v2t[side * HD : (side + 1) * HD], e.astype(BF))
                outs.append(o * (1.0 / total))
                slot = (block * (GROUP // 128) + pair) * 2 + side
                lse_ref[0, slot : slot + 1, :] = peak + jnp.log(total)
            o_ref[rows, cols] = jnp.concatenate(outs, axis=0).T.astype(BF)


def attend(place_vec, x, bias, key_mask, query_row, entries, buffers, z_size):
    tokens = x.shape[0]
    groups = D // GROUP
    slots = tokens // CAP_L * (GROUP // HD)
    n_copies = sum(3 * len(entry[1]) for entry in entries) if entries else 1
    layout = (entries, z_size)
    shape = jax.ShapeDtypeStruct((tokens, D), BF)
    block = pl.BlockSpec((tokens, GROUP), lambda g, p: (0, g))
    return pl.pallas_call(
        partial(attend_kernel, layout),
        grid_spec=pltpu.PrefetchScalarGridSpec(
            num_scalar_prefetch=1,
            grid=(groups,),
            in_specs=[
                whole((tokens, D)),
                pl.BlockSpec((3, 1, GROUP), lambda g, p: (0, 0, g)),
                whole((tokens, 128)),
                whole((tokens, 128)),
            ]
            + [ANY] * len(buffers),
            out_specs=[block] * 4 + [pl.BlockSpec((1, slots, CAP_L), lambda g, p: (g, 0, 0))],
            scratch_shapes=[pltpu.VMEM((3, D, D), BF), pltpu.SemaphoreType.DMA((n_copies,))],
        ),
        out_shape=[shape] * 4 + [jax.ShapeDtypeStruct((groups, slots, CAP_L), F32)],
        compiler_params=kernel_params(),
        cost_estimate=pl.CostEstimate(
            flops=8 * tokens * D * D, bytes_accessed=12 * tokens * D, transcendentals=0
        ),
        name="attend",
    )(place_vec, x, bias, key_mask, query_row, *buffers)


def attend_back_kernel(q_ref, k_ref, v_ref, do_ref, lse_ref, keys_ref, ones_ref, dq_ref, dk_ref, dv_ref, sum_ref):
    low = lane_half(CAP_L)
    sum_ref[...] = jnp.zeros_like(sum_ref)
    for block in range(q_ref.shape[0] // CAP_L):
        rows = slice(block * CAP_L, (block + 1) * CAP_L)
        key_mask, query_row = keys_ref[rows, :], ones_ref[rows, :]
        for pair in range(GROUP // 128):
            cols = slice(pair * 128, (pair + 1) * 128)
            q2, k2 = q_ref[rows, cols] * BF(HD ** -0.5), k_ref[rows, cols]
            v2, do2 = v_ref[rows, cols], do_ref[rows, cols]
            k2t = k2.T
            dq_t, dk, dv = [], [], []
            for side in range(2):
                here = low if side == 0 else ~low
                slot = (block * (GROUP // 128) + pair) * 2 + side
                s = dot_nt(jnp.where(here, k2, key_mask), jnp.where(here, q2, query_row))
                p = jnp.exp(s - lse_ref[0, slot : slot + 1, :])
                dp = dot_nt(jnp.where(here, v2, BF(0)), do2)
                dv.append(dot_nn(p.astype(BF), do2))
                inner = jnp.sum(dp * p, axis=0, keepdims=True)
                ds = (p * (dp - inner)).astype(BF)
                dk.append(dot_nn(ds, q2))
                dq_t.append(dot_nn(k2t[side * HD : (side + 1) * HD], ds))
            dq_low = (jnp.concatenate(dq_t, axis=0).T * HD ** -0.5).astype(BF)
            dv_low = jnp.where(low, dv[0], dv[1]).astype(BF)
            dq_ref[rows, cols] = dq_low
            dk_ref[rows, cols] = jnp.where(low, dk[0], dk[1]).astype(BF)
            dv_ref[rows, cols] = dv_low
            sum_ref[0:1, cols] += jnp.sum(dq_low.astype(F32), axis=0, keepdims=True)
            sum_ref[1:2, cols] += jnp.sum(dv_low.astype(F32), axis=0, keepdims=True)


def attend_back(q, k, v, do, lse, key_mask, query_row):
    tokens = q.shape[0]
    groups, slots, _ = lse.shape
    block = pl.BlockSpec((tokens, GROUP), lambda g: (0, g))
    shape = jax.ShapeDtypeStruct((tokens, D), BF)
    return pl.pallas_call(
        attend_back_kernel,
        grid=(groups,),
        in_specs=[block] * 4
        + [pl.BlockSpec((1, slots, CAP_L), lambda g: (g, 0, 0)), whole((tokens, 128)), whole((tokens, 128))],
        out_specs=[block] * 3 + [pl.BlockSpec((2, GROUP), lambda g: (0, g))],
        out_shape=[shape] * 3 + [jax.ShapeDtypeStruct((2, D), F32)],
        compiler_params=kernel_params(),
        cost_estimate=pl.CostEstimate(
            flops=20 * tokens * D * CAP_L, bytes_accessed=14 * tokens * D, transcendentals=0
        ),
        name="attend_back",
    )(q, k, v, do, lse, key_mask, query_row)


TILE = 512
CHUNK = 768
ERF_P = 0.3275911 / math.sqrt(2.0)
ERF_A = (0.254829592, -0.284496736, 1.421413741, -1.453152027, 1.061405429)


def gelu_parts(u):
    bell = jnp.exp(u * u * -0.5)
    t = 1.0 / (1.0 + ERF_P * jnp.abs(u))
    poly = ERF_A[4] * 0.5
    for term in ERF_A[3::-1]:
        poly = poly * t + term * 0.5
    below = poly * t * bell
    phi = jnp.where(u >= 0.0, 1.0 - below, below)
    return u * phi, phi + u * bell * (1.0 / math.sqrt(2.0 * math.pi))


def normalise(values):
    center = values - jnp.mean(values, axis=-1, keepdims=True)
    scale = lax.rsqrt(jnp.mean(center * center, axis=-1, keepdims=True) + LN_EPS)
    return center * scale, scale


def norm_back(grad, gain, normal, scale):
    inner = grad * gain
    first = jnp.mean(inner, axis=-1, keepdims=True)
    second = jnp.mean(inner * normal, axis=-1, keepdims=True)
    return (inner - first - normal * second) * scale


def col_sum(values):
    return jnp.sum(values.astype(F32), axis=0, keepdims=True)


def layer_kernel(layout, place_ref, o_ref, x_ref, cot_ref, vec_ref, b1_ref, *rest):
    entries, z_size, n_heads = layout
    n_in = len(entries) + 1 if entries else 3
    sources = rest[:n_in]
    (
        z_ref, dr1_ref, yr_ref, hr_ref, dur_ref, dfr_ref, dar_ref, dor_ref, sums_ref, db1_ref,
        wo, w1, w2, slope, sems,
    ) = rest[n_in:]

    @pl.when(pl.program_id(0) == 0)
    def _():
        sums_ref[...] = jnp.zeros_like(sums_ref)
        db1_ref[...] = jnp.zeros_like(db1_ref)
        copies = []

        def add(source, target):
            copies.append(pltpu.make_async_copy(source, target, sems.at[len(copies)]))

        if entries:
            for entry, source in zip(entries, sources):
                for index in range(len(entry[1])):
                    z_at, y_at, x_at, c_at = piece_origin(place_ref, z_size, entry, index)
                    row = pl.multiple_of(((z_at * 2 + y_at) * (n_heads // 2) + x_at) * 48, 16)
                    col = pl.multiple_of(c_at * HALF, 128)
                    add(source.at[index, pl.ds(144, 48), :], wo.at[pl.ds(row, 48), pl.ds(col, HALF)])
            for device in range(sources[-1].shape[0]):
                chip, core = device // 2, device % 2
                for part in range(2):
                    add(
                        sources[-1].at[device, part * 48 : (part + 1) * 48, :],
                        w1.at[chip * 48 : (chip + 1) * 48, pl.ds(core * (FF // 2) + part * D, D)],
                    )
                add(sources[-1].at[device, 96:192, :], w2.at[device * 96 : (device + 1) * 96, :])
        else:
            for source, target in zip(sources, (wo, w1, w2)):
                add(source, target)
        finish_copies(run_copies(copies))

    bo, b2, g1, c1, g2, c2 = (vec_ref[i : i + 1, :] for i in range(6))
    r1 = x_ref[...].astype(F32) + (dot_nn(o_ref[...], wo[...]) + bo)
    n1, scale1 = normalise(r1)
    y1 = n1 * g1 + c1
    yr = y1.astype(BF)
    yr_ref[...] = yr
    f = None
    for at in range(0, FF, CHUNK):
        cols = slice(at, at + CHUNK)
        u = dot_nn(yr, w1[:, cols]) + b1_ref[:, cols]
        act, grad = gelu_parts(u)
        act = act.astype(BF)
        hr_ref[:, cols] = act
        slope[:, cols] = grad
        part = dot_nn(act, w2[cols, :])
        f = part if f is None else f + part
    n2, scale2 = normalise(y1 + (f + b2))
    z_ref[...] = (n2 * g2 + c2).astype(BF)
    dz = cot_ref[...].astype(F32)
    dr2 = norm_back(dz, g2, n2, scale2)
    dfr = dr2.astype(BF)
    dfr_ref[...] = dfr
    sums_ref[1:2, :] += col_sum(dfr)
    sums_ref[4:5, :] += col_sum(dz * n2)
    sums_ref[5:6, :] += col_sum(dz)
    dy1 = dr2
    for at in range(0, FF, CHUNK):
        cols = slice(at, at + CHUNK)
        dur = (dot_nt(dfr, w2[cols, :]) * slope[:, cols]).astype(BF)
        dur_ref[:, cols] = dur
        db1_ref[:, cols] += col_sum(dur)
        dy1 = dy1 + dot_nt(dur, w1[:, cols])
    dr1 = norm_back(dy1, g1, n1, scale1)
    dr1_ref[...] = dr1
    dar = dr1.astype(BF)
    dar_ref[...] = dar
    sums_ref[0:1, :] += col_sum(dar)
    sums_ref[2:3, :] += col_sum(dy1 * n1)
    sums_ref[3:4, :] += col_sum(dy1)
    dor_ref[...] = dot_nt(dar, wo[...]).astype(BF)


def layer(place_vec, o, x, cotangent, vec, b1, entries, buffers, z_size, n_heads):
    tokens = x.shape[0]
    n_copies = sum(len(e[1]) for e in entries) + 3 * buffers[-1].shape[0] if entries else 3
    tile = pl.BlockSpec((TILE, D), lambda t, p: (t, 0))
    wide = pl.BlockSpec((TILE, FF), lambda t, p: (t, 0))
    low, full = jax.ShapeDtypeStruct((tokens, D), BF), jax.ShapeDtypeStruct((tokens, D), F32)
    low_wide = jax.ShapeDtypeStruct((tokens, FF), BF)
    return pl.pallas_call(
        partial(layer_kernel, (entries, z_size, n_heads)),
        grid_spec=pltpu.PrefetchScalarGridSpec(
            num_scalar_prefetch=1,
            grid=(tokens // TILE,),
            in_specs=[tile, tile, tile, whole((8, D)), whole((1, FF))] + [ANY] * len(buffers),
            out_specs=[tile, tile, tile, wide, wide, tile, tile, tile, whole((8, D)), whole((1, FF))],
            scratch_shapes=[
                pltpu.VMEM((D, D), BF),
                pltpu.VMEM((D, FF), BF),
                pltpu.VMEM((FF, D), BF),
                pltpu.VMEM((TILE, FF), F32),
                pltpu.SemaphoreType.DMA((n_copies,)),
            ],
        ),
        out_shape=[
            low, full, low, low_wide, low_wide, low, low, low,
            jax.ShapeDtypeStruct((8, D), F32), jax.ShapeDtypeStruct((1, FF), F32),
        ],
        compiler_params=kernel_params(),
        cost_estimate=pl.CostEstimate(
            flops=tokens * D * (4 * D + 8 * FF), bytes_accessed=tokens * (20 * D + 4 * FF), transcendentals=0
        ),
        name="layer",
    )(place_vec, o, x, cotangent, vec, b1, *buffers)


def outer_kernel(left_ref, right_ref, out_ref):
    out_ref[...] = dot_tn(left_ref[...], right_ref[...]).astype(BF)


def outer(left, right, tile_left, tile_right, name):
    tokens, rows = left.shape
    cols = right.shape[1]
    return pl.pallas_call(
        outer_kernel,
        grid=(rows // tile_left, cols // tile_right),
        in_specs=[
            pl.BlockSpec((tokens, tile_left), lambda i, j: (0, i)),
            pl.BlockSpec((tokens, tile_right), lambda i, j: (0, j)),
        ],
        out_specs=pl.BlockSpec((tile_left, tile_right), lambda i, j: (i, j)),
        out_shape=jax.ShapeDtypeStruct((rows, cols), BF),
        compiler_params=kernel_params(2),
        cost_estimate=pl.CostEstimate(
            flops=2 * tokens * rows * cols, bytes_accessed=2 * (tokens * (rows + cols) + rows * cols), transcendentals=0
        ),
        name=name,
    )(left, right)


def outer_three_kernel(x_ref, q_ref, k_ref, v_ref, out_ref):
    x = x_ref[...]
    for j, ref in enumerate((q_ref, k_ref, v_ref)):
        out_ref[j] = dot_tn(x, ref[...]).astype(BF)


def outer_three(x, dq, dk, dv):
    tokens = x.shape[0]
    block = pl.BlockSpec((tokens, GROUP), lambda g: (0, g))
    return pl.pallas_call(
        outer_three_kernel,
        grid=(D // GROUP,),
        in_specs=[whole((tokens, D))] + [block] * 3,
        out_specs=pl.BlockSpec((3, D, GROUP), lambda g: (0, 0, g)),
        out_shape=jax.ShapeDtypeStruct((3, D, D), BF),
        compiler_params=kernel_params(),
        cost_estimate=pl.CostEstimate(
            flops=6 * tokens * D * D, bytes_accessed=8 * tokens * D + 6 * D * D, transcendentals=0
        ),
        name="grad_in",
    )(x, dq, dk, dv)


def input_grad_kernel(layout, place_ref, dr1_ref, dq_ref, dk_ref, dv_ref, *rest):
    entries, z_size = layout
    n_in = len(entries) if entries else 1
    sources = rest[:n_in]
    out_ref, weight, sems = rest[n_in:]

    @pl.when(pl.program_id(0) == 0)
    def _():
        copies = []
        if entries:
            for entry, source in zip(entries, sources):
                for index in range(len(entry[1])):
                    z_at, y_at, x_at, c_at = piece_origin(place_ref, z_size, entry, index)
                    row = pl.multiple_of((z_at * 2 + y_at) * 96 + c_at * 48, 16)
                    col = pl.multiple_of(x_at * HALF, 128)
                    for j in range(3):
                        copies.append(
                            pltpu.make_async_copy(
                                source.at[index, pl.ds(j * 48, 48), :],
                                weight.at[j, pl.ds(row, 48), pl.ds(col, HALF)],
                                sems.at[len(copies)],
                            )
                        )
        else:
            copies.append(pltpu.make_async_copy(sources[0], weight, sems.at[0]))
        finish_copies(run_copies(copies))

    total = dr1_ref[...]
    for j, ref in enumerate((dq_ref, dk_ref, dv_ref)):
        total = total + dot_nt(ref[...], weight[j])
    out_ref[...] = total


def input_grad(place_vec, dr1, dq, dk, dv, entries, buffers, z_size):
    tokens = dr1.shape[0]
    n_copies = sum(3 * len(entry[1]) for entry in entries) if entries else 1
    tile = pl.BlockSpec((TILE, D), lambda t, p: (t, 0))
    return pl.pallas_call(
        partial(input_grad_kernel, (entries, z_size)),
        grid_spec=pltpu.PrefetchScalarGridSpec(
            num_scalar_prefetch=1,
            grid=(tokens // TILE,),
            in_specs=[tile] * 4 + [ANY] * len(buffers),
            out_specs=tile,
            scratch_shapes=[pltpu.VMEM((3, D, D), BF), pltpu.SemaphoreType.DMA((n_copies,))],
        ),
        out_shape=jax.ShapeDtypeStruct((tokens, D), F32),
        compiler_params=kernel_params(),
        cost_estimate=pl.CostEstimate(
            flops=6 * tokens * D * D, bytes_accessed=14 * tokens * D + 6 * D * D, transcendentals=0
        ),
        name="input_grad",
    )(place_vec, dr1, dq, dk, dv, *buffers)


def mask_columns(kinds, lengths):
    capacity = jnp.where(kinds == 0, CAP_L, jnp.where(kinds == 1, CAP_M, CAP_S)).astype(jnp.int32)
    place = jnp.arange(CAP_L, dtype=jnp.int32)[None, :]
    row = place // capacity[:, None]
    within = place - row * capacity[:, None]
    lane = jnp.arange(2 * HD, dtype=jnp.int32) % HD
    same = row[:, :, None] == lane[None, None, :]
    padded = jnp.pad(lengths, ((0, 0), (0, HD - ROWS_BLK)))
    padded = jnp.concatenate([padded, padded], axis=1)
    live = same & (within[:, :, None] < padded[:, None, :])
    used = (lane < ROWS_BLK)[None, None, :]
    keys = jnp.where(live | ~used, 0.0, -1e30).astype(BF)
    queries = jnp.where(same & used, 1.0, 0.0).astype(BF)
    tokens = kinds.shape[0] * CAP_L
    return keys.reshape(tokens, 2 * HD), queries.reshape(tokens, 2 * HD)


def split_vector(vec_values):
    split_points = [D, D + FF, 2 * D + FF, 3 * D + FF, 4 * D + FF, 5 * D + FF]
    return jnp.split(vec_values, split_points)


def adam_update(weight, first, second, average, gradient, rate):
    first_new = BETA_ONE * first + (1.0 - BETA_ONE) * gradient
    second_new = BETA_TWO * second + (1.0 - BETA_TWO) * gradient * gradient
    first_hat = first_new / (1.0 - BETA_ONE**STEP)
    second_hat = second_new / (1.0 - BETA_TWO**STEP)
    weight_new = weight - rate * (
        first_hat / (jnp.sqrt(second_hat) + ADAM_EPS) + WEIGHT_DECAY * weight
    )
    average_new = AVERAGE_KEEP * average + (1.0 - AVERAGE_KEEP) * weight_new
    return (weight_new, first_new, second_new, average_new)


def body(
    tokens,
    cotangent,
    bucket,
    lengths,
    in_weight,
    in_first,
    in_second,
    in_average,
    in_bias,
    bias_first,
    bias_second,
    bias_average,
    out_weight,
    out_first,
    out_second,
    out_average,
    up_weight,
    up_first,
    up_second,
    up_average,
    down_weight,
    down_first,
    down_second,
    down_average,
    vectors,
    vec_first,
    vec_second,
    vec_average,
):
    place = Place()
    n_rows, n_heads, total = place.n_rows, place.n_heads, place.total
    z_size = place.sizes["z"]
    share = cotangent.shape[0]
    head_index = lax.axis_index("heads")
    place_vec = jnp.stack([place.z, place.y, place.x, place.c]).astype(jnp.int32)
    in_rows, in_cols = in_weight.shape[1], in_weight.shape[2]
    out_rows, down_rows = out_weight.shape[0], down_weight.shape[0]
    bias_len, vec_len = in_bias.size, vectors.size
    pieces_fit = in_rows == 96 and in_cols == HALF // 2 and out_rows == 24 and n_heads == 4

    small = jnp.concatenate([vectors, in_bias.reshape(-1)]).astype(BF)
    if pieces_fit:
        low_in = swap_halves(place, in_weight.astype(BF), 1, 2)
        low_out = swap_halves(place, out_weight.astype(BF), 1, 0)
        low_up = swap_halves(place, up_weight.astype(BF), 1, 0)
        small_rows = jnp.pad(small[None, :], ((0, PACK_VEC - 1), (0, HALF - small.size)))
        piece = jnp.concatenate([low_in.reshape(3 * 48, HALF), low_out, small_rows], axis=0)
        entries = gather_pieces(place, piece)
        ffn_piece = jnp.concatenate([low_up[:, :D], low_up[:, D:], down_weight.astype(BF)], axis=0)
        ffn_all = lax.all_gather(ffn_piece, AXES, axis=0)
        buffers = [entry[0] for entry in entries]
        layout = [(None,) + entry[1:] for entry in entries]
        in_buffers, layer_buffers = buffers, buffers + [ffn_all]
        found, origin = [], []
        for buffer, shifts, y, x, c in entries:
            for index, shift in enumerate(shifts):
                found.append(buffer[index, 3 * 48 + 48, : small.size])
                z_at = (place.z + z_size - shift) % z_size
                origin.append(
                    ((z_at * 2 + (place.y ^ y)) * 2 + (place.x ^ x)) * 2 + (place.c ^ c)
                )
        hit = jnp.stack(origin)[None, :] == jnp.arange(total, dtype=jnp.int32)[:, None]
        all_small = jnp.dot(hit.astype(BF), jnp.stack(found), preferred_element_type=F32)
    else:
        layout = ()
        all_in = lax.all_gather(in_weight.astype(BF), "rows", axis=1, tiled=True)
        all_in = lax.all_gather(all_in, "heads", axis=2, tiled=True)
        all_out, all_up, all_down = (
            lax.all_gather(w.astype(BF), AXES, axis=0, tiled=True)
            for w in (out_weight, up_weight, down_weight)
        )
        in_buffers, layer_buffers = [all_in], [all_out, all_up, all_down]
        all_small = lax.all_gather(small, AXES, axis=0).astype(F32)

    bias_out, bias_up, bias_down, gain_one, shift_one, gain_two, shift_two = split_vector(
        all_small[:, :vec_len].reshape(-1)
    )
    bias_shape = (n_rows, n_heads) + in_bias.shape
    bias_all = all_small[:, vec_len:].reshape(bias_shape).transpose(2, 1, 3, 0, 4).reshape(2, D)
    bias_in = jnp.stack([bias_all[0], jnp.zeros_like(bias_all[0]), bias_all[1]])[:, None, :]
    vec_rows = jnp.stack([bias_out, bias_down, gain_one, shift_one, gain_two, shift_two, bias_out, bias_out])

    x = lax.dynamic_slice_in_dim(tokens, head_index * share, share, 0)
    blocks = share // CAP_L
    own_kinds = lax.dynamic_slice_in_dim(bucket, head_index * blocks, blocks, 0)
    own_lengths = lax.dynamic_slice_in_dim(lengths, head_index * blocks, blocks, 0)
    key_mask, query_row = mask_columns(own_kinds, own_lengths)

    q, k, v, o, lse = attend(place_vec, x, bias_in, key_mask, query_row, layout, in_buffers, z_size)
    layer_out, dr1, yr, hr, dur, dfr, dar, dor, sums, db1 = layer(
        place_vec, o, x, cotangent, vec_rows, bias_up[None, :], layout, layer_buffers, z_size, n_heads
    )
    grad_down = outer(hr, dfr, D, D, "grad_down")
    grad_up = outer(yr, dur, D, D, "grad_up")
    grad_out = outer(o, dar, D, D // 2, "grad_out")
    dq, dk, dv, bias_sums = attend_back(q, k, v, dor, lse, key_mask, query_row)
    grad_in = outer_three(x, dq, dk, dv)
    token_grad = input_grad(place_vec, dr1, dq, dk, dv, layout, in_buffers, z_size)

    grad_vec = jnp.concatenate([sums[0], db1[0], sums[1], sums[2], sums[3], sums[4], sums[5]])
    grad_vec = grad_vec.reshape(total, vec_len)
    grad_bias = bias_sums.reshape(2, n_heads, in_bias.shape[1], n_rows, in_bias.shape[2])
    grad_bias = grad_bias.transpose(3, 1, 0, 2, 4).reshape(total, bias_len)
    grad_small = jnp.concatenate([grad_vec, grad_bias], axis=1)
    if pieces_fit:
        def core_pair(value, axis):
            return scatter_pair(place, value, "c", axis)

        down = core_pair(grad_down.reshape(z_size, 2, 2, 2, down_rows, D), 3)
        sum_down = scatter_chip(place, down, True)
        up = core_pair(grad_up.reshape(z_size, 2, 2, 48, 2, FF // 2), 4)
        sum_up = swap_halves(place, scatter_chip(place, up, False), 0, 1)
        send_out = grad_out.reshape(z_size, 2, 2, 48, 2, HALF)
        send_in = grad_in.reshape(3, z_size, 2, 2, 48, 2, HALF)
        send_small = jnp.pad(grad_small.astype(BF), ((0, 0), (0, HALF - small.size)))
        send_small = send_small.reshape(z_size, 2, 2, 2, 1, HALF)

        def packed(core):
            part_in = pick(send_in, core, 3).transpose(1, 2, 4, 0, 3, 5)
            part_in = part_in.reshape(z_size, 2, 2, 144, HALF)
            part_small = jnp.pad(pick(send_small, core, 3), ((0, 0),) * 3 + ((0, PACK_VEC - 1), (0, 0)))
            return jnp.concatenate([part_in, pick(send_out, core, 4), part_small], axis=3)

        mixed = add_low(packed(place.c), place.send(packed(1 - place.c), "c"))
        mixed = scatter_chip(place, mixed, True)
        sum_in = swap_halves(place, mixed[:144].reshape(3, 48, HALF), 2, 1)
        sum_out = swap_halves(place, mixed[144:192], 0, 1)
        sum_small = mixed[192, : small.size]
    else:
        def spread(value):
            return lax.psum_scatter(value, AXES, scatter_dimension=0, tiled=True).astype(F32)

        sum_in = lax.psum_scatter(grad_in, "heads", scatter_dimension=2, tiled=True)
        sum_in = lax.psum_scatter(sum_in, "rows", scatter_dimension=1, tiled=True).astype(F32)
        sum_out, sum_up, sum_down = spread(grad_out), spread(grad_up), spread(grad_down)
        sum_small = lax.psum_scatter(grad_small, AXES, scatter_dimension=0, tiled=True)[0]
    sum_vec = sum_small[:vec_len]
    sum_bias = sum_small[vec_len:].reshape(in_bias.shape)

    local_square = (
        jnp.sum(sum_in * sum_in)
        + jnp.sum(sum_out * sum_out)
        + jnp.sum(sum_up * sum_up)
        + jnp.sum(sum_down * sum_down)
        + jnp.sum(sum_small * sum_small)
    )
    grad_norm = jnp.sqrt(sum_all(place, local_square))
    clip_limit = CLIP_RMS * math.sqrt(PARAMS)
    factor = clip_limit / jnp.maximum(grad_norm, clip_limit)
    in_new = adam_update(in_weight, in_first, in_second, in_average, sum_in * factor, LEARN_RATE)
    bias_new = adam_update(
        in_bias, bias_first, bias_second, bias_average, sum_bias * factor, LEARN_RATE
    )
    out_new = adam_update(
        out_weight, out_first, out_second, out_average, sum_out * factor, LEARN_RATE
    )
    up_new = adam_update(up_weight, up_first, up_second, up_average, sum_up * factor, LEARN_RATE)
    down_new = adam_update(
        down_weight, down_first, down_second, down_average, sum_down * factor, LEARN_RATE
    )
    vec_new = adam_update(
        vectors, vec_first, vec_second, vec_average, sum_vec * factor, VECTOR_RATE
    )
    return (
        layer_out,
        token_grad,
        grad_norm,
        *in_new,
        *bias_new,
        *out_new,
        *up_new,
        *down_new,
        *vec_new,
    )


def solution(mesh):
    in_specs = (
        P("rows", None),
        P(("rows", "heads"), None),
        P("rows"),
        P("rows", None),
        P(None, "rows", "heads"),
        P(None, "rows", "heads"),
        P(None, "rows", "heads"),
        P(None, "rows", "heads"),
        P(None, "heads", "rows"),
        P(None, "heads", "rows"),
        P(None, "heads", "rows"),
        P(None, "heads", "rows"),
        P(("rows", "heads"), None),
        P(("rows", "heads"), None),
        P(("rows", "heads"), None),
        P(("rows", "heads"), None),
        P(("rows", "heads"), None),
        P(("rows", "heads"), None),
        P(("rows", "heads"), None),
        P(("rows", "heads"), None),
        P(("rows", "heads"), None),
        P(("rows", "heads"), None),
        P(("rows", "heads"), None),
        P(("rows", "heads"), None),
        P(("rows", "heads")),
        P(("rows", "heads")),
        P(("rows", "heads")),
        P(("rows", "heads")),
    )
    out_specs = (
        P(("rows", "heads"), None),
        P(("rows", "heads"), None),
        P(),
        P(None, "rows", "heads"),
        P(None, "rows", "heads"),
        P(None, "rows", "heads"),
        P(None, "rows", "heads"),
        P(None, "heads", "rows"),
        P(None, "heads", "rows"),
        P(None, "heads", "rows"),
        P(None, "heads", "rows"),
        P(("rows", "heads"), None),
        P(("rows", "heads"), None),
        P(("rows", "heads"), None),
        P(("rows", "heads"), None),
        P(("rows", "heads"), None),
        P(("rows", "heads"), None),
        P(("rows", "heads"), None),
        P(("rows", "heads"), None),
        P(("rows", "heads"), None),
        P(("rows", "heads"), None),
        P(("rows", "heads"), None),
        P(("rows", "heads"), None),
        P(("rows", "heads")),
        P(("rows", "heads")),
        P(("rows", "heads")),
        P(("rows", "heads")),
    )
    return jax.shard_map(body, mesh=mesh, in_specs=in_specs, out_specs=out_specs, check_vma=False)
```

```python
from functools import partial
import math

import jax
import jax.numpy as jnp
from jax import lax
from jax.experimental import pallas as pl
from jax.experimental.pallas import tpu as pltpu
from jax.sharding import PartitionSpec as P

D = 768
HD = 64
FF = 3072
CAP_L = 512
CAP_M = 128
CAP_S = 64
STEP = 10
ROWS_BLK = 8
PARAMS = 7087104

LN_EPS = 1e-05
LEARN_RATE = 0.1
VECTOR_RATE = 0.3
BETA_ONE = 0.9
BETA_TWO = 0.999
ADAM_EPS = 1e-08
WEIGHT_DECAY = 0.01
AVERAGE_KEEP = 0.75
CLIP_RMS = 0.001

AXES = ("rows", "heads")
BF = jnp.bfloat16
F32 = jnp.float32
VMEM_BYTES = 58 * 1024 * 1024
GROUP = 256
HALF = D // 2
PACK_VEC = 16


def dot_nn(left, right):
    return lax.dot_general(left, right, (((1,), (0,)), ((), ())), preferred_element_type=F32)


def dot_nt(left, right):
    return lax.dot_general(left, right, (((1,), (1,)), ((), ())), preferred_element_type=F32)


def dot_tn(left, right):
    return lax.dot_general(left, right, (((0,), (0,)), ((), ())), preferred_element_type=F32)


def kernel_params(steps=1):
    return pltpu.CompilerParams(
        vmem_limit_bytes=VMEM_BYTES, dimension_semantics=("arbitrary",) * steps
    )


def whole(shape):
    return pl.BlockSpec(shape, lambda *_: (0,) * len(shape))


ANY = pl.BlockSpec(memory_space=pl.ANY)


def call(kernel, place_vec, args, after, in_specs, out_specs, out_shape, grid, scratch, flops, name):
    def run(place_ref, *refs):
        return kernel(place_ref, *refs[len(after) :])

    return pl.pallas_call(
        run,
        grid_spec=pltpu.PrefetchScalarGridSpec(
            num_scalar_prefetch=1,
            grid=grid,
            in_specs=[ANY] * len(after) + in_specs,
            out_specs=out_specs,
            scratch_shapes=scratch,
        ),
        out_shape=out_shape,
        compiler_params=kernel_params(len(grid)),
        cost_estimate=pl.CostEstimate(flops=flops // 1000, bytes_accessed=1024, transcendentals=0),
        name=name,
    )(place_vec, *after, *args)


class Place:
    def __init__(self):
        self.n_rows = lax.axis_size("rows")
        self.n_heads = lax.axis_size("heads")
        self.total = self.n_rows * self.n_heads
        self.sizes = {"z": self.n_rows // 2, "y": 2, "x": self.n_heads // 2, "c": 2}
        self.strides = {"c": 1, "x": 2, "y": self.n_heads, "z": 2 * self.n_heads}
        row, head = lax.axis_index("rows"), lax.axis_index("heads")
        self.z, self.y = row // 2, row % 2
        self.x, self.c = head // 2, head % 2

    def send(self, value, digit, shift=1):
        size, stride = self.sizes[digit], self.strides[digit]
        pairs = []
        for device in range(self.total):
            own = (device // stride) % size
            pairs.append((device, device + ((own + shift) % size - own) * stride))
        return lax.ppermute(value, AXES, pairs)


def gather_pieces(place, piece):
    z_size = place.sizes["z"]
    column = jnp.stack([piece] + [place.send(piece, "z", shift) for shift in range(1, z_size)])
    from_x = place.send(column, "x")
    from_y = place.send(column, "y")
    cut = z_size // 2
    diag_low = place.send(from_x[:cut], "y")
    diag_high = place.send(from_y[cut:], "x")
    shifts = tuple(range(z_size))
    near = [
        (column, shifts, 0, 0, 0),
        (from_x, shifts, 0, 1, 0),
        (from_y, shifts, 1, 0, 0),
        (diag_low, shifts[:cut], 1, 1, 0),
        (diag_high, shifts[cut:], 1, 1, 0),
    ]
    far = [(place.send(buffer, "c"), s, y, x, 1) for buffer, s, y, x, _ in near]
    return near + far


def pick(value, index, axis):
    return lax.dynamic_index_in_dim(value, index, axis, keepdims=False)


def low_sum(*parts):
    return sum(part.astype(F32) for part in parts).astype(BF)


def trade(place, value):
    got = lax.all_to_all(value, "rows", split_axis=0, concat_axis=0, tiled=True)
    return jnp.sum(got.astype(F32), axis=0)


def swap_halves(place, value, cut_axis, join_axis):
    size = value.shape[cut_axis] // 2
    keep = lax.dynamic_slice_in_dim(value, place.c * size, size, cut_axis)
    give = lax.dynamic_slice_in_dim(value, (1 - place.c) * size, size, cut_axis)
    got = place.send(give, "c")
    first = jnp.where(place.c == 0, keep, got)
    second = jnp.where(place.c == 0, got, keep)
    return jnp.concatenate([first, second], axis=join_axis)


GIVE_ROWS = 144


def split_kernel(place_ref, in_ref, out_ref, up_ref, keep_ref, give_ref):
    zero = jnp.zeros((8, D), BF)
    for away, ref in enumerate((keep_ref, give_ref)):
        core = place_ref[3] ^ away
        for j in range(3):
            ref[0:48, j * 256 : j * 256 + 192] = in_ref[j, pl.ds(pl.multiple_of(core * 48, 8), 48), :].astype(BF)
            ref[0:48, j * 256 + 192 : (j + 1) * 256] = zero[:, :64].repeat(6, axis=0)
        ref[48:72, 0:HALF] = out_ref[:, pl.ds(pl.multiple_of(core * HALF, 128), HALF)].astype(BF)
        ref[48:72, HALF:] = jnp.zeros((24, HALF), BF)
        for t in range(2):
            col = pl.multiple_of(core * (FF // 2) + t * D, 128)
            ref[80 + t * 32 : 104 + t * 32, :] = up_ref[:, pl.ds(col, D)].astype(BF)
        for at in (72, 104, 136):
            ref[at : at + 8, :] = zero


def join_kernel(place_ref, keep_ref, got_ref, down_ref, small_ref, piece_ref, ffn_ref):
    first = place_ref[3] == 0
    keep, got = keep_ref[...], got_ref[...]
    low = jnp.where(first, keep, got)
    high = jnp.where(first, got, keep)
    for j in range(3):
        cols = slice(j * 256, j * 256 + 192)
        piece_ref[j * 48 : (j + 1) * 48, :] = jnp.concatenate([low[0:48, cols], high[0:48, cols]], axis=1)
    piece_ref[144:168, :] = low[48:72, :HALF]
    piece_ref[168:192, :] = high[48:72, :HALF]
    small = jnp.concatenate([small_ref[...], jnp.zeros((1, HALF - small_ref.shape[1]), F32)], axis=1)
    row = lax.broadcasted_iota(jnp.int32, (PACK_VEC, HALF), 0)
    piece_ref[192:208, :] = jnp.where(row == 0, small, 0.0).astype(BF)
    for t in range(2):
        ffn_ref[t * 48 : t * 48 + 24, :] = low[80 + t * 32 : 104 + t * 32, :]
        ffn_ref[t * 48 + 24 : t * 48 + 48, :] = high[80 + t * 32 : 104 + t * 32, :]
    ffn_ref[96:192, :] = down_ref[...].astype(BF)


def make_pieces(place, place_vec, in_weight, out_weight, up_weight, down_weight, small):
    half = jax.ShapeDtypeStruct((GIVE_ROWS, D), BF)
    weights = (in_weight, out_weight, up_weight)
    keep, give = call(
        split_kernel, place_vec, weights, (), [whole(w.shape) for w in weights],
        [whole(half.shape)] * 2, [half] * 2, (1,), [], 1000, "split",
    )
    operands = (keep, place.send(give, "c"), down_weight, small)
    shapes = [jax.ShapeDtypeStruct((208, HALF), BF), jax.ShapeDtypeStruct((192, D), BF)]
    return call(
        join_kernel, place_vec, operands, (), [whole(w.shape) for w in operands],
        [whole(w.shape) for w in shapes], shapes, (1,), [], 1000, "join",
    )


def run_copies(copies):
    for copy in copies:
        copy.start()
    return copies


def finish_copies(copies):
    for copy in copies:
        copy.wait()


def piece_origin(place_ref, z_size, entry, index):
    _, shifts, y, x, c = entry
    shift = shifts[index]
    z_at = lax.rem(place_ref[0] + (z_size - shift), z_size)
    return z_at, place_ref[1] ^ y, place_ref[2] ^ x, place_ref[3] ^ c


def mask_block(place_ref, block):
    kind = place_ref[4 + block * (ROWS_BLK + 1)]
    bits = jnp.where(kind == 0, 9, jnp.where(kind == 1, 7, 6))
    place = lax.broadcasted_iota(jnp.int32, (CAP_L, 2 * HD), 0)
    lane = lax.broadcasted_iota(jnp.int32, (1, 2 * HD), 1) % HD
    length = jnp.zeros((1, 2 * HD), jnp.int32)
    for row in range(ROWS_BLK):
        length = jnp.where(lane == row, place_ref[4 + block * (ROWS_BLK + 1) + 1 + row], length)
    row = lax.shift_right_logical(place, jnp.broadcast_to(bits, place.shape))
    within = place - lax.shift_left(row, jnp.broadcast_to(bits, place.shape))
    same = row == lane
    used = lane < ROWS_BLK
    closed = used & ~(same & (within < length))
    return jnp.where(closed, -1e30, 0.0).astype(BF), jnp.where(same & used, 1.0, 0.0).astype(BF)


def lane_half(rows):
    return lax.broadcasted_iota(jnp.int32, (rows, 2 * HD), 1) < HD


def div_mod(values, divisor):
    quotient = jnp.floor((values + 0.5) * (1.0 / divisor))
    return quotient, values - quotient * divisor


def counted(shape, axis):
    return lax.broadcasted_iota(jnp.int32, shape, axis).astype(F32)


def spread_small(small, lane_of, device_of):
    devices, lanes = small.shape
    column = counted((1, D), 1)
    hit = jnp.where(counted((lanes, D), 0) == lane_of(column), 1.0, 0.0).astype(BF)
    taken = jnp.where(counted((devices, D), 0) == device_of(column), dot_nn(small, hit), 0.0)
    return jnp.sum(taken, axis=0, keepdims=True)


def fill_small(small, vec_len, n_rows, bias_ref, vec_ref, b1_ref):
    n_heads = small.shape[0] // n_rows
    per_device = D // n_heads // HD
    width = HD // n_rows

    def bias_lane(j):
        def lane(col):
            head, place = div_mod(div_mod(col, per_device * HD)[1], HD)
            return vec_len + (j * per_device + head) * width + div_mod(place, width)[1]

        return lane

    def bias_device(col):
        return div_mod(div_mod(col, HD)[1], width)[0] * n_heads + div_mod(col, per_device * HD)[0]

    bias_ref[0] = spread_small(small, bias_lane(0), bias_device)
    bias_ref[1] = jnp.zeros((1, D), F32)
    bias_ref[2] = spread_small(small, bias_lane(1), bias_device)
    for index in range(10):
        start = index * D
        row = spread_small(small, lambda col: div_mod(start + col, vec_len)[1], lambda col: div_mod(start + col, vec_len)[0])
        if 1 <= index <= 4:
            b1_ref[:, (index - 1) * D : index * D] = row
        else:
            at = 0 if index == 0 else index - 4
            vec_ref[at : at + 1, :] = row


def attend_kernel(layout, place_ref, x_ref, *rest):
    entries, z_size, vec_len, n_rows = layout
    n_in = len(entries) if entries else 2
    sources = rest[:n_in]
    q_ref, k_ref, v_ref, o_ref, lse_ref, *more = rest[n_in:]
    if entries:
        vec_ref, b1_ref, whole_ref, weight, bias_ref, small, sems, sem_out = more
    else:
        weight, bias_ref, sems = more
    group = pl.program_id(0)

    @pl.when(group == 0)
    def _():
        copies = []
        if entries:
            for entry, source in zip(entries, sources):
                for index in range(len(entry[1])):
                    z_at, y_at, x_at, c_at = piece_origin(place_ref, z_size, entry, index)
                    row = pl.multiple_of((z_at * 2 + y_at) * 96 + c_at * 48, 16)
                    col = pl.multiple_of(x_at * HALF, 128)
                    device = ((z_at * 2 + y_at) * 2 + x_at) * 2 + c_at
                    copies.append(
                        pltpu.make_async_copy(
                            source.at[index, pl.ds(192, PACK_VEC), :], small.at[device], sems.at[len(copies)]
                        )
                    )
                    for j in range(3):
                        copies.append(
                            pltpu.make_async_copy(
                                source.at[index, pl.ds(j * 48, 48), :],
                                weight.at[j, pl.ds(row, 48), pl.ds(col, HALF)],
                                sems.at[len(copies)],
                            )
                        )
        else:
            copies.append(pltpu.make_async_copy(sources[0], weight, sems.at[0]))
            copies.append(pltpu.make_async_copy(sources[1], bias_ref, sems.at[1]))
        finish_copies(run_copies(copies))
        if entries:
            shares = jnp.sum(small[...].astype(F32), axis=1).astype(BF)
            fill_small(shares, vec_len, n_rows, bias_ref, vec_ref, b1_ref)
            pltpu.make_async_copy(weight, whole_ref, sem_out).start()

    if entries:

        @pl.when(group == pl.num_programs(0) - 1)
        def _():
            pltpu.make_async_copy(weight, whole_ref, sem_out).wait()

    x = x_ref[...]
    at = pl.multiple_of(group * GROUP, GROUP)
    for j, out in enumerate((q_ref, k_ref, v_ref)):
        out[...] = (dot_nn(x, weight[j, :, pl.ds(at, GROUP)]) + bias_ref[j, :, pl.ds(at, GROUP)]).astype(BF)
    low = lane_half(CAP_L)
    for block in range(x_ref.shape[0] // CAP_L):
        rows = slice(block * CAP_L, (block + 1) * CAP_L)
        key_mask, query_row = mask_block(place_ref, block)
        for pair in range(GROUP // 128):
            cols = slice(pair * 128, (pair + 1) * 128)
            q2, k2 = q_ref[rows, cols] * BF(HD ** -0.5), k_ref[rows, cols]
            v2t = v_ref[rows, cols].T
            outs = []
            for side in range(2):
                here = low if side == 0 else ~low
                s = dot_nt(jnp.where(here, k2, key_mask), jnp.where(here, q2, query_row))
                peak = jnp.max(s, axis=0, keepdims=True)
                e = jnp.exp(s - peak)
                total = jnp.sum(e, axis=0, keepdims=True)
                o = dot_nn(v2t[side * HD : (side + 1) * HD], e.astype(BF))
                outs.append(o * (1.0 / total))
                slot = block * 2 + side
                lse_ref[pair, slot : slot + 1, :] = peak + jnp.log(total)
            o_ref[rows, cols] = jnp.concatenate(outs, axis=0).T.astype(BF)


def own_tokens(tokens, tile):
    return pl.BlockSpec((tile, D), lambda t, p: ((p[2] * 2 + p[3]) * (tokens // tile) + (t if tile < tokens else 0), 0))


def attend(place_vec, x, tokens, entries, buffers, z_size, vec_len, n_rows):
    slots = tokens // CAP_L * 2
    block = pl.BlockSpec((tokens, GROUP), lambda g, p: (0, g))
    out_specs = [block] * 4 + [pl.BlockSpec((GROUP // 128, slots, CAP_L), lambda g, p: (g, 0, 0))]
    out_shape = [jax.ShapeDtypeStruct((tokens, D), BF)] * 4 + [jax.ShapeDtypeStruct((D // 128, slots, CAP_L), F32)]
    scratch = [pltpu.VMEM((3, D, D), BF), pltpu.VMEM((3, 1, D), F32)]
    n_copies = 2
    if entries:
        pieces = sum(len(entry[1]) for entry in entries)
        n_copies = 4 * pieces
        out_specs += [whole((8, D)), whole((1, FF)), ANY]
        out_shape += [jax.ShapeDtypeStruct((8, D), F32), jax.ShapeDtypeStruct((1, FF), F32)]
        out_shape += [jax.ShapeDtypeStruct((3, D, D), BF)]
        scratch += [pltpu.VMEM((pieces, PACK_VEC, HALF), BF)]
    return call(
        partial(attend_kernel, (entries, z_size, vec_len, n_rows)),
        place_vec,
        (x, *buffers),
        (),
        [own_tokens(tokens, tokens)] + [ANY] * len(buffers),
        out_specs,
        out_shape,
        (D // GROUP,),
        scratch + [pltpu.SemaphoreType.DMA((n_copies,))] + [pltpu.SemaphoreType.DMA] * bool(entries),
        10 * tokens * D * D,
        "attend",
    )


def small_bias(sums, vec_len, n_rows):
    width = HD // n_rows
    heads = HALF // 2 // HD
    out = 0.0
    col = counted((1, HALF), 1)
    mine = counted((2 * n_rows, HALF), 0) == div_mod(div_mod(col, HD)[1], width)[0] * 2 + div_mod(col, heads * HD)[0]
    head, place = div_mod(div_mod(counted((HALF, 1), 0), heads * HD)[1], HD)
    for j in range(2):
        hit = counted((HALF, HALF), 1) == vec_len + (j * heads + head) * width + div_mod(place, width)[1]
        spread = jnp.where(mine, sums[j : j + 1, :], 0.0).astype(BF)
        out = out + dot_nn(spread, jnp.where(hit, 1.0, 0.0).astype(BF))
    return out


def attend_back_kernel(
    layout, flip, place_ref, q_ref, k_ref, v_ref, do_ref, lse_ref, x_ref, vec_ref,
    dq_ref, dk_ref, dv_ref, *rest,
):
    z_size, split, vec_len = layout
    low = lane_half(CAP_L)
    sum_q, sum_v = [], []
    masks = [mask_block(place_ref, block) for block in range(q_ref.shape[0] // CAP_L)]
    for pair in range(HALF // 128):
        cols = slice(pair * 128, (pair + 1) * 128)
        pair_q, pair_v = 0.0, 0.0
        for block in range(q_ref.shape[0] // CAP_L):
            rows = slice(block * CAP_L, (block + 1) * CAP_L)
            key_mask, query_row = masks[block]
            q2, k2 = q_ref[rows, cols] * BF(HD ** -0.5), k_ref[rows, cols]
            v2, do2 = v_ref[rows, cols], do_ref[rows, cols]
            k2t = k2.T
            dq_t, dk, dv = [], [], []
            for side in range(2):
                here = low if side == 0 else ~low
                slot = block * 2 + side
                s = dot_nt(jnp.where(here, k2, key_mask), jnp.where(here, q2, query_row))
                p = jnp.exp(s - lse_ref[pair, slot : slot + 1, :])
                dp = dot_nt(jnp.where(here, v2, BF(0)), do2)
                dv.append(dot_nn(p.astype(BF), do2))
                inner = jnp.sum(dp * p, axis=0, keepdims=True)
                ds = (p * (dp - inner)).astype(BF)
                dk.append(dot_nn(ds, q2))
                dq_t.append(dot_nn(k2t[side * HD : (side + 1) * HD], ds))
            dq_low = (jnp.concatenate(dq_t, axis=0).T * HD ** -0.5).astype(BF)
            dv_low = jnp.where(low, dv[0], dv[1]).astype(BF)
            dq_ref[rows, cols] = dq_low
            dk_ref[rows, cols] = jnp.where(low, dk[0], dk[1]).astype(BF)
            dv_ref[rows, cols] = dv_low
            pair_q = pair_q + col_sum(dq_low)
            pair_v = pair_v + col_sum(dv_low)
        sum_q.append(pair_q)
        sum_v.append(pair_v)
    x = x_ref[...]
    sums = jnp.concatenate([jnp.concatenate(sum_q, axis=1), jnp.concatenate(sum_v, axis=1)], axis=0)
    if not split:
        grad_ref, bias_ref = rest
        bias_ref[...] = sums
        for j, ref in enumerate((dq_ref, dk_ref, dv_ref)):
            grad_ref[j] = dot_tn(x, ref[...]).astype(BF)
        return
    *grad_refs, held, held_small, sems = rest
    held_small[...] = (vec_ref[0] + small_bias(sums, vec_len, 2 * z_size)).astype(BF)
    copies = []

    def scatter(source, rows, step):
        for row in range(2 * z_size):
            for away in range(2):
                core = place_ref[3] ^ away
                copies.append(
                    pltpu.make_async_copy(source(row, core), grad_refs[away].at[row, rows], sems.at[step, row * 2 + away])
                )
                copies[-1].start()

    scatter(lambda row, core: held_small, pl.ds(144, SMALL_ROWS), 3)
    for j, ref in enumerate((dq_ref, dk_ref, dv_ref)):
        held[j] = dot_tn(x, ref[...]).astype(BF)
        scatter(
            lambda row, core: held.at[j, pl.ds(pl.multiple_of(row * 96 + core * 48, 16), 48)], pl.ds(j * 48, 48), j
        )
    finish_copies(copies)


SMALL_ROWS = 16


def attend_back(place_vec, q, k, v, do, lse, x, vec, vec_len, z_size, split, flip, after):
    tokens = q.shape[0]
    slots = lse.shape[1]

    def half(g, p):
        return (0, (p[2] % 2) ^ flip)

    block = pl.BlockSpec((tokens, HALF), half)
    out_shape = [jax.ShapeDtypeStruct((tokens, HALF), BF)] * 3
    out_specs = [whole((tokens, HALF))] * 3
    if split:
        out_shape += [jax.ShapeDtypeStruct((2 * z_size, 144 + SMALL_ROWS, HALF), BF)] * 2
        out_specs += [ANY] * 2
        scratch = [
            pltpu.VMEM((3, D, HALF), BF),
            pltpu.VMEM((SMALL_ROWS, HALF), BF),
            pltpu.SemaphoreType.DMA((4, 4 * z_size)),
        ]
    else:
        out_shape += [jax.ShapeDtypeStruct((3, D, HALF), BF), jax.ShapeDtypeStruct((2, HALF), F32)]
        out_specs += [whole((3, D, HALF)), whole((2, HALF))]
        scratch = []
    return call(
        partial(attend_back_kernel, (z_size, split, vec_len), flip),
        place_vec,
        (q, k, v, do, lse, x, vec),
        after,
        [block] * 4
        + [pl.BlockSpec((HALF // 128, slots, CAP_L), lambda g, p: ((p[2] % 2) ^ flip, 0, 0))]
        + [own_tokens(tokens, tokens), pl.BlockSpec((1, SMALL_ROWS, HALF), lambda g, p: ((p[2] % 2) ^ flip, 0, 0))],
        out_specs,
        out_shape,
        (1,),
        scratch,
        14 * tokens * D * D,
        "attend_back",
    )


TILE = 256
CHUNK = 768
ERF_P = 0.3275911 / math.sqrt(2.0)
ERF_A = (0.254829592, -0.284496736, 1.421413741, -1.453152027, 1.061405429)
BELL_RATE = -0.5 * math.log2(math.e)
BELL_SCALE = 1.0 / math.sqrt(2.0 * math.pi)


def gelu_parts(u):
    bell = jnp.exp2(u * u * BELL_RATE)
    scale = 1.0 + ERF_P * jnp.abs(u)
    t = pl.reciprocal(scale, approx=True)
    t = t * (2.0 - scale * t)
    poly = ERF_A[4] * 0.5
    for term in ERF_A[3::-1]:
        poly = poly * t + term * 0.5
    below = poly * t * bell
    phi = jnp.where(u >= 0.0, 1.0 - below, below)
    return u * phi, phi + u * bell * BELL_SCALE


def normalise(values):
    center = values - jnp.mean(values, axis=-1, keepdims=True)
    scale = lax.rsqrt(jnp.mean(center * center, axis=-1, keepdims=True) + LN_EPS)
    return center * scale, scale


def norm_back(grad, gain, normal, scale):
    inner = grad * gain
    first = jnp.mean(inner, axis=-1, keepdims=True)
    second = jnp.mean(inner * normal, axis=-1, keepdims=True)
    return (inner - first - normal * second) * scale


def col_sum(values):
    return jnp.sum(values.astype(F32), axis=0, keepdims=True)


def ffn_copies(layout, place_ref, sources, wo, w1, w2, sems):
    entries, z_size, n_heads = layout
    count = [0]

    def copy(source, target):
        made = pltpu.make_async_copy(source, target, sems.at[count[0]])
        count[0] += 1
        made.start()
        return made

    if not entries:
        return [[copy(source, target)] for source, target in zip(sources, (wo, w1, w2))]
    to_out, to_up, to_down = [], [], []
    for entry, source in zip(entries, sources):
        for index in range(len(entry[1])):
            z_at, y_at, x_at, c_at = piece_origin(place_ref, z_size, entry, index)
            row = pl.multiple_of(((z_at * 2 + y_at) * (n_heads // 2) + x_at) * 48, 16)
            col = pl.multiple_of(c_at * HALF, 128)
            to_out.append(copy(source.at[index, pl.ds(144, 48), :], wo.at[pl.ds(row, 48), pl.ds(col, HALF)]))
    for device in range(sources[-1].shape[0]):
        chip, core = device // 2, device % 2
        for part in range(2):
            to_up.append(
                copy(
                    sources[-1].at[device, part * 48 : (part + 1) * 48, :],
                    w1.at[chip * 48 : (chip + 1) * 48, pl.ds(core * (FF // 2) + part * D, D)],
                )
            )
    for device in range(sources[-1].shape[0]):
        to_down.append(copy(sources[-1].at[device, 96:192, :], w2.at[device * 96 : (device + 1) * 96, :]))
    return to_out, to_up, to_down


def layer_kernel(layout, place_ref, o_ref, x_ref, cot_ref, vec_ref, b1_ref, *rest):
    n_in = len(layout[0]) + 1 if layout[0] else 3
    sources = rest[:n_in]
    z_ref, dr1_ref, yr_ref, dur_ref, dor_ref, sums_ref, db1_ref, *grad_refs = rest[n_in:-10]
    wo, w1, w2, hr, slope, dfr_all, dar_all, held, sems, sems_out = rest[-10:]
    step = pl.program_id(0)

    @pl.when(step == 0)
    def _():
        sums_ref[...] = jnp.zeros_like(sums_ref)
        db1_ref[...] = jnp.zeros_like(db1_ref)
        for copies in ffn_copies(layout, place_ref, sources, wo, w1, w2, sems):
            finish_copies(copies)

    bo, b2, g1, c1, g2, c2 = (vec_ref[i : i + 1, :] for i in range(6))
    at_rows = pl.ds(pl.multiple_of(step * TILE, TILE), TILE)
    r1 = x_ref[...].astype(F32) + (dot_nn(o_ref[at_rows, :], wo[...]) + bo)
    n1, scale1 = normalise(r1)
    y1 = n1 * g1 + c1
    yr = y1.astype(BF)
    yr_ref[...] = yr
    f = None
    for at in range(0, FF, CHUNK):
        cols = slice(at, at + CHUNK)
        u = dot_nn(yr, w1[:, cols]) + b1_ref[:, cols]
        act, rate = gelu_parts(u)
        act = act.astype(BF)
        hr[at_rows, cols] = act
        slope[:, cols] = rate
        part = dot_nn(act, w2[cols, :])
        f = part if f is None else f + part
    n2, scale2 = normalise(y1 + (f + b2))
    z_ref[...] = (n2 * g2 + c2).astype(BF)
    dz = cot_ref[...].astype(F32)
    dr2 = norm_back(dz, g2, n2, scale2)
    dfr = dr2.astype(BF)
    dfr_all[at_rows, :] = dfr
    sums_ref[1:2, :] += col_sum(dfr)
    sums_ref[4:5, :] += col_sum(dz * n2)
    sums_ref[5:6, :] += col_sum(dz)
    dy1 = dr2
    for at in range(0, FF, CHUNK):
        cols = slice(at, at + CHUNK)
        dur = (dot_nt(dfr, w2[cols, :]) * slope[:, cols]).astype(BF)
        dur_ref[:, cols] = dur
        db1_ref[:, cols] += col_sum(dur)
        dy1 = dy1 + dot_nt(dur, w1[:, cols])
    dr1 = norm_back(dy1, g1, n1, scale1)
    dr1_ref[...] = dr1
    dar = dr1.astype(BF)
    dar_all[at_rows, :] = dar
    sums_ref[0:1, :] += col_sum(dar)
    sums_ref[2:3, :] += col_sum(dy1 * n1)
    sums_ref[3:4, :] += col_sum(dy1)
    dor_ref[...] = dot_nt(dar, wo[...]).astype(BF)

    @pl.when(step == pl.num_programs(0) - 1)
    def _():
        pending = [[], []]
        for index in range(FF // D + 1):
            slot = index % 2
            finish_copies(pending[slot])
            if index < FF // D:
                held[slot] = dot_tn(hr[:, index * D : (index + 1) * D], dfr_all[...]).astype(BF)
            else:
                held[slot] = dot_tn(o_ref[...], dar_all[...]).astype(BF)
            pending[slot] = layer_copies(layout, place_ref, held.at[slot], grad_refs, index, sems_out.at[slot])
        for copies in pending:
            finish_copies(copies)


def piece_target(grad_refs, away, flip, row):
    near, far, far_other = grad_refs
    return near.at[flip, row] if not away else (far_other if flip else far).at[row]


def layer_copies(layout, place_ref, held, grad_refs, index, sems):
    is_out = index == FF // D
    if not layout[0]:
        target = grad_refs[1] if is_out else grad_refs[0].at[pl.ds(index * D, D), :]
        return run_copies([pltpu.make_async_copy(held, target, sems.at[0])])
    copies = []

    def add(source, target):
        copies.append(pltpu.make_async_copy(source, target, sems.at[len(copies)]))

    for away in range(2):
        core = place_ref[3] ^ away
        for flip in range(2):
            x = place_ref[2] ^ flip
            if is_out:
                col = pl.multiple_of(core * HALF, 128)
                for row in range(2 * layout[1]):
                    at = pl.multiple_of((row * 2 + x) * 48, 16)
                    target = piece_target(grad_refs, away, flip, row)
                    add(held.at[pl.ds(at, 48), pl.ds(col, HALF)], target.at[pl.ds(192, 48), :])
            else:
                for part in range(2):
                    at = pl.multiple_of((part * 2 + x) * 192 + core * 96, 16)
                    target = piece_target(grad_refs, away, flip, index * 2 + part)
                    for half in range(2):
                        add(held.at[pl.ds(at, 96), pl.ds(half * HALF, HALF)], target.at[pl.ds(half * 96, 96), :])
    return run_copies(copies)


def piece_shapes(z_size, rows):
    piece = (2 * z_size, rows, HALF)
    return [jax.ShapeDtypeStruct((2, *piece), BF)] + [jax.ShapeDtypeStruct(piece, BF)] * 2


def layer(place_vec, o, x, cotangent, vec, b1, entries, buffers, z_size, n_heads):
    tokens = o.shape[0]
    n_copies = sum(len(e[1]) for e in entries) + 3 * buffers[-1].shape[0] if entries else 3
    tile = pl.BlockSpec((TILE, D), lambda t, p: (t, 0))
    wide = pl.BlockSpec((TILE, FF), lambda t, p: (t, 0))
    low, full = jax.ShapeDtypeStruct((tokens, D), BF), jax.ShapeDtypeStruct((tokens, D), F32)
    if entries:
        grads = piece_shapes(z_size, 240)
    else:
        grads = [jax.ShapeDtypeStruct((FF, D), BF), jax.ShapeDtypeStruct((D, D), BF)]
    return call(
        partial(layer_kernel, (entries, z_size, n_heads)),
        place_vec,
        (o, x, cotangent, vec, b1, *buffers),
        (),
        [whole((tokens, D)), own_tokens(tokens, TILE), tile, whole((8, D)), whole((1, FF))] + [ANY] * len(buffers),
        [tile, tile, tile, wide, tile, whole((8, D)), whole((1, FF))] + [ANY] * len(grads),
        [
            low, full, low, jax.ShapeDtypeStruct((tokens, FF), BF), low,
            jax.ShapeDtypeStruct((8, D), F32), jax.ShapeDtypeStruct((1, FF), F32), *grads,
        ],
        (tokens // TILE,),
        [
            pltpu.VMEM((D, D), BF),
            pltpu.VMEM((D, FF), BF),
            pltpu.VMEM((FF, D), BF),
            pltpu.VMEM((tokens, FF), BF),
            pltpu.VMEM((TILE, FF), F32),
            pltpu.VMEM((tokens, D), BF),
            pltpu.VMEM((tokens, D), BF),
            pltpu.VMEM((2, D, D), BF),
            pltpu.SemaphoreType.DMA((n_copies,)),
            pltpu.SemaphoreType.DMA((2, 32)),
        ],
        tokens * D * (6 * D + 10 * FF),
        "layer",
    )


def small_vectors(sums, db1, vec_len, devices):
    rows = [sums[0:1, :]] + [db1[:, at : at + D] for at in range(0, FF, D)]
    rows += [sums[i : i + 1, :] for i in range(1, 6)]
    out = 0.0
    for index, row in enumerate(rows):
        owner = div_mod(counted((1, D), 1) + index * D, vec_len)[0]
        spread = jnp.where(counted((devices, D), 0) == owner, row, 0.0).astype(BF)
        lane = div_mod(counted((D, 1), 0) + index * D, vec_len)[1]
        out = out + dot_nn(spread, jnp.where(counted((D, HALF), 1) == lane, 1.0, 0.0).astype(BF))
    return out


def grad_up_kernel(layout, place_ref, yr_ref, sums_ref, db1_ref, dur_ref, *rest):
    if not layout[0]:
        rest[0][...] = dot_tn(yr_ref[...], dur_ref[...]).astype(BF)
        return
    *grad_refs, small_ref, held, sems = rest
    step = pl.program_id(0)

    def up(index):
        slot = index % 2
        away = 1 - index // 2
        made = []
        for flip in range(2):
            x = place_ref[2] ^ flip
            for row in range(2 * layout[1]):
                at = pl.multiple_of((row * 2 + x) * 48, 16)
                target = piece_target(grad_refs, away, flip, row)
                for part in range(2):
                    source = held.at[slot, pl.ds(at, 48), pl.ds(part * HALF, HALF)]
                    used = sems.at[slot, part, flip * 2 * layout[1] + row]
                    made.append(pltpu.make_async_copy(source, target.at[pl.ds((slot * 2 + part) * 48, 48), :], used))
        return made

    steps = FF // D
    for index in range(steps):

        @pl.when(step == index)
        def _():
            if index == 0:
                rows = small_vectors(sums_ref, db1_ref, layout[2], 2 * SMALL_ROWS)
                device = lax.broadcasted_iota(jnp.int32, rows.shape, 0)
                for x in range(2):
                    kept = jnp.where((device // 2) % 2 == x, rows, 0.0)
                    source = lax.broadcasted_iota(jnp.int32, (SMALL_ROWS, rows.shape[0]), 1)
                    target = lax.broadcasted_iota(jnp.int32, (SMALL_ROWS, rows.shape[0]), 0)
                    take = (source == (target // 2) * 4 + x * 2 + target % 2).astype(F32)
                    small_ref[x] = dot_nn(take.astype(BF), kept.astype(BF))
            if index >= 2:
                finish_copies(up(index - 2))
            held[index % 2] = dot_tn(yr_ref[...], dur_ref[...]).astype(BF)
            run_copies(up(index))
            if index == steps - 1:
                finish_copies(up(index - 1))
                finish_copies(up(index))


def grad_up(place_vec, yr, sums, db1, dur, entries, z_size, vec_len, after):
    tokens = yr.shape[0]
    if entries:
        shapes = piece_shapes(z_size, 192) + [jax.ShapeDtypeStruct((2, SMALL_ROWS, HALF), F32)]
        specs = [ANY] * 3 + [whole((2, SMALL_ROWS, HALF))]

        def columns(g, p):
            return (0, (p[3] ^ (1 - g // 2)) * 2 + g % 2)
    else:
        shapes = [jax.ShapeDtypeStruct((D, FF), BF)]
        specs = [pl.BlockSpec((D, D), lambda g, p: (0, g))]

        def columns(g, p):
            return (0, g)

    return call(
        partial(grad_up_kernel, (entries, z_size, vec_len)),
        place_vec,
        (yr, sums, db1, dur),
        after,
        [whole((tokens, D)), whole((8, D)), whole((1, FF)), pl.BlockSpec((tokens, D), columns)],
        specs,
        shapes,
        (FF // D,),
        [pltpu.VMEM((2, D, D), BF), pltpu.SemaphoreType.DMA((2, 2, 4 * z_size))] if entries else [],
        2 * tokens * D * FF,
        "grad_up",
    )


def input_grad_kernel(place_ref, base_ref, weight_ref, *rest):
    *grads, out_ref = rest
    total = base_ref[...]
    for flip in range(2):
        col = pl.multiple_of(((place_ref[2] % 2) ^ flip) * HALF, 128)
        for j in range(3):
            total = total + dot_nt(grads[flip * 3 + j][...], weight_ref[j, :, pl.ds(col, HALF)])
    out_ref[...] = total


def input_grad(place_vec, base, near, far, weight, after):
    tokens = base.shape[0]
    tile = pl.BlockSpec((TILE, D), lambda t, p: (t, 0))
    half = pl.BlockSpec((TILE, HALF), lambda t, p: (t, 0))
    return call(
        input_grad_kernel,
        place_vec,
        (base, weight, *near, *far),
        after,
        [tile, whole((3, D, D))] + [half] * 6,
        tile,
        jax.ShapeDtypeStruct((tokens, D), F32),
        (tokens // TILE,),
        [],
        6 * tokens * D * D,
        "input_grad",
    )


def split_vector(vec_values):
    split_points = [D, D + FF, 2 * D + FF, 3 * D + FF, 4 * D + FF, 5 * D + FF]
    return jnp.split(vec_values, split_points)


def squares_kernel(place_ref, *refs):
    *parts, small_ref, out_ref = refs
    total = 0.0
    for ref in parts:
        value = ref[...]
        total = total + jnp.sum(jnp.sum(value * value, axis=0, keepdims=True), axis=1, keepdims=True)
    small = small_ref[...]
    total = total + jnp.sum(small * small, axis=1, keepdims=True)
    out_ref[...] = jnp.broadcast_to(total[None], out_ref.shape)


def sum_squares(place, place_vec, parts, small):
    operands = (*parts, small)
    shape = jax.ShapeDtypeStruct((place.total, 8, 128), F32)
    own = call(
        squares_kernel, place_vec, operands, (), [whole(w.shape) for w in operands], whole(shape.shape), shape,
        (1,), [], 1000, "squares",
    )
    return lax.all_to_all(own, AXES, split_axis=0, concat_axis=0, tiled=True)


def adam_kernel(rates, place_ref, squares_ref, *refs):
    count = len(rates)
    norm = jnp.sqrt(jnp.sum(squares_ref[...], axis=0)[0:1, 0:1])
    refs[5 * count][...] = norm
    clip_limit = CLIP_RMS * math.sqrt(PARAMS)
    factor = clip_limit / jnp.maximum(norm, clip_limit)
    for index, rate in enumerate(rates):
        weight, first, second, average, gradient = (refs[index * 5 + i][...] for i in range(5))
        clipped = gradient * factor.reshape((1,) * gradient.ndim)
        first_new = BETA_ONE * first + (1.0 - BETA_ONE) * clipped
        second_new = BETA_TWO * second + (1.0 - BETA_TWO) * clipped * clipped
        first_hat = first_new / (1.0 - BETA_ONE**STEP)
        second_hat = second_new / (1.0 - BETA_TWO**STEP)
        weight_new = weight - rate * (first_hat / (jnp.sqrt(second_hat) + ADAM_EPS) + WEIGHT_DECAY * weight)
        outs = refs[5 * count + 1 + index * 4 : 5 * count + 5 + index * 4]
        outs[0][...] = weight_new
        outs[1][...] = first_new
        outs[2][...] = second_new
        outs[3][...] = AVERAGE_KEEP * average + (1.0 - AVERAGE_KEEP) * weight_new


def adam(place_vec, squares, groups, rates):
    flat = [value for group in groups for value in group]
    shapes = [jax.ShapeDtypeStruct((1, 1), F32)]
    shapes += [jax.ShapeDtypeStruct(group[0].shape, F32) for group in groups for _ in range(4)]
    return call(
        partial(adam_kernel, rates), place_vec, (squares, *flat), (),
        [whole(value.shape) for value in (squares, *flat)], [whole(value.shape) for value in shapes], shapes,
        (1,), [], 1000, "adam",
    )


def body(
    tokens,
    cotangent,
    bucket,
    lengths,
    in_weight,
    in_first,
    in_second,
    in_average,
    in_bias,
    bias_first,
    bias_second,
    bias_average,
    out_weight,
    out_first,
    out_second,
    out_average,
    up_weight,
    up_first,
    up_second,
    up_average,
    down_weight,
    down_first,
    down_second,
    down_average,
    vectors,
    vec_first,
    vec_second,
    vec_average,
):
    place = Place()
    n_rows, n_heads, total = place.n_rows, place.n_heads, place.total
    z_size = place.sizes["z"]
    share = cotangent.shape[0]
    row_index, head_index = lax.axis_index("rows"), lax.axis_index("heads")
    blocks = share // CAP_L
    own_kinds = lax.dynamic_slice_in_dim(bucket, head_index * blocks, blocks, 0)
    own_lengths = lax.dynamic_slice_in_dim(lengths, head_index * blocks, blocks, 0)
    own_blocks = jnp.concatenate([own_kinds[:, None], own_lengths], axis=1).reshape(-1)
    place_vec = jnp.concatenate([jnp.stack([place.z, place.y, place.x, place.c]), own_blocks]).astype(jnp.int32)
    in_rows, in_cols = in_weight.shape[1], in_weight.shape[2]
    out_rows, down_rows = out_weight.shape[0], down_weight.shape[0]
    bias_len, vec_len = in_bias.size, vectors.size
    pieces_fit = in_rows == 96 and in_cols == HALF // 2 and out_rows == 24 and n_heads == 4

    small = jnp.concatenate([vectors, in_bias.reshape(-1)])
    if pieces_fit:
        piece, ffn_piece = make_pieces(
            place, place_vec, in_weight, out_weight, up_weight, down_weight, small[None, :]
        )
        entries = gather_pieces(place, piece)
        ffn_all = lax.all_gather(ffn_piece, AXES, axis=0)
        buffers = [entry[0] for entry in entries]
        layout = [(None,) + entry[1:] for entry in entries]
        in_buffers, layer_buffers = buffers, buffers + [ffn_all]
    else:
        layout = ()
        all_in = lax.all_gather(in_weight.astype(BF), "rows", axis=1, tiled=True)
        all_in = lax.all_gather(all_in, "heads", axis=2, tiled=True)
        all_out, all_up, all_down = (
            lax.all_gather(w.astype(BF), AXES, axis=0, tiled=True)
            for w in (out_weight, up_weight, down_weight)
        )
        layer_buffers = [all_out, all_up, all_down]
        all_small = lax.all_gather(small.astype(BF), AXES, axis=0).astype(F32)
        bias_out, bias_up, bias_down, gain_one, shift_one, gain_two, shift_two = split_vector(
            all_small[:, :vec_len].reshape(-1)
        )
        bias_shape = (n_rows, n_heads) + in_bias.shape
        bias_all = all_small[:, vec_len:].reshape(bias_shape).transpose(2, 1, 3, 0, 4).reshape(2, D)
        bias_in = jnp.stack([bias_all[0], jnp.zeros_like(bias_all[0]), bias_all[1]])[:, None, :]
        vec_rows = jnp.stack([bias_out, bias_down, gain_one, shift_one, gain_two, shift_two, bias_out, bias_out])
        in_buffers = [all_in, bias_in]

    q, k, v, o, lse, *small_rows = attend(
        place_vec, tokens, share, layout, in_buffers, z_size, vec_len, n_rows
    )
    vec_rows, b1, all_in = small_rows if pieces_fit else (vec_rows, bias_up[None, :], all_in)
    layer_out, dr1, yr, dur, dor, sums, db1, *grads_down = layer(
        place_vec, o, tokens, cotangent, vec_rows, b1, layout, layer_buffers, z_size, n_heads
    )

    def back(vec, flip, *after):
        return attend_back(
            place_vec, q, k, v, dor, lse, tokens, vec, vec_len, z_size, pieces_fit, flip, after
        )

    if pieces_fit:
        down_near, down_far, down_far_x = grads_down
        down_x = low_sum(down_near[1], place.send(down_far_x, "c"))
        got_down_x = place.send(down_x, "x")
        down_c = place.send(down_far, "c")
        up_near, up_far, up_far_x, vec_small = grad_up(
            place_vec, yr, sums, db1, dur, layout, z_size, vec_len, (down_x,)
        )
        up_x = low_sum(up_near[1], place.send(up_far_x, "c"))
        got_up_x = place.send(up_x, "x")
        up_c = place.send(up_far, "c")
        down = low_sum(down_near[0], down_c, got_down_x)
        down_sums = trade(place, down)
        other = back(vec_small, 1, up_x, down)

        far_c = place.send(other[4], "c")
        far_x = low_sum(other[3], far_c)
        got_far_x = place.send(far_x, "x")
        up = low_sum(up_near[0], up_c, got_up_x)
        up_sums = trade(place, up)
        mine = back(vec_small, 0, far_x, up, down_sums)

        near_c = place.send(mine[4], "c")
        near = low_sum(mine[3], near_c, got_far_x)
        in_sum = trade(place, near)
        token_grad = input_grad(place_vec, dr1, mine[:3], other[:3], all_in, (near,))

        own_small = pick(in_sum[144:], row_index * 2 + place.c, 0)[None, :]
        squares = sum_squares(place, place_vec, (down_sums, up_sums, in_sum[:144]), own_small)
        sum_down = jnp.concatenate([down_sums[:96], down_sums[96:192]], axis=1)
        sum_up = jnp.concatenate([up_sums[at : at + 48] for at in range(0, 192, 48)], axis=1)
        sum_up = swap_halves(place, sum_up, 0, 1)
        sum_out = swap_halves(place, down_sums[192:], 0, 1)
        sum_in = swap_halves(place, in_sum[:144].reshape(3, 48, HALF), 2, 1)
        sum_vec = own_small[0, :vec_len]
        sum_bias = own_small[0, vec_len : vec_len + bias_len].reshape(in_bias.shape)
    else:
        def spread(value):
            return lax.psum_scatter(value, AXES, scatter_dimension=0, tiled=True).astype(F32)

        def join(far, near, axis):
            return jnp.where(
                place.x == 0, jnp.concatenate([near, far], axis=axis), jnp.concatenate([far, near], axis=axis)
            )

        grads_up = grad_up(place_vec, yr, sums, db1, dur, layout, z_size, vec_len, ())
        unused = jnp.zeros((2, SMALL_ROWS, HALF), F32)
        grad_vec = jnp.concatenate([sums[0], db1[0], *(sums[i] for i in range(1, 6))])
        other, mine = back(unused, 1), back(unused, 0)
        token_grad = input_grad(place_vec, dr1, mine[:3], other[:3], all_in, ())
        grad_in = join(other[3], mine[3], 2)
        sum_in = lax.psum_scatter(grad_in, "heads", scatter_dimension=2, tiled=True)
        sum_in = lax.psum_scatter(sum_in, "rows", scatter_dimension=1, tiled=True).astype(F32)
        sum_up, sum_out, sum_down = spread(grads_up[0]), spread(grads_down[1]), spread(grads_down[0])
        sum_vec = lax.psum_scatter(grad_vec, AXES, scatter_dimension=0, tiled=True)
        grad_bias = join(other[4], mine[4], 1).reshape(2, n_heads * in_bias.shape[1], -1)
        sum_bias = lax.psum_scatter(grad_bias, "heads", scatter_dimension=1, tiled=True)
        sum_bias = lax.psum_scatter(sum_bias, "rows", scatter_dimension=2, tiled=True)

        flat_small = jnp.concatenate([sum_vec, sum_bias.reshape(-1)])[None, :]
        parts = (sum_in.reshape(-1, in_cols), sum_out, sum_up, sum_down)
        squares = sum_squares(place, place_vec, parts, flat_small)
    row = (1, vec_len)
    grad_norm, *new = adam(
        place_vec,
        squares,
        (
            (in_weight, in_first, in_second, in_average, sum_in),
            tuple(v.transpose(1, 0, 2) for v in (in_bias, bias_first, bias_second, bias_average, sum_bias)),
            (out_weight, out_first, out_second, out_average, sum_out),
            (up_weight, up_first, up_second, up_average, sum_up),
            (down_weight, down_first, down_second, down_average, sum_down),
            tuple(value.reshape(row) for value in (vectors, vec_first, vec_second, vec_average, sum_vec)),
        ),
        (LEARN_RATE,) * 5 + (VECTOR_RATE,),
    )
    return (
        layer_out,
        token_grad,
        grad_norm[0, 0],
        *new[:4],
        *(value.transpose(1, 0, 2) for value in new[4:8]),
        *new[8:20],
        *(value.reshape(vec_len) for value in new[20:]),
    )


def solution(mesh):
    in_specs = (
        P("rows", None),
        P(("rows", "heads"), None),
        P("rows"),
        P("rows", None),
        P(None, "rows", "heads"),
        P(None, "rows", "heads"),
        P(None, "rows", "heads"),
        P(None, "rows", "heads"),
        P(None, "heads", "rows"),
        P(None, "heads", "rows"),
        P(None, "heads", "rows"),
        P(None, "heads", "rows"),
        P(("rows", "heads"), None),
        P(("rows", "heads"), None),
        P(("rows", "heads"), None),
        P(("rows", "heads"), None),
        P(("rows", "heads"), None),
        P(("rows", "heads"), None),
        P(("rows", "heads"), None),
        P(("rows", "heads"), None),
        P(("rows", "heads"), None),
        P(("rows", "heads"), None),
        P(("rows", "heads"), None),
        P(("rows", "heads"), None),
        P(("rows", "heads")),
        P(("rows", "heads")),
        P(("rows", "heads")),
        P(("rows", "heads")),
    )
    out_specs = (
        P(("rows", "heads"), None),
        P(("rows", "heads"), None),
        P(),
        P(None, "rows", "heads"),
        P(None, "rows", "heads"),
        P(None, "rows", "heads"),
        P(None, "rows", "heads"),
        P(None, "heads", "rows"),
        P(None, "heads", "rows"),
        P(None, "heads", "rows"),
        P(None, "heads", "rows"),
        P(("rows", "heads"), None),
        P(("rows", "heads"), None),
        P(("rows", "heads"), None),
        P(("rows", "heads"), None),
        P(("rows", "heads"), None),
        P(("rows", "heads"), None),
        P(("rows", "heads"), None),
        P(("rows", "heads"), None),
        P(("rows", "heads"), None),
        P(("rows", "heads"), None),
        P(("rows", "heads"), None),
        P(("rows", "heads"), None),
        P(("rows", "heads")),
        P(("rows", "heads")),
        P(("rows", "heads")),
        P(("rows", "heads")),
    )
    return jax.shard_map(body, mesh=mesh, in_specs=in_specs, out_specs=out_specs, check_vma=False)
```

```python
from functools import partial
import math

import jax
import jax.numpy as jnp
from jax import lax
from jax.experimental import pallas as pl
from jax.experimental.pallas import tpu as pltpu
from jax.sharding import PartitionSpec as P

D = 768
HD = 64
FF = 3072
CAP_L = 512
CAP_M = 128
CAP_S = 64
STEP = 10
ROWS_BLK = 8
PARAMS = 7087104

LN_EPS = 1e-05
LEARN_RATE = 0.1
VECTOR_RATE = 0.3
BETA_ONE = 0.9
BETA_TWO = 0.999
ADAM_EPS = 1e-08
WEIGHT_DECAY = 0.01
AVERAGE_KEEP = 0.75
CLIP_RMS = 0.001

AXES = ("rows", "heads")
BF = jnp.bfloat16
F32 = jnp.float32
VMEM_BYTES = 58 * 1024 * 1024
GROUP = 256
HALF = D // 2
PACK_VEC = 16


def dot_nn(left, right):
    return lax.dot_general(left, right, (((1,), (0,)), ((), ())), preferred_element_type=F32)


def dot_nt(left, right):
    return lax.dot_general(left, right, (((1,), (1,)), ((), ())), preferred_element_type=F32)


def dot_tn(left, right):
    return lax.dot_general(left, right, (((0,), (0,)), ((), ())), preferred_element_type=F32)


def kernel_params(steps=1, vmem=VMEM_BYTES):
    return pltpu.CompilerParams(
        vmem_limit_bytes=vmem, dimension_semantics=("arbitrary",) * steps
    )


def whole(shape):
    return pl.BlockSpec(shape, lambda *_: (0,) * len(shape))


ANY = pl.BlockSpec(memory_space=pl.ANY)


def call(kernel, place_vec, args, after, in_specs, out_specs, out_shape, grid, scratch, flops, name, vmem=VMEM_BYTES):
    def run(place_ref, *refs):
        return kernel(place_ref, *refs[len(after) :])

    return pl.pallas_call(
        run,
        grid_spec=pltpu.PrefetchScalarGridSpec(
            num_scalar_prefetch=1,
            grid=grid,
            in_specs=[ANY] * len(after) + in_specs,
            out_specs=out_specs,
            scratch_shapes=scratch,
        ),
        out_shape=out_shape,
        compiler_params=kernel_params(len(grid), vmem),
        cost_estimate=pl.CostEstimate(flops=flops // 1000, bytes_accessed=1024, transcendentals=0),
        name=name,
    )(place_vec, *after, *args)


def gate(place_vec, value, after):
    def run(place_ref, *refs):
        pass

    return pl.pallas_call(
        run,
        grid_spec=pltpu.PrefetchScalarGridSpec(
            num_scalar_prefetch=1, grid=(1,), in_specs=[ANY] * (len(after) + 1), out_specs=ANY
        ),
        out_shape=jax.ShapeDtypeStruct(value.shape, value.dtype),
        input_output_aliases={1: 0},
        compiler_params=kernel_params(),
        cost_estimate=pl.CostEstimate(flops=1, bytes_accessed=1, transcendentals=0),
        name="gate",
    )(place_vec, value, *after)


class Place:
    def __init__(self):
        self.n_rows = lax.axis_size("rows")
        self.n_heads = lax.axis_size("heads")
        self.total = self.n_rows * self.n_heads
        self.sizes = {"z": self.n_rows // 2, "y": 2, "x": self.n_heads // 2, "c": 2}
        self.strides = {"c": 1, "x": 2, "y": self.n_heads, "z": 2 * self.n_heads}
        row, head = lax.axis_index("rows"), lax.axis_index("heads")
        self.z, self.y = row // 2, row % 2
        self.x, self.c = head // 2, head % 2

    def send(self, value, digit, shift=1):
        size, stride = self.sizes[digit], self.strides[digit]
        pairs = []
        for device in range(self.total):
            own = (device // stride) % size
            pairs.append((device, device + ((own + shift) % size - own) * stride))
        return lax.ppermute(value, AXES, pairs)


def gather_pieces(place, piece):
    z_size = place.sizes["z"]
    column = jnp.stack([piece] + [place.send(piece, "z", shift) for shift in range(1, z_size)])
    from_x = place.send(column, "x")
    from_y = place.send(column, "y")
    cut = z_size // 2
    diag_low = place.send(from_x[:cut], "y")
    diag_high = place.send(from_y[cut:], "x")
    shifts = tuple(range(z_size))
    near = [
        (column, shifts, 0, 0, 0),
        (from_x, shifts, 0, 1, 0),
        (from_y, shifts, 1, 0, 0),
        (diag_low, shifts[:cut], 1, 1, 0),
        (diag_high, shifts[cut:], 1, 1, 0),
    ]
    far = [(place.send(buffer, "c"), s, y, x, 1) for buffer, s, y, x, _ in near]
    return near + far


def pick(value, index, axis):
    return lax.dynamic_index_in_dim(value, index, axis, keepdims=False)


def low_sum(*parts):
    return sum(part.astype(F32) for part in parts).astype(BF)


def trade(place, value, digits):
    steps = [0]
    for digit in digits:
        steps = [step + i * place.strides[digit] for step in steps for i in range(place.sizes[digit])]
    groups = [
        [device + step for step in steps]
        for device in range(place.total)
        if all((device // place.strides[d]) % place.sizes[d] == 0 for d in digits)
    ]
    got = lax.all_to_all(value, AXES, split_axis=0, concat_axis=0, tiled=True, axis_index_groups=groups)
    return jnp.sum(got.astype(F32), axis=0)


def swap_halves(place, value, cut_axis, join_axis):
    size = value.shape[cut_axis] // 2
    keep = lax.dynamic_slice_in_dim(value, place.c * size, size, cut_axis)
    give = lax.dynamic_slice_in_dim(value, (1 - place.c) * size, size, cut_axis)
    got = place.send(give, "c")
    first = jnp.where(place.c == 0, keep, got)
    second = jnp.where(place.c == 0, got, keep)
    return jnp.concatenate([first, second], axis=join_axis)


GIVE_ROWS = 144


def split_kernel(place_ref, in_ref, out_ref, up_ref, keep_ref, give_ref):
    zero = jnp.zeros((8, D), BF)
    for away, ref in enumerate((keep_ref, give_ref)):
        core = place_ref[3] ^ away
        for j in range(3):
            ref[0:48, j * 256 : j * 256 + 192] = in_ref[j, pl.ds(pl.multiple_of(core * 48, 8), 48), :].astype(BF)
            ref[0:48, j * 256 + 192 : (j + 1) * 256] = zero[:, :64].repeat(6, axis=0)
        ref[48:72, 0:HALF] = out_ref[:, pl.ds(pl.multiple_of(core * HALF, 128), HALF)].astype(BF)
        ref[48:72, HALF:] = jnp.zeros((24, HALF), BF)
        for t in range(2):
            col = pl.multiple_of(core * (FF // 2) + t * D, 128)
            ref[80 + t * 32 : 104 + t * 32, :] = up_ref[:, pl.ds(col, D)].astype(BF)
        for at in (72, 104, 136):
            ref[at : at + 8, :] = zero


def join_kernel(place_ref, keep_ref, got_ref, down_ref, small_ref, piece_ref, ffn_ref):
    first = place_ref[3] == 0
    keep, got = keep_ref[...], got_ref[...]
    low = jnp.where(first, keep, got)
    high = jnp.where(first, got, keep)
    for j in range(3):
        cols = slice(j * 256, j * 256 + 192)
        piece_ref[j * 48 : (j + 1) * 48, :] = jnp.concatenate([low[0:48, cols], high[0:48, cols]], axis=1)
    piece_ref[144:168, :] = low[48:72, :HALF]
    piece_ref[168:192, :] = high[48:72, :HALF]
    small = jnp.concatenate([small_ref[...], jnp.zeros((1, HALF - small_ref.shape[1]), F32)], axis=1)
    row = lax.broadcasted_iota(jnp.int32, (PACK_VEC, HALF), 0)
    piece_ref[192:208, :] = jnp.where(row == 0, small, 0.0).astype(BF)
    for t in range(2):
        ffn_ref[t * 48 : t * 48 + 24, :] = low[80 + t * 32 : 104 + t * 32, :]
        ffn_ref[t * 48 + 24 : t * 48 + 48, :] = high[80 + t * 32 : 104 + t * 32, :]
    ffn_ref[96:192, :] = down_ref[...].astype(BF)


def make_pieces(place, place_vec, in_weight, out_weight, up_weight, down_weight, small):
    half = jax.ShapeDtypeStruct((GIVE_ROWS, D), BF)
    weights = (in_weight, out_weight, up_weight)
    keep, give = call(
        split_kernel, place_vec, weights, (), [whole(w.shape) for w in weights],
        [whole(half.shape)] * 2, [half] * 2, (1,), [], 1000, "split",
    )
    operands = (keep, place.send(give, "c"), down_weight, small)
    shapes = [jax.ShapeDtypeStruct((208, HALF), BF), jax.ShapeDtypeStruct((192, D), BF)]
    return call(
        join_kernel, place_vec, operands, (), [whole(w.shape) for w in operands],
        [whole(w.shape) for w in shapes], shapes, (1,), [], 1000, "join",
    )


def run_copies(copies):
    for copy in copies:
        copy.start()
    return copies


def finish_copies(copies):
    for copy in copies:
        copy.wait()


def piece_origin(place_ref, z_size, entry, index):
    _, shifts, y, x, c = entry
    shift = shifts[index]
    z_at = lax.rem(place_ref[0] + (z_size - shift), z_size)
    return z_at, place_ref[1] ^ y, place_ref[2] ^ x, place_ref[3] ^ c


def mask_block(place_ref, block):
    kind = place_ref[4 + block * (ROWS_BLK + 1)]
    bits = jnp.where(kind == 0, 9, jnp.where(kind == 1, 7, 6))
    place = lax.broadcasted_iota(jnp.int32, (CAP_L, 2 * HD), 0)
    lane = lax.broadcasted_iota(jnp.int32, (1, 2 * HD), 1) % HD
    length = jnp.zeros((1, 2 * HD), jnp.int32)
    for row in range(ROWS_BLK):
        length = jnp.where(lane == row, place_ref[4 + block * (ROWS_BLK + 1) + 1 + row], length)
    row = lax.shift_right_logical(place, jnp.broadcast_to(bits, place.shape))
    within = place - lax.shift_left(row, jnp.broadcast_to(bits, place.shape))
    same = row == lane
    used = lane < ROWS_BLK
    closed = used & ~(same & (within < length))
    return jnp.where(closed, -1e30, 0.0).astype(BF), jnp.where(same & used, 1.0, 0.0).astype(BF)


def lane_half(rows):
    return lax.broadcasted_iota(jnp.int32, (rows, 2 * HD), 1) < HD


def div_mod(values, divisor):
    quotient = jnp.floor((values + 0.5) * (1.0 / divisor))
    return quotient, values - quotient * divisor


def counted(shape, axis):
    return lax.broadcasted_iota(jnp.int32, shape, axis).astype(F32)


def spread_small(small, lane_of, device_of):
    devices, lanes = small.shape
    column = counted((1, D), 1)
    hit = jnp.where(counted((lanes, D), 0) == lane_of(column), 1.0, 0.0).astype(BF)
    taken = jnp.where(counted((devices, D), 0) == device_of(column), dot_nn(small, hit), 0.0)
    return jnp.sum(taken, axis=0, keepdims=True)


def fill_small(small, vec_len, n_rows, bias_ref, vec_ref, b1_ref):
    n_heads = small.shape[0] // n_rows
    per_device = D // n_heads // HD
    width = HD // n_rows

    def bias_lane(j):
        def lane(col):
            head, place = div_mod(div_mod(col, per_device * HD)[1], HD)
            return vec_len + (j * per_device + head) * width + div_mod(place, width)[1]

        return lane

    def bias_device(col):
        return div_mod(div_mod(col, HD)[1], width)[0] * n_heads + div_mod(col, per_device * HD)[0]

    bias_ref[0] = spread_small(small, bias_lane(0), bias_device)
    bias_ref[1] = jnp.zeros((1, D), F32)
    bias_ref[2] = spread_small(small, bias_lane(1), bias_device)
    for index in range(10):
        start = index * D
        row = spread_small(small, lambda col: div_mod(start + col, vec_len)[1], lambda col: div_mod(start + col, vec_len)[0])
        if 1 <= index <= 4:
            b1_ref[:, (index - 1) * D : index * D] = row
        else:
            at = 0 if index == 0 else index - 4
            vec_ref[at : at + 1, :] = row


def attend_kernel(layout, place_ref, x_ref, *rest):
    entries, z_size, vec_len, n_rows = layout
    n_in = len(entries) if entries else 2
    sources = rest[:n_in]
    q_ref, k_ref, v_ref, o_ref, lse_ref, *more = rest[n_in:]
    if entries:
        vec_ref, b1_ref, whole_ref, weight, bias_ref, small, sems, sem_out = more
    else:
        weight, bias_ref, sems = more
    group = pl.program_id(0)

    @pl.when(group == 0)
    def _():
        copies = []
        if entries:
            for entry, source in zip(entries, sources):
                for index in range(len(entry[1])):
                    z_at, y_at, x_at, c_at = piece_origin(place_ref, z_size, entry, index)
                    row = pl.multiple_of((z_at * 2 + y_at) * 96 + c_at * 48, 16)
                    col = pl.multiple_of(x_at * HALF, 128)
                    device = ((z_at * 2 + y_at) * 2 + x_at) * 2 + c_at
                    copies.append(
                        pltpu.make_async_copy(
                            source.at[index, pl.ds(192, PACK_VEC), :], small.at[device], sems.at[len(copies)]
                        )
                    )
                    for j in range(3):
                        copies.append(
                            pltpu.make_async_copy(
                                source.at[index, pl.ds(j * 48, 48), :],
                                weight.at[j, pl.ds(row, 48), pl.ds(col, HALF)],
                                sems.at[len(copies)],
                            )
                        )
        else:
            copies.append(pltpu.make_async_copy(sources[0], weight, sems.at[0]))
            copies.append(pltpu.make_async_copy(sources[1], bias_ref, sems.at[1]))
        finish_copies(run_copies(copies))
        if entries:
            shares = jnp.sum(small[...].astype(F32), axis=1).astype(BF)
            fill_small(shares, vec_len, n_rows, bias_ref, vec_ref, b1_ref)
            pltpu.make_async_copy(weight, whole_ref, sem_out).start()

    if entries:

        @pl.when(group == pl.num_programs(0) - 1)
        def _():
            pltpu.make_async_copy(weight, whole_ref, sem_out).wait()

    x = x_ref[...]
    at = pl.multiple_of(group * GROUP, GROUP)
    for j, out in enumerate((q_ref, k_ref, v_ref)):
        out[...] = (dot_nn(x, weight[j, :, pl.ds(at, GROUP)]) + bias_ref[j, :, pl.ds(at, GROUP)]).astype(BF)
    low = lane_half(CAP_L)
    for block in range(x_ref.shape[0] // CAP_L):
        rows = slice(block * CAP_L, (block + 1) * CAP_L)
        key_mask, query_row = mask_block(place_ref, block)
        for pair in range(GROUP // 128):
            cols = slice(pair * 128, (pair + 1) * 128)
            q2, k2 = q_ref[rows, cols] * BF(HD ** -0.5), k_ref[rows, cols]
            v2t = v_ref[rows, cols].T
            outs = []
            for side in range(2):
                here = low if side == 0 else ~low
                s = dot_nt(jnp.where(here, k2, key_mask), jnp.where(here, q2, query_row))
                peak = jnp.max(s, axis=0, keepdims=True)
                e = jnp.exp(s - peak)
                total = jnp.sum(e, axis=0, keepdims=True)
                o = dot_nn(v2t[side * HD : (side + 1) * HD], e.astype(BF))
                outs.append(o * (1.0 / total))
                slot = block * 2 + side
                lse_ref[pair, slot : slot + 1, :] = peak + jnp.log(total)
            o_ref[rows, cols] = jnp.concatenate(outs, axis=0).T.astype(BF)


def own_tokens(tokens, tile):
    return pl.BlockSpec((tile, D), lambda t, p: ((p[2] * 2 + p[3]) * (tokens // tile) + (t if tile < tokens else 0), 0))


def attend(place_vec, x, tokens, entries, buffers, z_size, vec_len, n_rows):
    slots = tokens // CAP_L * 2
    block = pl.BlockSpec((tokens, GROUP), lambda g, p: (0, g))
    out_specs = [block] * 4 + [pl.BlockSpec((GROUP // 128, slots, CAP_L), lambda g, p: (g, 0, 0))]
    out_shape = [jax.ShapeDtypeStruct((tokens, D), BF)] * 4 + [jax.ShapeDtypeStruct((D // 128, slots, CAP_L), F32)]
    scratch = [pltpu.VMEM((3, D, D), BF), pltpu.VMEM((3, 1, D), F32)]
    n_copies = 2
    if entries:
        pieces = sum(len(entry[1]) for entry in entries)
        n_copies = 4 * pieces
        out_specs += [whole((8, D)), whole((1, FF)), ANY]
        out_shape += [jax.ShapeDtypeStruct((8, D), F32), jax.ShapeDtypeStruct((1, FF), F32)]
        out_shape += [jax.ShapeDtypeStruct((3, D, D), BF)]
        scratch += [pltpu.VMEM((pieces, PACK_VEC, HALF), BF)]
    return call(
        partial(attend_kernel, (entries, z_size, vec_len, n_rows)),
        place_vec,
        (x, *buffers),
        (),
        [own_tokens(tokens, tokens)] + [ANY] * len(buffers),
        out_specs,
        out_shape,
        (D // GROUP,),
        scratch + [pltpu.SemaphoreType.DMA((n_copies,))] + [pltpu.SemaphoreType.DMA] * bool(entries),
        10 * tokens * D * D,
        "attend",
    )


def small_bias(sums, vec_len, n_rows):
    width = HD // n_rows
    heads = HALF // 2 // HD
    out = 0.0
    col = counted((1, HALF), 1)
    mine = counted((2 * n_rows, HALF), 0) == div_mod(div_mod(col, HD)[1], width)[0] * 2 + div_mod(col, heads * HD)[0]
    head, place = div_mod(div_mod(counted((HALF, 1), 0), heads * HD)[1], HD)
    for j in range(2):
        hit = counted((HALF, HALF), 1) == vec_len + (j * heads + head) * width + div_mod(place, width)[1]
        spread = jnp.where(mine, sums[j : j + 1, :], 0.0).astype(BF)
        out = out + dot_nn(spread, jnp.where(hit, 1.0, 0.0).astype(BF))
    return out


def attend_back_kernel(
    layout, flip, place_ref, q_ref, k_ref, v_ref, do_ref, lse_ref, x_ref, vec_ref,
    dq_ref, dk_ref, dv_ref, *rest,
):
    z_size, split, vec_len = layout
    low = lane_half(CAP_L)
    sum_q, sum_v = [], []
    masks = [mask_block(place_ref, block) for block in range(q_ref.shape[0] // CAP_L)]
    for pair in range(HALF // 128):
        cols = slice(pair * 128, (pair + 1) * 128)
        pair_q, pair_v = 0.0, 0.0
        for block in range(q_ref.shape[0] // CAP_L):
            rows = slice(block * CAP_L, (block + 1) * CAP_L)
            key_mask, query_row = masks[block]
            q2, k2 = q_ref[rows, cols] * BF(HD ** -0.5), k_ref[rows, cols]
            v2, do2 = v_ref[rows, cols], do_ref[rows, cols]
            k2t = k2.T
            dq_t, dk, dv = [], [], []
            for side in range(2):
                here = low if side == 0 else ~low
                slot = block * 2 + side
                s = dot_nt(jnp.where(here, k2, key_mask), jnp.where(here, q2, query_row))
                p = jnp.exp(s - lse_ref[pair, slot : slot + 1, :])
                dp = dot_nt(jnp.where(here, v2, BF(0)), do2)
                dv.append(dot_nn(p.astype(BF), do2))
                inner = jnp.sum(dp * p, axis=0, keepdims=True)
                ds = (p * (dp - inner)).astype(BF)
                dk.append(dot_nn(ds, q2))
                dq_t.append(dot_nn(k2t[side * HD : (side + 1) * HD], ds))
            dq_low = (jnp.concatenate(dq_t, axis=0).T * HD ** -0.5).astype(BF)
            dv_low = jnp.where(low, dv[0], dv[1]).astype(BF)
            dq_ref[rows, cols] = dq_low
            dk_ref[rows, cols] = jnp.where(low, dk[0], dk[1]).astype(BF)
            dv_ref[rows, cols] = dv_low
            pair_q = pair_q + col_sum(dq_low)
            pair_v = pair_v + col_sum(dv_low)
        sum_q.append(pair_q)
        sum_v.append(pair_v)
    x = x_ref[...]
    sums = jnp.concatenate([jnp.concatenate(sum_q, axis=1), jnp.concatenate(sum_v, axis=1)], axis=0)
    if not split:
        grad_ref, bias_ref = rest
        bias_ref[...] = sums
        for j, ref in enumerate((dq_ref, dk_ref, dv_ref)):
            grad_ref[j] = dot_tn(x, ref[...]).astype(BF)
        return
    *grad_refs, held, held_small, sems = rest
    held_small[...] = (vec_ref[0] + small_bias(sums, vec_len, 2 * z_size)).astype(BF)
    copies = []

    def scatter(source, rows, step):
        for row in range(2 * z_size):
            for away in range(2):
                core = place_ref[3] ^ away
                copies.append(
                    pltpu.make_async_copy(source(row, core), grad_refs[away].at[row, rows], sems.at[step, row * 2 + away])
                )
                copies[-1].start()

    scatter(lambda row, core: held_small, pl.ds(144, SMALL_ROWS), 3)
    for j, ref in enumerate((dq_ref, dk_ref, dv_ref)):
        held[j] = dot_tn(x, ref[...]).astype(BF)
        scatter(
            lambda row, core: held.at[j, pl.ds(pl.multiple_of(row * 96 + core * 48, 16), 48)], pl.ds(j * 48, 48), j
        )
    finish_copies(copies)


SMALL_ROWS = 16


def attend_back(place_vec, q, k, v, do, lse, x, vec, vec_len, z_size, split, flip, after):
    tokens = q.shape[0]
    slots = lse.shape[1]

    def half(g, p):
        return (0, (p[2] % 2) ^ flip)

    block = pl.BlockSpec((tokens, HALF), half)
    out_shape = [jax.ShapeDtypeStruct((tokens, HALF), BF)] * 3
    out_specs = [whole((tokens, HALF))] * 3
    if split:
        out_shape += [jax.ShapeDtypeStruct((2 * z_size, 144 + SMALL_ROWS, HALF), BF)] * 2
        out_specs += [ANY] * 2
        scratch = [
            pltpu.VMEM((3, D, HALF), BF),
            pltpu.VMEM((SMALL_ROWS, HALF), BF),
            pltpu.SemaphoreType.DMA((4, 4 * z_size)),
        ]
    else:
        out_shape += [jax.ShapeDtypeStruct((3, D, HALF), BF), jax.ShapeDtypeStruct((2, HALF), F32)]
        out_specs += [whole((3, D, HALF)), whole((2, HALF))]
        scratch = []
    return call(
        partial(attend_back_kernel, (z_size, split, vec_len), flip),
        place_vec,
        (q, k, v, do, lse, x, vec),
        after,
        [block] * 4
        + [pl.BlockSpec((HALF // 128, slots, CAP_L), lambda g, p: ((p[2] % 2) ^ flip, 0, 0))]
        + [own_tokens(tokens, tokens), pl.BlockSpec((1, SMALL_ROWS, HALF), lambda g, p: ((p[2] % 2) ^ flip, 0, 0))],
        out_specs,
        out_shape,
        (1,),
        scratch,
        14 * tokens * D * D,
        "attend_back",
    )


TILE = 256
CHUNK = 768
ERF_P = 0.3275911 / math.sqrt(2.0)
ERF_A = (0.254829592, -0.284496736, 1.421413741, -1.453152027, 1.061405429)
BELL_RATE = -0.5 * math.log2(math.e)
BELL_SCALE = 1.0 / math.sqrt(2.0 * math.pi)


def gelu_parts(u):
    bell = jnp.exp2(u * u * BELL_RATE)
    scale = 1.0 + ERF_P * jnp.abs(u)
    t = pl.reciprocal(scale, approx=True)
    t = t * (2.0 - scale * t)
    poly = ERF_A[4] * 0.5
    for term in ERF_A[3::-1]:
        poly = poly * t + term * 0.5
    below = poly * t * bell
    phi = jnp.where(u >= 0.0, 1.0 - below, below)
    return u * phi, phi + u * bell * BELL_SCALE


def normalise(values):
    center = values - jnp.mean(values, axis=-1, keepdims=True)
    scale = lax.rsqrt(jnp.mean(center * center, axis=-1, keepdims=True) + LN_EPS)
    return center * scale, scale


def norm_back(grad, gain, normal, scale):
    inner = grad * gain
    first = jnp.mean(inner, axis=-1, keepdims=True)
    second = jnp.mean(inner * normal, axis=-1, keepdims=True)
    return (inner - first - normal * second) * scale


def col_sum(values):
    return jnp.sum(values.astype(F32), axis=0, keepdims=True)


def ffn_copies(layout, place_ref, sources, wo, w1, w2, sems):
    entries, z_size, n_heads = layout
    count = [0]

    def copy(source, target):
        made = pltpu.make_async_copy(source, target, sems.at[count[0]])
        count[0] += 1
        made.start()
        return made

    if not entries:
        return [[copy(source, target)] for source, target in zip(sources, (wo, w1, w2))]
    to_out, to_up, to_down = [], [], []
    for entry, source in zip(entries, sources):
        for index in range(len(entry[1])):
            z_at, y_at, x_at, c_at = piece_origin(place_ref, z_size, entry, index)
            row = pl.multiple_of(((z_at * 2 + y_at) * (n_heads // 2) + x_at) * 48, 16)
            col = pl.multiple_of(c_at * HALF, 128)
            to_out.append(copy(source.at[index, pl.ds(144, 48), :], wo.at[pl.ds(row, 48), pl.ds(col, HALF)]))
    for device in range(sources[-1].shape[0]):
        chip, core = device // 2, device % 2
        for part in range(2):
            to_up.append(
                copy(
                    sources[-1].at[device, part * 48 : (part + 1) * 48, :],
                    w1.at[chip * 48 : (chip + 1) * 48, pl.ds(core * (FF // 2) + part * D, D)],
                )
            )
    for device in range(sources[-1].shape[0]):
        to_down.append(copy(sources[-1].at[device, 96:192, :], w2.at[device * 96 : (device + 1) * 96, :]))
    return to_out, to_up, to_down


def layer_kernel(layout, place_ref, o_ref, x_ref, cot_ref, vec_ref, b1_ref, *rest):
    n_in = len(layout[0]) + 1 if layout[0] else 3
    sources = rest[:n_in]
    z_ref, dr1_ref, yr_ref, dur_ref, dor_ref, sums_ref, db1_ref, *grad_refs = rest[n_in:-12]
    wo, w1, w2, hr, slope, dfr_all, dar_all, held, sems, sems_out, n1_all, scale_all = rest[-12:]
    step = pl.program_id(0)

    @pl.when(step == 0)
    def _():
        sums_ref[...] = jnp.zeros_like(sums_ref)
        db1_ref[...] = jnp.zeros_like(db1_ref)
        to_out, to_up, to_down = ffn_copies(layout, place_ref, sources, wo, w1, w2, sems)
        finish_copies(to_out)
        for at in range(0, x_ref.shape[0], TILE):
            rows = slice(at, at + TILE)
            r1 = x_ref[rows, :].astype(F32) + (dot_nn(o_ref[rows, :], wo[...]) + vec_ref[0:1, :])
            normal, scale = normalise(r1)
            n1_all[rows, :] = normal
            scale_all[rows, :] = scale
        finish_copies(to_up)
        finish_copies(to_down)

    b2, g1, c1, g2, c2 = (vec_ref[i : i + 1, :] for i in range(1, 6))
    at_rows = pl.ds(pl.multiple_of(step * TILE, TILE), TILE)
    n1, scale1 = n1_all[at_rows, :], scale_all[at_rows, :]
    y1 = n1 * g1 + c1
    yr = y1.astype(BF)
    yr_ref[...] = yr
    f = None
    for at in range(0, FF, CHUNK):
        cols = slice(at, at + CHUNK)
        u = dot_nn(yr, w1[:, cols]) + b1_ref[:, cols]
        act, rate = gelu_parts(u)
        act = act.astype(BF)
        hr[at_rows, cols] = act
        slope[:, cols] = rate
        part = dot_nn(act, w2[cols, :])
        f = part if f is None else f + part
    n2, scale2 = normalise(y1 + (f + b2))
    z_ref[...] = (n2 * g2 + c2).astype(BF)
    dz = cot_ref[...].astype(F32)
    dr2 = norm_back(dz, g2, n2, scale2)
    dfr = dr2.astype(BF)
    dfr_all[at_rows, :] = dfr
    sums_ref[1:2, :] += col_sum(dfr)
    sums_ref[4:5, :] += col_sum(dz * n2)
    sums_ref[5:6, :] += col_sum(dz)
    dy1 = dr2
    for at in range(0, FF, CHUNK):
        cols = slice(at, at + CHUNK)
        dur = (dot_nt(dfr, w2[cols, :]) * slope[:, cols]).astype(BF)
        dur_ref[:, cols] = dur
        db1_ref[:, cols] += col_sum(dur)
        dy1 = dy1 + dot_nt(dur, w1[:, cols])
    dr1 = norm_back(dy1, g1, n1, scale1)
    dr1_ref[...] = dr1
    dar = dr1.astype(BF)
    dar_all[at_rows, :] = dar
    sums_ref[0:1, :] += col_sum(dar)
    sums_ref[2:3, :] += col_sum(dy1 * n1)
    sums_ref[3:4, :] += col_sum(dy1)
    dor_ref[...] = dot_nt(dar, wo[...]).astype(BF)

    @pl.when(step == pl.num_programs(0) - 1)
    def _():
        pending = [[], []]
        for index in range(FF // D + 1):
            slot = index % 2
            finish_copies(pending[slot])
            if index < FF // D:
                held[slot] = dot_tn(hr[:, index * D : (index + 1) * D], dfr_all[...]).astype(BF)
            else:
                held[slot] = dot_tn(o_ref[...], dar_all[...]).astype(BF)
            pending[slot] = layer_copies(layout, place_ref, held.at[slot], grad_refs, index, sems_out.at[slot])
        for copies in pending:
            finish_copies(copies)


def piece_target(grad_refs, away, flip, row):
    near, far, far_other = grad_refs
    return near.at[flip, row] if not away else (far_other if flip else far).at[row]


CUT_ROWS = 96


def layer_copies(layout, place_ref, held, grad_refs, index, sems):
    is_out = index == FF // D
    if not layout[0]:
        target = grad_refs[1] if is_out else grad_refs[0].at[pl.ds(index * D, D), :]
        return run_copies([pltpu.make_async_copy(held, target, sems.at[0])])
    near, far, far_other = grad_refs
    copies = []

    def add(source, away, first, second, z, rows):
        at = (second, z, rows)
        target = near.at[(first, *at)] if not away else (far_other if first else far).at[at]
        copies.append(pltpu.make_async_copy(source, target, sems.at[len(copies)]))

    for away in range(2):
        core = place_ref[3] ^ away
        for first in range(2):
            for second in range(2):
                for half in range(2):
                    y, x = (first, second) if half else (second, first)
                    plane = (place_ref[1] ^ y) * 2 + (place_ref[2] ^ x)
                    if not is_out:
                        row = pl.multiple_of(plane * 192 + core * 96, 16)
                        block = held.at[pl.ds(row, 96), pl.ds(half * HALF, HALF)]
                        add(block, away, first, second, index, pl.ds(half * CUT_ROWS, 96))
                    elif half:
                        col = pl.multiple_of(core * HALF, 128)
                        for z in range(layout[1]):
                            row = pl.multiple_of((z * 4 + plane) * 48, 16)
                            add(held.at[pl.ds(row, 48), pl.ds(col, HALF)], away, first, second, z, pl.ds(192, 48))
    return run_copies(copies)


def piece_shapes(z_size, rows):
    piece = (2 * z_size, rows, HALF)
    return [jax.ShapeDtypeStruct((2, *piece), BF)] + [jax.ShapeDtypeStruct(piece, BF)] * 2


def layer(place_vec, o, x, cotangent, vec, b1, entries, buffers, z_size, n_heads):
    tokens = o.shape[0]
    n_copies = sum(len(e[1]) for e in entries) + 3 * buffers[-1].shape[0] if entries else 3
    tile = pl.BlockSpec((TILE, D), lambda t, p: (t, 0))
    wide = pl.BlockSpec((TILE, FF), lambda t, p: (t, 0))
    low, full = jax.ShapeDtypeStruct((tokens, D), BF), jax.ShapeDtypeStruct((tokens, D), F32)
    if entries:
        piece = (2, z_size, 240, HALF)
        grads = [jax.ShapeDtypeStruct((2, *piece), BF)] + [jax.ShapeDtypeStruct(piece, BF)] * 2
    else:
        grads = [jax.ShapeDtypeStruct((FF, D), BF), jax.ShapeDtypeStruct((D, D), BF)]
    return call(
        partial(layer_kernel, (entries, z_size, n_heads)),
        place_vec,
        (o, x, cotangent, vec, b1, *buffers),
        (),
        [whole((tokens, D)), own_tokens(tokens, tokens), tile, whole((8, D)), whole((1, FF))] + [ANY] * len(buffers),
        [tile, tile, tile, wide, tile, whole((8, D)), whole((1, FF))] + [ANY] * len(grads),
        [
            low, full, low, jax.ShapeDtypeStruct((tokens, FF), BF), low,
            jax.ShapeDtypeStruct((8, D), F32), jax.ShapeDtypeStruct((1, FF), F32), *grads,
        ],
        (tokens // TILE,),
        [
            pltpu.VMEM((D, D), BF),
            pltpu.VMEM((D, FF), BF),
            pltpu.VMEM((FF, D), BF),
            pltpu.VMEM((tokens, FF), BF),
            pltpu.VMEM((TILE, FF), F32),
            pltpu.VMEM((tokens, D), BF),
            pltpu.VMEM((tokens, D), BF),
            pltpu.VMEM((2, D, D), BF),
            pltpu.SemaphoreType.DMA((n_copies,)),
            pltpu.SemaphoreType.DMA((2, 32)),
            pltpu.VMEM((tokens, D), F32),
            pltpu.VMEM((tokens, 1), F32),
        ],
        tokens * D * (6 * D + 10 * FF),
        "layer",
    )


def small_vectors(sums, db1, vec_len, devices):
    rows = [sums[0:1, :]] + [db1[:, at : at + D] for at in range(0, FF, D)]
    rows += [sums[i : i + 1, :] for i in range(1, 6)]
    out = 0.0
    for index, row in enumerate(rows):
        owner = div_mod(counted((1, D), 1) + index * D, vec_len)[0]
        spread = jnp.where(counted((devices, D), 0) == owner, row, 0.0).astype(BF)
        lane = div_mod(counted((D, 1), 0) + index * D, vec_len)[1]
        out = out + dot_nn(spread, jnp.where(counted((D, HALF), 1) == lane, 1.0, 0.0).astype(BF))
    return out


def grad_up_kernel(layout, place_ref, yr_ref, sums_ref, db1_ref, dur_ref, *rest):
    if not layout[0]:
        rest[0][...] = dot_tn(yr_ref[...], dur_ref[...]).astype(BF)
        return
    *grad_refs, small_ref, held, sems = rest
    step = pl.program_id(0)

    def up(index):
        slot = index % 2
        away = 1 - index // 2
        made = []
        for flip in range(2):
            x = place_ref[2] ^ flip
            for row in range(2 * layout[1]):
                at = pl.multiple_of((row * 2 + x) * 48, 16)
                target = piece_target(grad_refs, away, flip, row)
                for part in range(2):
                    source = held.at[slot, pl.ds(at, 48), pl.ds(part * HALF, HALF)]
                    used = sems.at[slot, part, flip * 2 * layout[1] + row]
                    made.append(pltpu.make_async_copy(source, target.at[pl.ds((slot * 2 + part) * 48, 48), :], used))
        return made

    steps = FF // D
    for index in range(steps):

        @pl.when(step == index)
        def _():
            if index == 0:
                rows = small_vectors(sums_ref, db1_ref, layout[2], 2 * SMALL_ROWS)
                device = lax.broadcasted_iota(jnp.int32, rows.shape, 0)
                for x in range(2):
                    kept = jnp.where((device // 2) % 2 == x, rows, 0.0)
                    source = lax.broadcasted_iota(jnp.int32, (SMALL_ROWS, rows.shape[0]), 1)
                    target = lax.broadcasted_iota(jnp.int32, (SMALL_ROWS, rows.shape[0]), 0)
                    take = (source == (target // 2) * 4 + x * 2 + target % 2).astype(F32)
                    small_ref[x] = dot_nn(take.astype(BF), kept.astype(BF))
            if index >= 2:
                finish_copies(up(index - 2))
            held[index % 2] = dot_tn(yr_ref[...], dur_ref[...]).astype(BF)
            run_copies(up(index))
            if index == steps - 1:
                finish_copies(up(index - 1))
                finish_copies(up(index))


def grad_up(place_vec, yr, sums, db1, dur, entries, z_size, vec_len, after):
    tokens = yr.shape[0]
    if entries:
        shapes = piece_shapes(z_size, 192) + [jax.ShapeDtypeStruct((2, SMALL_ROWS, HALF), F32)]
        specs = [ANY] * 3 + [whole((2, SMALL_ROWS, HALF))]

        def columns(g, p):
            return (0, (p[3] ^ (1 - g // 2)) * 2 + g % 2)
    else:
        shapes = [jax.ShapeDtypeStruct((D, FF), BF)]
        specs = [pl.BlockSpec((D, D), lambda g, p: (0, g))]

        def columns(g, p):
            return (0, g)

    return call(
        partial(grad_up_kernel, (entries, z_size, vec_len)),
        place_vec,
        (yr, sums, db1, dur),
        after,
        [whole((tokens, D)), whole((8, D)), whole((1, FF)), pl.BlockSpec((tokens, D), columns)],
        specs,
        shapes,
        (FF // D,),
        [pltpu.VMEM((2, D, D), BF), pltpu.SemaphoreType.DMA((2, 2, 4 * z_size))] if entries else [],
        2 * tokens * D * FF,
        "grad_up",
    )


def input_grad_kernel(place_ref, base_ref, weight_ref, *rest):
    *grads, out_ref = rest
    total = base_ref[...]
    for flip in range(2):
        col = pl.multiple_of(((place_ref[2] % 2) ^ flip) * HALF, 128)
        for j in range(3):
            total = total + dot_nt(grads[flip * 3 + j][...], weight_ref[j, :, pl.ds(col, HALF)])
    out_ref[...] = total


def input_grad(place_vec, base, near, far, weight, after):
    tokens = base.shape[0]
    tile = pl.BlockSpec((TILE, D), lambda t, p: (t, 0))
    half = pl.BlockSpec((TILE, HALF), lambda t, p: (t, 0))
    return call(
        input_grad_kernel,
        place_vec,
        (base, weight, *near, *far),
        after,
        [tile, whole((3, D, D))] + [half] * 6,
        tile,
        jax.ShapeDtypeStruct((tokens, D), F32),
        (tokens // TILE,),
        [],
        6 * tokens * D * D,
        "input_grad",
    )


def split_vector(vec_values):
    split_points = [D, D + FF, 2 * D + FF, 3 * D + FF, 4 * D + FF, 5 * D + FF]
    return jnp.split(vec_values, split_points)


def squares_kernel(place_ref, *refs):
    *parts, small_ref, out_ref = refs
    total = 0.0
    for ref in parts:
        value = ref[...]
        total = total + jnp.sum(jnp.sum(value * value, axis=0, keepdims=True), axis=1, keepdims=True)
    small = small_ref[...]
    total = total + jnp.sum(small * small, axis=1, keepdims=True)
    out_ref[...] = jnp.broadcast_to(total[None], out_ref.shape)


def sum_squares(place, place_vec, parts, small):
    operands = (*parts, small)
    shape = jax.ShapeDtypeStruct((place.total, 8, 128), F32)
    own = call(
        squares_kernel, place_vec, operands, (), [whole(w.shape) for w in operands], whole(shape.shape), shape,
        (1,), [], 1000, "squares",
    )
    return lax.all_to_all(own, AXES, split_axis=0, concat_axis=0, tiled=True)


def final_kernel(vec_len, place_ref, got_ref, *refs):
    *parts, sum_ref, vec_ref, bias_ref, out_ref, held = refs
    total = 0.0
    for entry in range(got_ref.shape[0]):
        total = total + got_ref[entry].astype(F32)
    for j in range(3):
        sum_ref[j] = total[j * 48 : (j + 1) * 48]
    held[...] = total[144:]
    small = held[pl.ds((place_ref[0] * 2 + place_ref[1]) * 2 + place_ref[3], 1), :]
    vec_ref[...] = small[:, :vec_len]
    bias_ref[...] = small[:, vec_len : vec_len + bias_ref.shape[1]]
    squares = jnp.sum(small * small, axis=1, keepdims=True)
    for value in [total[:144]] + [ref[...] for ref in parts]:
        squares = squares + jnp.sum(jnp.sum(value * value, axis=0, keepdims=True), axis=1, keepdims=True)
    out_ref[...] = jnp.broadcast_to(squares[None], out_ref.shape)


def final_sums(place, place_vec, pieces, parts, vec_len, bias_len, after):
    got = lax.all_to_all(pieces, "rows", split_axis=0, concat_axis=0, tiled=True)
    operands = (got, *parts)
    shapes = [(3, 48, HALF), (1, vec_len), (1, bias_len), (place.total, 8, 128)]
    *sums, own = call(
        partial(final_kernel, vec_len), place_vec, operands, after, [whole(w.shape) for w in operands],
        [whole(shape) for shape in shapes], [jax.ShapeDtypeStruct(shape, F32) for shape in shapes],
        (1,), [pltpu.VMEM((SMALL_ROWS, HALF), F32)], 1000, "final", 16 * 1024 * 1024,
    )
    return *sums, lax.all_to_all(own, AXES, split_axis=0, concat_axis=0, tiled=True)


def adam_kernel(rates, place_ref, squares_ref, *refs):
    count = len(rates)
    norm = jnp.sqrt(jnp.sum(squares_ref[...], axis=0)[0:1, 0:1])
    refs[5 * count][...] = norm
    clip_limit = CLIP_RMS * math.sqrt(PARAMS)
    factor = clip_limit / jnp.maximum(norm, clip_limit)
    for index, rate in enumerate(rates):
        weight, first, second, average, gradient = (refs[index * 5 + i][...] for i in range(5))
        clipped = gradient * factor.reshape((1,) * gradient.ndim)
        first_new = BETA_ONE * first + (1.0 - BETA_ONE) * clipped
        second_new = BETA_TWO * second + (1.0 - BETA_TWO) * clipped * clipped
        first_hat = first_new / (1.0 - BETA_ONE**STEP)
        second_hat = second_new / (1.0 - BETA_TWO**STEP)
        weight_new = weight - rate * (first_hat / (jnp.sqrt(second_hat) + ADAM_EPS) + WEIGHT_DECAY * weight)
        outs = refs[5 * count + 1 + index * 4 : 5 * count + 5 + index * 4]
        outs[0][...] = weight_new
        outs[1][...] = first_new
        outs[2][...] = second_new
        outs[3][...] = AVERAGE_KEEP * average + (1.0 - AVERAGE_KEEP) * weight_new


def adam(place_vec, squares, groups, rates):
    flat = [value for group in groups for value in group]
    shapes = [jax.ShapeDtypeStruct((1, 1), F32)]
    shapes += [jax.ShapeDtypeStruct(group[0].shape, F32) for group in groups for _ in range(4)]
    return call(
        partial(adam_kernel, rates), place_vec, (squares, *flat), (),
        [whole(value.shape) for value in (squares, *flat)], [whole(value.shape) for value in shapes], shapes,
        (1,), [], 1000, "adam",
    )


def body(
    tokens,
    cotangent,
    bucket,
    lengths,
    in_weight,
    in_first,
    in_second,
    in_average,
    in_bias,
    bias_first,
    bias_second,
    bias_average,
    out_weight,
    out_first,
    out_second,
    out_average,
    up_weight,
    up_first,
    up_second,
    up_average,
    down_weight,
    down_first,
    down_second,
    down_average,
    vectors,
    vec_first,
    vec_second,
    vec_average,
):
    place = Place()
    n_rows, n_heads, total = place.n_rows, place.n_heads, place.total
    z_size = place.sizes["z"]
    share = cotangent.shape[0]
    row_index, head_index = lax.axis_index("rows"), lax.axis_index("heads")
    blocks = share // CAP_L
    own_kinds = lax.dynamic_slice_in_dim(bucket, head_index * blocks, blocks, 0)
    own_lengths = lax.dynamic_slice_in_dim(lengths, head_index * blocks, blocks, 0)
    own_blocks = jnp.concatenate([own_kinds[:, None], own_lengths], axis=1).reshape(-1)
    place_vec = jnp.concatenate([jnp.stack([place.z, place.y, place.x, place.c]), own_blocks]).astype(jnp.int32)
    in_rows, in_cols = in_weight.shape[1], in_weight.shape[2]
    out_rows, down_rows = out_weight.shape[0], down_weight.shape[0]
    bias_len, vec_len = in_bias.size, vectors.size
    pieces_fit = in_rows == 96 and in_cols == HALF // 2 and out_rows == 24 and n_heads == 4

    small = jnp.concatenate([vectors, in_bias.reshape(-1)])
    if pieces_fit:
        piece, ffn_piece = make_pieces(
            place, place_vec, in_weight, out_weight, up_weight, down_weight, small[None, :]
        )
        entries = gather_pieces(place, piece)
        ffn_all = lax.all_gather(ffn_piece, AXES, axis=0)
        buffers = [entry[0] for entry in entries]
        layout = [(None,) + entry[1:] for entry in entries]
        in_buffers, layer_buffers = buffers, buffers + [ffn_all]
    else:
        layout = ()
        all_in = lax.all_gather(in_weight.astype(BF), "rows", axis=1, tiled=True)
        all_in = lax.all_gather(all_in, "heads", axis=2, tiled=True)
        all_out, all_up, all_down = (
            lax.all_gather(w.astype(BF), AXES, axis=0, tiled=True)
            for w in (out_weight, up_weight, down_weight)
        )
        layer_buffers = [all_out, all_up, all_down]
        all_small = lax.all_gather(small.astype(BF), AXES, axis=0).astype(F32)
        bias_out, bias_up, bias_down, gain_one, shift_one, gain_two, shift_two = split_vector(
            all_small[:, :vec_len].reshape(-1)
        )
        bias_shape = (n_rows, n_heads) + in_bias.shape
        bias_all = all_small[:, vec_len:].reshape(bias_shape).transpose(2, 1, 3, 0, 4).reshape(2, D)
        bias_in = jnp.stack([bias_all[0], jnp.zeros_like(bias_all[0]), bias_all[1]])[:, None, :]
        vec_rows = jnp.stack([bias_out, bias_down, gain_one, shift_one, gain_two, shift_two, bias_out, bias_out])
        in_buffers = [all_in, bias_in]

    q, k, v, o, lse, *small_rows = attend(
        place_vec, tokens, share, layout, in_buffers, z_size, vec_len, n_rows
    )
    vec_rows, b1, all_in = small_rows if pieces_fit else (vec_rows, bias_up[None, :], all_in)
    layer_out, dr1, yr, dur, dor, sums, db1, *grads_down = layer(
        place_vec, o, tokens, cotangent, vec_rows, b1, layout, layer_buffers, z_size, n_heads
    )

    def back(vec, flip, *after):
        return attend_back(
            place_vec, q, k, v, dor, lse, tokens, vec, vec_len, z_size, pieces_fit, flip, after
        )

    if pieces_fit:
        down_near, down_far, down_far_first = grads_down
        parts = (slice(0, CUT_ROWS), slice(CUT_ROWS, None))
        down_c = place.send(down_far_first, "c")
        down_go = [low_sum(down_near[1, :, :, part], down_c[:, :, part]) for part in parts]
        got_first = [place.send(part, digit) for part, digit in zip(down_go, "xy")]
        down_c = place.send(down_far, "c")
        up_near, up_far, up_far_x, vec_small = grad_up(
            place_vec, yr, sums, db1, dur, layout, z_size, vec_len, tuple(down_go)
        )

        def down_terms(index, flip):
            part = parts[index]
            return down_near[0, flip, :, part], down_c[flip, :, part], got_first[index][flip]

        down_next = [low_sum(*down_terms(index, 1)) for index in range(2)]
        got_second = [place.send(part, digit) for part, digit in zip(down_next, "yx")]
        up_far_x = gate(place_vec, up_far_x, tuple(down_next))
        up_x = low_sum(up_near[1], place.send(up_far_x, "c"))
        got_up_x = place.send(up_x, "x")
        up_c = place.send(up_far, "c")
        down = jnp.concatenate([low_sum(*down_terms(index, 0), got_second[index]) for index in range(2)], axis=1)
        down_sums = trade(place, down, "z")
        other = back(vec_small, 1, up_x, down)

        far_c = place.send(other[4], "c")
        far_x = low_sum(other[3], far_c)
        got_far_x = place.send(far_x, "x")
        up = low_sum(up_near[0], up_c, got_up_x)
        up_sums = trade(place, up, "zy")
        mine = back(vec_small, 0, far_x, up, down_sums)

        near_c = place.send(mine[4], "c")
        near = low_sum(mine[3], near_c, got_far_x)
        token_grad = input_grad(place_vec, dr1, mine[:3], other[:3], all_in, (near,))

        in_sum, sum_vec, sum_bias, squares = final_sums(
            place, place_vec, near, (down_sums, up_sums), vec_len, bias_len, (token_grad,)
        )
        sum_down = jnp.concatenate([down_sums[:96], down_sums[96:192]], axis=1)
        sum_up = jnp.concatenate([up_sums[at : at + 48] for at in range(0, 192, 48)], axis=1)
        sum_up = swap_halves(place, sum_up, 0, 1)
        sum_out = swap_halves(place, down_sums[192:], 0, 1)
        sum_in = swap_halves(place, in_sum, 2, 1)
        sum_bias = sum_bias.reshape(in_bias.shape)
    else:
        def spread(value):
            return lax.psum_scatter(value, AXES, scatter_dimension=0, tiled=True).astype(F32)

        def join(far, near, axis):
            return jnp.where(
                place.x == 0, jnp.concatenate([near, far], axis=axis), jnp.concatenate([far, near], axis=axis)
            )

        grads_up = grad_up(place_vec, yr, sums, db1, dur, layout, z_size, vec_len, ())
        unused = jnp.zeros((2, SMALL_ROWS, HALF), F32)
        grad_vec = jnp.concatenate([sums[0], db1[0], *(sums[i] for i in range(1, 6))])
        other, mine = back(unused, 1), back(unused, 0)
        token_grad = input_grad(place_vec, dr1, mine[:3], other[:3], all_in, ())
        grad_in = join(other[3], mine[3], 2)
        sum_in = lax.psum_scatter(grad_in, "heads", scatter_dimension=2, tiled=True)
        sum_in = lax.psum_scatter(sum_in, "rows", scatter_dimension=1, tiled=True).astype(F32)
        sum_up, sum_out, sum_down = spread(grads_up[0]), spread(grads_down[1]), spread(grads_down[0])
        sum_vec = lax.psum_scatter(grad_vec, AXES, scatter_dimension=0, tiled=True)
        grad_bias = join(other[4], mine[4], 1).reshape(2, n_heads * in_bias.shape[1], -1)
        sum_bias = lax.psum_scatter(grad_bias, "heads", scatter_dimension=1, tiled=True)
        sum_bias = lax.psum_scatter(sum_bias, "rows", scatter_dimension=2, tiled=True)

        flat_small = jnp.concatenate([sum_vec, sum_bias.reshape(-1)])[None, :]
        parts = (sum_in.reshape(-1, in_cols), sum_out, sum_up, sum_down)
        squares = sum_squares(place, place_vec, parts, flat_small)
    row = (1, vec_len)
    grad_norm, *new = adam(
        place_vec,
        squares,
        (
            (in_weight, in_first, in_second, in_average, sum_in),
            tuple(v.transpose(1, 0, 2) for v in (in_bias, bias_first, bias_second, bias_average, sum_bias)),
            (out_weight, out_first, out_second, out_average, sum_out),
            (up_weight, up_first, up_second, up_average, sum_up),
            (down_weight, down_first, down_second, down_average, sum_down),
            tuple(value.reshape(row) for value in (vectors, vec_first, vec_second, vec_average, sum_vec)),
        ),
        (LEARN_RATE,) * 5 + (VECTOR_RATE,),
    )
    return (
        layer_out,
        token_grad,
        grad_norm[0, 0],
        *new[:4],
        *(value.transpose(1, 0, 2) for value in new[4:8]),
        *new[8:20],
        *(value.reshape(vec_len) for value in new[20:]),
    )


def solution(mesh):
    in_specs = (
        P("rows", None),
        P(("rows", "heads"), None),
        P("rows"),
        P("rows", None),
        P(None, "rows", "heads"),
        P(None, "rows", "heads"),
        P(None, "rows", "heads"),
        P(None, "rows", "heads"),
        P(None, "heads", "rows"),
        P(None, "heads", "rows"),
        P(None, "heads", "rows"),
        P(None, "heads", "rows"),
        P(("rows", "heads"), None),
        P(("rows", "heads"), None),
        P(("rows", "heads"), None),
        P(("rows", "heads"), None),
        P(("rows", "heads"), None),
        P(("rows", "heads"), None),
        P(("rows", "heads"), None),
        P(("rows", "heads"), None),
        P(("rows", "heads"), None),
        P(("rows", "heads"), None),
        P(("rows", "heads"), None),
        P(("rows", "heads"), None),
        P(("rows", "heads")),
        P(("rows", "heads")),
        P(("rows", "heads")),
        P(("rows", "heads")),
    )
    out_specs = (
        P(("rows", "heads"), None),
        P(("rows", "heads"), None),
        P(),
        P(None, "rows", "heads"),
        P(None, "rows", "heads"),
        P(None, "rows", "heads"),
        P(None, "rows", "heads"),
        P(None, "heads", "rows"),
        P(None, "heads", "rows"),
        P(None, "heads", "rows"),
        P(None, "heads", "rows"),
        P(("rows", "heads"), None),
        P(("rows", "heads"), None),
        P(("rows", "heads"), None),
        P(("rows", "heads"), None),
        P(("rows", "heads"), None),
        P(("rows", "heads"), None),
        P(("rows", "heads"), None),
        P(("rows", "heads"), None),
        P(("rows", "heads"), None),
        P(("rows", "heads"), None),
        P(("rows", "heads"), None),
        P(("rows", "heads"), None),
        P(("rows", "heads")),
        P(("rows", "heads")),
        P(("rows", "heads")),
        P(("rows", "heads")),
    )
    return jax.shard_map(body, mesh=mesh, in_specs=in_specs, out_specs=out_specs, check_vma=False)
```

```python
from functools import partial
import math

import jax
import jax.numpy as jnp
from jax import lax
from jax.experimental import pallas as pl
from jax.experimental.pallas import tpu as pltpu
from jax.sharding import PartitionSpec as P

D = 768
HD = 64
FF = 3072
CAP_L = 512
CAP_M = 128
CAP_S = 64
STEP = 10
ROWS_BLK = 8
PARAMS = 7087104

LN_EPS = 1e-05
LEARN_RATE = 0.1
VECTOR_RATE = 0.3
BETA_ONE = 0.9
BETA_TWO = 0.999
ADAM_EPS = 1e-08
WEIGHT_DECAY = 0.01
AVERAGE_KEEP = 0.75
CLIP_RMS = 0.001

AXES = ("rows", "heads")
BF = jnp.bfloat16
F32 = jnp.float32
VMEM_BYTES = 58 * 1024 * 1024
GROUP = 256
HALF = D // 2
PACK_VEC = 16


def dot_nn(left, right):
    return lax.dot_general(left, right, (((1,), (0,)), ((), ())), preferred_element_type=F32)


def dot_nt(left, right):
    return lax.dot_general(left, right, (((1,), (1,)), ((), ())), preferred_element_type=F32)


def dot_tn(left, right):
    return lax.dot_general(left, right, (((0,), (0,)), ((), ())), preferred_element_type=F32)


def kernel_params(steps=1, vmem=VMEM_BYTES):
    return pltpu.CompilerParams(
        vmem_limit_bytes=vmem, dimension_semantics=("arbitrary",) * steps
    )


def whole(shape):
    return pl.BlockSpec(shape, lambda *_: (0,) * len(shape))


ANY = pl.BlockSpec(memory_space=pl.ANY)


def call(kernel, place_vec, args, after, in_specs, out_specs, out_shape, grid, scratch, flops, name, vmem=VMEM_BYTES):
    def run(place_ref, *refs):
        return kernel(place_ref, *refs[len(after) :])

    return pl.pallas_call(
        run,
        grid_spec=pltpu.PrefetchScalarGridSpec(
            num_scalar_prefetch=1,
            grid=grid,
            in_specs=[ANY] * len(after) + in_specs,
            out_specs=out_specs,
            scratch_shapes=scratch,
        ),
        out_shape=out_shape,
        compiler_params=kernel_params(len(grid), vmem),
        cost_estimate=pl.CostEstimate(flops=flops // 1000, bytes_accessed=1024, transcendentals=0),
        name=name,
    )(place_vec, *after, *args)


def gate(place_vec, value, after):
    def run(place_ref, *refs):
        pass

    return pl.pallas_call(
        run,
        grid_spec=pltpu.PrefetchScalarGridSpec(
            num_scalar_prefetch=1, grid=(1,), in_specs=[ANY] * (len(after) + 1), out_specs=ANY
        ),
        out_shape=jax.ShapeDtypeStruct(value.shape, value.dtype),
        input_output_aliases={1: 0},
        compiler_params=kernel_params(),
        cost_estimate=pl.CostEstimate(flops=1, bytes_accessed=1, transcendentals=0),
        name="gate",
    )(place_vec, value, *after)


class Place:
    def __init__(self):
        self.n_rows = lax.axis_size("rows")
        self.n_heads = lax.axis_size("heads")
        self.total = self.n_rows * self.n_heads
        self.sizes = {"z": self.n_rows // 2, "y": 2, "x": self.n_heads // 2, "c": 2}
        self.strides = {"c": 1, "x": 2, "y": self.n_heads, "z": 2 * self.n_heads}
        row, head = lax.axis_index("rows"), lax.axis_index("heads")
        self.z, self.y = row // 2, row % 2
        self.x, self.c = head // 2, head % 2

    def send(self, value, digit, shift=1):
        size, stride = self.sizes[digit], self.strides[digit]
        pairs = []
        for device in range(self.total):
            own = (device // stride) % size
            pairs.append((device, device + ((own + shift) % size - own) * stride))
        return lax.ppermute(value, AXES, pairs)


def gather_pieces(place, piece):
    z_size = place.sizes["z"]
    column = jnp.stack([piece] + [place.send(piece, "z", shift) for shift in range(1, z_size)])
    from_x = place.send(column, "x")
    from_y = place.send(column, "y")
    cut = z_size // 2
    diag_low = place.send(from_x[:cut], "y")
    diag_high = place.send(from_y[cut:], "x")
    shifts = tuple(range(z_size))
    near = [
        (column, shifts, 0, 0, 0),
        (from_x, shifts, 0, 1, 0),
        (from_y, shifts, 1, 0, 0),
        (diag_low, shifts[:cut], 1, 1, 0),
        (diag_high, shifts[cut:], 1, 1, 0),
    ]
    far = [(place.send(buffer, "c"), s, y, x, 1) for buffer, s, y, x, _ in near]
    return near + far


def pick(value, index, axis):
    return lax.dynamic_index_in_dim(value, index, axis, keepdims=False)


def low_sum(*parts):
    return sum(part.astype(F32) for part in parts).astype(BF)


def trade(place, value, digits):
    steps = [0]
    for digit in digits:
        steps = [step + i * place.strides[digit] for step in steps for i in range(place.sizes[digit])]
    groups = [
        [device + step for step in steps]
        for device in range(place.total)
        if all((device // place.strides[d]) % place.sizes[d] == 0 for d in digits)
    ]
    got = lax.all_to_all(value, AXES, split_axis=0, concat_axis=0, tiled=True, axis_index_groups=groups)
    return jnp.sum(got.astype(F32), axis=0)


def swap_halves(place, value, cut_axis, join_axis):
    size = value.shape[cut_axis] // 2
    keep = lax.dynamic_slice_in_dim(value, place.c * size, size, cut_axis)
    give = lax.dynamic_slice_in_dim(value, (1 - place.c) * size, size, cut_axis)
    got = place.send(give, "c")
    first = jnp.where(place.c == 0, keep, got)
    second = jnp.where(place.c == 0, got, keep)
    return jnp.concatenate([first, second], axis=join_axis)


GIVE_ROWS = 144


def split_kernel(place_ref, in_ref, out_ref, up_ref, keep_ref, give_ref):
    zero = jnp.zeros((8, D), BF)
    for away, ref in enumerate((keep_ref, give_ref)):
        core = place_ref[3] ^ away
        for j in range(3):
            ref[0:48, j * 256 : j * 256 + 192] = in_ref[j, pl.ds(pl.multiple_of(core * 48, 8), 48), :].astype(BF)
            ref[0:48, j * 256 + 192 : (j + 1) * 256] = zero[:, :64].repeat(6, axis=0)
        ref[48:72, 0:HALF] = out_ref[:, pl.ds(pl.multiple_of(core * HALF, 128), HALF)].astype(BF)
        ref[48:72, HALF:] = jnp.zeros((24, HALF), BF)
        for t in range(2):
            col = pl.multiple_of(core * (FF // 2) + t * D, 128)
            ref[80 + t * 32 : 104 + t * 32, :] = up_ref[:, pl.ds(col, D)].astype(BF)
        for at in (72, 104, 136):
            ref[at : at + 8, :] = zero


def join_kernel(place_ref, keep_ref, got_ref, down_ref, small_ref, piece_ref, ffn_ref):
    first = place_ref[3] == 0
    keep, got = keep_ref[...], got_ref[...]
    low = jnp.where(first, keep, got)
    high = jnp.where(first, got, keep)
    for j in range(3):
        cols = slice(j * 256, j * 256 + 192)
        piece_ref[j * 48 : (j + 1) * 48, :] = jnp.concatenate([low[0:48, cols], high[0:48, cols]], axis=1)
    piece_ref[144:168, :] = low[48:72, :HALF]
    piece_ref[168:192, :] = high[48:72, :HALF]
    small = jnp.concatenate([small_ref[...], jnp.zeros((1, HALF - small_ref.shape[1]), F32)], axis=1)
    row = lax.broadcasted_iota(jnp.int32, (PACK_VEC, HALF), 0)
    piece_ref[192:208, :] = jnp.where(row == 0, small, 0.0).astype(BF)
    for t in range(2):
        ffn_ref[t * 48 : t * 48 + 24, :] = low[80 + t * 32 : 104 + t * 32, :]
        ffn_ref[t * 48 + 24 : t * 48 + 48, :] = high[80 + t * 32 : 104 + t * 32, :]
    ffn_ref[96:192, :] = down_ref[...].astype(BF)


def make_pieces(place, place_vec, in_weight, out_weight, up_weight, down_weight, small):
    half = jax.ShapeDtypeStruct((GIVE_ROWS, D), BF)
    weights = (in_weight, out_weight, up_weight)
    keep, give = call(
        split_kernel, place_vec, weights, (), [whole(w.shape) for w in weights],
        [whole(half.shape)] * 2, [half] * 2, (1,), [], 1000, "split",
    )
    operands = (keep, place.send(give, "c"), down_weight, small)
    shapes = [jax.ShapeDtypeStruct((208, HALF), BF), jax.ShapeDtypeStruct((192, D), BF)]
    return call(
        join_kernel, place_vec, operands, (), [whole(w.shape) for w in operands],
        [whole(w.shape) for w in shapes], shapes, (1,), [], 1000, "join",
    )


def run_copies(copies):
    for copy in copies:
        copy.start()
    return copies


def finish_copies(copies):
    for copy in copies:
        copy.wait()


def piece_origin(place_ref, z_size, entry, index):
    _, shifts, y, x, c = entry
    shift = shifts[index]
    z_at = lax.rem(place_ref[0] + (z_size - shift), z_size)
    return z_at, place_ref[1] ^ y, place_ref[2] ^ x, place_ref[3] ^ c


def mask_block(place_ref, block):
    kind = place_ref[4 + block * (ROWS_BLK + 1)]
    bits = jnp.where(kind == 0, 9, jnp.where(kind == 1, 7, 6))
    place = lax.broadcasted_iota(jnp.int32, (CAP_L, 2 * HD), 0)
    lane = lax.broadcasted_iota(jnp.int32, (1, 2 * HD), 1) % HD
    length = jnp.zeros((1, 2 * HD), jnp.int32)
    for row in range(ROWS_BLK):
        length = jnp.where(lane == row, place_ref[4 + block * (ROWS_BLK + 1) + 1 + row], length)
    row = lax.shift_right_logical(place, jnp.broadcast_to(bits, place.shape))
    within = place - lax.shift_left(row, jnp.broadcast_to(bits, place.shape))
    same = row == lane
    used = lane < ROWS_BLK
    closed = used & ~(same & (within < length))
    return jnp.where(closed, -1e30, 0.0).astype(BF), jnp.where(same & used, 1.0, 0.0).astype(BF)


def lane_half(rows):
    return lax.broadcasted_iota(jnp.int32, (rows, 2 * HD), 1) < HD


def div_mod(values, divisor):
    quotient = jnp.floor((values + 0.5) * (1.0 / divisor))
    return quotient, values - quotient * divisor


def counted(shape, axis):
    return lax.broadcasted_iota(jnp.int32, shape, axis).astype(F32)


def spread_small(small, lane_of, device_of):
    devices, lanes = small.shape
    column = counted((1, D), 1)
    hit = jnp.where(counted((lanes, D), 0) == lane_of(column), 1.0, 0.0).astype(BF)
    taken = jnp.where(counted((devices, D), 0) == device_of(column), dot_nn(small, hit), 0.0)
    return jnp.sum(taken, axis=0, keepdims=True)


def fill_small(small, vec_len, n_rows, bias_ref, vec_ref, b1_ref):
    n_heads = small.shape[0] // n_rows
    per_device = D // n_heads // HD
    width = HD // n_rows

    def bias_lane(j):
        def lane(col):
            head, place = div_mod(div_mod(col, per_device * HD)[1], HD)
            return vec_len + (j * per_device + head) * width + div_mod(place, width)[1]

        return lane

    def bias_device(col):
        return div_mod(div_mod(col, HD)[1], width)[0] * n_heads + div_mod(col, per_device * HD)[0]

    bias_ref[0] = spread_small(small, bias_lane(0), bias_device)
    bias_ref[1] = jnp.zeros((1, D), F32)
    bias_ref[2] = spread_small(small, bias_lane(1), bias_device)
    for index in range(10):
        start = index * D
        row = spread_small(small, lambda col: div_mod(start + col, vec_len)[1], lambda col: div_mod(start + col, vec_len)[0])
        if 1 <= index <= 4:
            b1_ref[:, (index - 1) * D : index * D] = row
        else:
            at = 0 if index == 0 else index - 4
            vec_ref[at : at + 1, :] = row


def attend_kernel(layout, place_ref, x_ref, *rest):
    entries, z_size, vec_len, n_rows = layout
    n_in = len(entries) if entries else 2
    sources = rest[:n_in]
    q_ref, k_ref, v_ref, o_ref, lse_ref, *more = rest[n_in:]
    if entries:
        vec_ref, b1_ref, whole_ref, weight, bias_ref, small, sems, sem_out = more
    else:
        weight, bias_ref, sems = more
    group = pl.program_id(0)

    @pl.when(group == 0)
    def _():
        copies = []
        if entries:
            for entry, source in zip(entries, sources):
                for index in range(len(entry[1])):
                    z_at, y_at, x_at, c_at = piece_origin(place_ref, z_size, entry, index)
                    row = pl.multiple_of((z_at * 2 + y_at) * 96 + c_at * 48, 16)
                    col = pl.multiple_of(x_at * HALF, 128)
                    device = ((z_at * 2 + y_at) * 2 + x_at) * 2 + c_at
                    copies.append(
                        pltpu.make_async_copy(
                            source.at[index, pl.ds(192, PACK_VEC), :], small.at[device], sems.at[len(copies)]
                        )
                    )
                    for j in range(3):
                        copies.append(
                            pltpu.make_async_copy(
                                source.at[index, pl.ds(j * 48, 48), :],
                                weight.at[j, pl.ds(row, 48), pl.ds(col, HALF)],
                                sems.at[len(copies)],
                            )
                        )
        else:
            copies.append(pltpu.make_async_copy(sources[0], weight, sems.at[0]))
            copies.append(pltpu.make_async_copy(sources[1], bias_ref, sems.at[1]))
        finish_copies(run_copies(copies))
        if entries:
            shares = jnp.sum(small[...].astype(F32), axis=1).astype(BF)
            fill_small(shares, vec_len, n_rows, bias_ref, vec_ref, b1_ref)
            pltpu.make_async_copy(weight, whole_ref, sem_out).start()

    if entries:

        @pl.when(group == pl.num_programs(0) - 1)
        def _():
            pltpu.make_async_copy(weight, whole_ref, sem_out).wait()

    x = x_ref[...]
    at = pl.multiple_of(group * GROUP, GROUP)
    for j, out in enumerate((q_ref, k_ref, v_ref)):
        out[...] = (dot_nn(x, weight[j, :, pl.ds(at, GROUP)]) + bias_ref[j, :, pl.ds(at, GROUP)]).astype(BF)
    low = lane_half(CAP_L)
    for block in range(x_ref.shape[0] // CAP_L):
        rows = slice(block * CAP_L, (block + 1) * CAP_L)
        key_mask, query_row = mask_block(place_ref, block)
        for pair in range(GROUP // 128):
            cols = slice(pair * 128, (pair + 1) * 128)
            q2, k2 = q_ref[rows, cols] * BF(HD ** -0.5), k_ref[rows, cols]
            v2t = v_ref[rows, cols].T
            outs = []
            for side in range(2):
                here = low if side == 0 else ~low
                s = dot_nt(jnp.where(here, k2, key_mask), jnp.where(here, q2, query_row))
                peak = jnp.max(s, axis=0, keepdims=True)
                e = jnp.exp(s - peak)
                total = jnp.sum(e, axis=0, keepdims=True)
                o = dot_nn(v2t[side * HD : (side + 1) * HD], e.astype(BF))
                outs.append(o * (1.0 / total))
                slot = block * 2 + side
                lse_ref[pair, slot : slot + 1, :] = peak + jnp.log(total)
            o_ref[rows, cols] = jnp.concatenate(outs, axis=0).T.astype(BF)


def own_tokens(tokens, tile):
    return pl.BlockSpec((tile, D), lambda t, p: ((p[2] * 2 + p[3]) * (tokens // tile) + (t if tile < tokens else 0), 0))


def attend(place_vec, x, tokens, entries, buffers, z_size, vec_len, n_rows):
    slots = tokens // CAP_L * 2
    block = pl.BlockSpec((tokens, GROUP), lambda g, p: (0, g))
    out_specs = [block] * 4 + [pl.BlockSpec((GROUP // 128, slots, CAP_L), lambda g, p: (g, 0, 0))]
    out_shape = [jax.ShapeDtypeStruct((tokens, D), BF)] * 4 + [jax.ShapeDtypeStruct((D // 128, slots, CAP_L), F32)]
    scratch = [pltpu.VMEM((3, D, D), BF), pltpu.VMEM((3, 1, D), F32)]
    n_copies = 2
    if entries:
        pieces = sum(len(entry[1]) for entry in entries)
        n_copies = 4 * pieces
        out_specs += [whole((8, D)), whole((1, FF)), ANY]
        out_shape += [jax.ShapeDtypeStruct((8, D), F32), jax.ShapeDtypeStruct((1, FF), F32)]
        out_shape += [jax.ShapeDtypeStruct((3, D, D), BF)]
        scratch += [pltpu.VMEM((pieces, PACK_VEC, HALF), BF)]
    return call(
        partial(attend_kernel, (entries, z_size, vec_len, n_rows)),
        place_vec,
        (x, *buffers),
        (),
        [own_tokens(tokens, tokens)] + [ANY] * len(buffers),
        out_specs,
        out_shape,
        (D // GROUP,),
        scratch + [pltpu.SemaphoreType.DMA((n_copies,))] + [pltpu.SemaphoreType.DMA] * bool(entries),
        10 * tokens * D * D,
        "attend",
    )


def small_bias(sums, vec_len, n_rows):
    width = HD // n_rows
    heads = HALF // 2 // HD
    out = 0.0
    col = counted((1, HALF), 1)
    mine = counted((2 * n_rows, HALF), 0) == div_mod(div_mod(col, HD)[1], width)[0] * 2 + div_mod(col, heads * HD)[0]
    head, place = div_mod(div_mod(counted((HALF, 1), 0), heads * HD)[1], HD)
    for j in range(2):
        hit = counted((HALF, HALF), 1) == vec_len + (j * heads + head) * width + div_mod(place, width)[1]
        spread = jnp.where(mine, sums[j : j + 1, :], 0.0).astype(BF)
        out = out + dot_nn(spread, jnp.where(hit, 1.0, 0.0).astype(BF))
    return out


def attend_back_kernel(
    layout, flip, place_ref, q_ref, k_ref, v_ref, do_ref, lse_ref, x_ref, vec_ref,
    dq_ref, dk_ref, dv_ref, *rest,
):
    z_size, split, vec_len = layout
    low = lane_half(CAP_L)
    sum_q, sum_v = [], []
    masks = [mask_block(place_ref, block) for block in range(q_ref.shape[0] // CAP_L)]
    for pair in range(HALF // 128):
        cols = slice(pair * 128, (pair + 1) * 128)
        pair_q, pair_v = 0.0, 0.0
        for block in range(q_ref.shape[0] // CAP_L):
            rows = slice(block * CAP_L, (block + 1) * CAP_L)
            key_mask, query_row = masks[block]
            q2, k2 = q_ref[rows, cols] * BF(HD ** -0.5), k_ref[rows, cols]
            v2, do2 = v_ref[rows, cols], do_ref[rows, cols]
            k2t = k2.T
            dq_t, dk, dv = [], [], []
            for side in range(2):
                here = low if side == 0 else ~low
                slot = block * 2 + side
                s = dot_nt(jnp.where(here, k2, key_mask), jnp.where(here, q2, query_row))
                p = jnp.exp(s - lse_ref[pair, slot : slot + 1, :])
                dp = dot_nt(jnp.where(here, v2, BF(0)), do2)
                dv.append(dot_nn(p.astype(BF), do2))
                inner = jnp.sum(dp * p, axis=0, keepdims=True)
                ds = (p * (dp - inner)).astype(BF)
                dk.append(dot_nn(ds, q2))
                dq_t.append(dot_nn(k2t[side * HD : (side + 1) * HD], ds))
            dq_low = (jnp.concatenate(dq_t, axis=0).T * HD ** -0.5).astype(BF)
            dv_low = jnp.where(low, dv[0], dv[1]).astype(BF)
            dq_ref[rows, cols] = dq_low
            dk_ref[rows, cols] = jnp.where(low, dk[0], dk[1]).astype(BF)
            dv_ref[rows, cols] = dv_low
            pair_q = pair_q + col_sum(dq_low)
            pair_v = pair_v + col_sum(dv_low)
        sum_q.append(pair_q)
        sum_v.append(pair_v)
    x = x_ref[...]
    sums = jnp.concatenate([jnp.concatenate(sum_q, axis=1), jnp.concatenate(sum_v, axis=1)], axis=0)
    if not split:
        grad_ref, bias_ref = rest
        bias_ref[...] = sums
        for j, ref in enumerate((dq_ref, dk_ref, dv_ref)):
            grad_ref[j] = dot_tn(x, ref[...]).astype(BF)
        return
    *grad_refs, held, held_small, sems = rest
    held_small[...] = (vec_ref[0] + small_bias(sums, vec_len, 2 * z_size)).astype(BF)
    copies = []

    def scatter(source, rows, step):
        for row in range(2 * z_size):
            for away in range(2):
                core = place_ref[3] ^ away
                copies.append(
                    pltpu.make_async_copy(source(row, core), grad_refs[away].at[row, rows], sems.at[step, row * 2 + away])
                )
                copies[-1].start()

    scatter(lambda row, core: held_small, pl.ds(144, SMALL_ROWS), 3)
    for j, ref in enumerate((dq_ref, dk_ref, dv_ref)):
        held[j] = dot_tn(x, ref[...]).astype(BF)
        scatter(
            lambda row, core: held.at[j, pl.ds(pl.multiple_of(row * 96 + core * 48, 16), 48)], pl.ds(j * 48, 48), j
        )
    finish_copies(copies)


SMALL_ROWS = 16


def attend_back(place_vec, q, k, v, do, lse, x, vec, vec_len, z_size, split, flip, after):
    tokens = q.shape[0]
    slots = lse.shape[1]

    def half(g, p):
        return (0, (p[2] % 2) ^ flip)

    block = pl.BlockSpec((tokens, HALF), half)
    out_shape = [jax.ShapeDtypeStruct((tokens, HALF), BF)] * 3
    out_specs = [whole((tokens, HALF))] * 3
    if split:
        out_shape += [jax.ShapeDtypeStruct((2 * z_size, 144 + SMALL_ROWS, HALF), BF)] * 2
        out_specs += [ANY] * 2
        scratch = [
            pltpu.VMEM((3, D, HALF), BF),
            pltpu.VMEM((SMALL_ROWS, HALF), BF),
            pltpu.SemaphoreType.DMA((4, 4 * z_size)),
        ]
    else:
        out_shape += [jax.ShapeDtypeStruct((3, D, HALF), BF), jax.ShapeDtypeStruct((2, HALF), F32)]
        out_specs += [whole((3, D, HALF)), whole((2, HALF))]
        scratch = []
    return call(
        partial(attend_back_kernel, (z_size, split, vec_len), flip),
        place_vec,
        (q, k, v, do, lse, x, vec),
        after,
        [block] * 4
        + [pl.BlockSpec((HALF // 128, slots, CAP_L), lambda g, p: ((p[2] % 2) ^ flip, 0, 0))]
        + [own_tokens(tokens, tokens), pl.BlockSpec((1, SMALL_ROWS, HALF), lambda g, p: ((p[2] % 2) ^ flip, 0, 0))],
        out_specs,
        out_shape,
        (1,),
        scratch,
        14 * tokens * D * D,
        "attend_back",
    )


TILE = 256
CHUNK = 768
ERF_P = 0.3275911 / math.sqrt(2.0)
ERF_A = (0.254829592, -0.284496736, 1.421413741, -1.453152027, 1.061405429)
BELL_RATE = -0.5 * math.log2(math.e)
BELL_SCALE = 1.0 / math.sqrt(2.0 * math.pi)


def gelu_parts(u):
    bell = jnp.exp2(u * u * BELL_RATE)
    scale = 1.0 + ERF_P * jnp.abs(u)
    t = pl.reciprocal(scale, approx=True)
    t = t * (2.0 - scale * t)
    poly = ERF_A[4] * 0.5
    for term in ERF_A[3::-1]:
        poly = poly * t + term * 0.5
    below = poly * t * bell
    phi = jnp.where(u >= 0.0, 1.0 - below, below)
    return u * phi, phi + u * bell * BELL_SCALE


def normalise(values):
    center = values - jnp.mean(values, axis=-1, keepdims=True)
    scale = lax.rsqrt(jnp.mean(center * center, axis=-1, keepdims=True) + LN_EPS)
    return center * scale, scale


def norm_back(grad, gain, normal, scale):
    inner = grad * gain
    first = jnp.mean(inner, axis=-1, keepdims=True)
    second = jnp.mean(inner * normal, axis=-1, keepdims=True)
    return (inner - first - normal * second) * scale


def col_sum(values):
    return jnp.sum(values.astype(F32), axis=0, keepdims=True)


def ffn_copies(layout, place_ref, sources, wo, w1, w2, sems):
    entries, z_size, n_heads = layout
    count = [0]

    def copy(source, target):
        made = pltpu.make_async_copy(source, target, sems.at[count[0]])
        count[0] += 1
        made.start()
        return made

    if not entries:
        return [[copy(source, target)] for source, target in zip(sources, (wo, w1, w2))]
    to_out, to_up, to_down = [], [], []
    for entry, source in zip(entries, sources):
        for index in range(len(entry[1])):
            z_at, y_at, x_at, c_at = piece_origin(place_ref, z_size, entry, index)
            row = pl.multiple_of(((z_at * 2 + y_at) * (n_heads // 2) + x_at) * 48, 16)
            col = pl.multiple_of(c_at * HALF, 128)
            to_out.append(copy(source.at[index, pl.ds(144, 48), :], wo.at[pl.ds(row, 48), pl.ds(col, HALF)]))
    for device in range(sources[-1].shape[0]):
        chip, core = device // 2, device % 2
        for part in range(2):
            to_up.append(
                copy(
                    sources[-1].at[device, part * 48 : (part + 1) * 48, :],
                    w1.at[chip * 48 : (chip + 1) * 48, pl.ds(core * (FF // 2) + part * D, D)],
                )
            )
    for device in range(sources[-1].shape[0]):
        to_down.append(copy(sources[-1].at[device, 96:192, :], w2.at[device * 96 : (device + 1) * 96, :]))
    return to_out, to_up, to_down


def layer_kernel(layout, place_ref, o_ref, x_ref, cot_ref, vec_ref, b1_ref, *rest):
    n_in = len(layout[0]) + 1 if layout[0] else 3
    sources = rest[:n_in]
    z_ref, dr1_ref, yr_ref, dur_ref, dor_ref, sums_ref, db1_ref, *grad_refs = rest[n_in:-12]
    wo, w1, w2, hr, slope, dfr_all, dar_all, held, sems, sems_out, n1_all, scale_all = rest[-12:]
    step = pl.program_id(0)

    @pl.when(step == 0)
    def _():
        sums_ref[...] = jnp.zeros_like(sums_ref)
        db1_ref[...] = jnp.zeros_like(db1_ref)
        to_out, to_up, to_down = ffn_copies(layout, place_ref, sources, wo, w1, w2, sems)
        finish_copies(to_out)
        for at in range(0, x_ref.shape[0], TILE):
            rows = slice(at, at + TILE)
            r1 = x_ref[rows, :].astype(F32) + (dot_nn(o_ref[rows, :], wo[...]) + vec_ref[0:1, :])
            normal, scale = normalise(r1)
            n1_all[rows, :] = normal
            scale_all[rows, :] = scale
        finish_copies(to_up)
        finish_copies(to_down)

    b2, g1, c1, g2, c2 = (vec_ref[i : i + 1, :] for i in range(1, 6))
    at_rows = pl.ds(pl.multiple_of(step * TILE, TILE), TILE)
    n1, scale1 = n1_all[at_rows, :], scale_all[at_rows, :]
    y1 = n1 * g1 + c1
    yr = y1.astype(BF)
    yr_ref[...] = yr
    f = None
    for at in range(0, FF, CHUNK):
        cols = slice(at, at + CHUNK)
        u = dot_nn(yr, w1[:, cols]) + b1_ref[:, cols]
        act, rate = gelu_parts(u)
        act = act.astype(BF)
        hr[at_rows, cols] = act
        slope[:, cols] = rate
        part = dot_nn(act, w2[cols, :])
        f = part if f is None else f + part
    n2, scale2 = normalise(y1 + (f + b2))
    z_ref[...] = (n2 * g2 + c2).astype(BF)
    dz = cot_ref[...].astype(F32)
    dr2 = norm_back(dz, g2, n2, scale2)
    dfr = dr2.astype(BF)
    dfr_all[at_rows, :] = dfr
    sums_ref[1:2, :] += col_sum(dfr)
    sums_ref[4:5, :] += col_sum(dz * n2)
    sums_ref[5:6, :] += col_sum(dz)
    dy1 = dr2
    for at in range(0, FF, CHUNK):
        cols = slice(at, at + CHUNK)
        dur = (dot_nt(dfr, w2[cols, :]) * slope[:, cols]).astype(BF)
        dur_ref[:, cols] = dur
        db1_ref[:, cols] += col_sum(dur)
        dy1 = dy1 + dot_nt(dur, w1[:, cols])
    dr1 = norm_back(dy1, g1, n1, scale1)
    dr1_ref[...] = dr1
    dar = dr1.astype(BF)
    dar_all[at_rows, :] = dar
    sums_ref[0:1, :] += col_sum(dar)
    sums_ref[2:3, :] += col_sum(dy1 * n1)
    sums_ref[3:4, :] += col_sum(dy1)
    dor_ref[...] = dot_nt(dar, wo[...]).astype(BF)

    @pl.when(step == pl.num_programs(0) - 1)
    def _():
        pending = [[], []]
        for index in range(FF // D + 1):
            slot = index % 2
            finish_copies(pending[slot])
            if index < FF // D:
                held[slot] = dot_tn(hr[:, index * D : (index + 1) * D], dfr_all[...]).astype(BF)
            else:
                held[slot] = dot_tn(o_ref[...], dar_all[...]).astype(BF)
            pending[slot] = layer_copies(layout, place_ref, held.at[slot], grad_refs, index, sems_out.at[slot])
        for copies in pending:
            finish_copies(copies)


def piece_target(grad_refs, away, flip, row):
    near, far, far_other = grad_refs
    return near.at[flip, row] if not away else (far_other if flip else far).at[row]


CUT_ROWS = 96


def layer_copies(layout, place_ref, held, grad_refs, index, sems):
    is_out = index == FF // D
    if not layout[0]:
        target = grad_refs[1] if is_out else grad_refs[0].at[pl.ds(index * D, D), :]
        return run_copies([pltpu.make_async_copy(held, target, sems.at[0])])
    near, far, far_other = grad_refs
    copies = []

    def add(source, away, first, second, z, rows):
        at = (second, z, rows)
        target = near.at[(first, *at)] if not away else (far_other if first else far).at[at]
        copies.append(pltpu.make_async_copy(source, target, sems.at[len(copies)]))

    for away in range(2):
        core = place_ref[3] ^ away
        for first in range(2):
            for second in range(2):
                for half in range(2):
                    y, x = (first, second) if half else (second, first)
                    plane = (place_ref[1] ^ y) * 2 + (place_ref[2] ^ x)
                    if not is_out:
                        row = pl.multiple_of(plane * 192 + core * 96, 16)
                        block = held.at[pl.ds(row, 96), pl.ds(half * HALF, HALF)]
                        add(block, away, first, second, index, pl.ds(half * CUT_ROWS, 96))
                    elif half:
                        col = pl.multiple_of(core * HALF, 128)
                        for z in range(layout[1]):
                            row = pl.multiple_of((z * 4 + plane) * 48, 16)
                            add(held.at[pl.ds(row, 48), pl.ds(col, HALF)], away, first, second, z, pl.ds(192, 48))
    return run_copies(copies)


def piece_shapes(z_size, rows):
    piece = (2 * z_size, rows, HALF)
    return [jax.ShapeDtypeStruct((2, *piece), BF)] + [jax.ShapeDtypeStruct(piece, BF)] * 2


def layer(place_vec, o, x, cotangent, vec, b1, entries, buffers, z_size, n_heads):
    tokens = o.shape[0]
    n_copies = sum(len(e[1]) for e in entries) + 3 * buffers[-1].shape[0] if entries else 3
    tile = pl.BlockSpec((TILE, D), lambda t, p: (t, 0))
    wide = pl.BlockSpec((TILE, FF), lambda t, p: (t, 0))
    low, full = jax.ShapeDtypeStruct((tokens, D), BF), jax.ShapeDtypeStruct((tokens, D), F32)
    if entries:
        piece = (2, z_size, 240, HALF)
        grads = [jax.ShapeDtypeStruct((2, *piece), BF)] + [jax.ShapeDtypeStruct(piece, BF)] * 2
    else:
        grads = [jax.ShapeDtypeStruct((FF, D), BF), jax.ShapeDtypeStruct((D, D), BF)]
    return call(
        partial(layer_kernel, (entries, z_size, n_heads)),
        place_vec,
        (o, x, cotangent, vec, b1, *buffers),
        (),
        [whole((tokens, D)), own_tokens(tokens, tokens), tile, whole((8, D)), whole((1, FF))] + [ANY] * len(buffers),
        [tile, tile, tile, wide, tile, whole((8, D)), whole((1, FF))] + [ANY] * len(grads),
        [
            low, full, low, jax.ShapeDtypeStruct((tokens, FF), BF), low,
            jax.ShapeDtypeStruct((8, D), F32), jax.ShapeDtypeStruct((1, FF), F32), *grads,
        ],
        (tokens // TILE,),
        [
            pltpu.VMEM((D, D), BF),
            pltpu.VMEM((D, FF), BF),
            pltpu.VMEM((FF, D), BF),
            pltpu.VMEM((tokens, FF), BF),
            pltpu.VMEM((TILE, FF), F32),
            pltpu.VMEM((tokens, D), BF),
            pltpu.VMEM((tokens, D), BF),
            pltpu.VMEM((2, D, D), BF),
            pltpu.SemaphoreType.DMA((n_copies,)),
            pltpu.SemaphoreType.DMA((2, 32)),
            pltpu.VMEM((tokens, D), F32),
            pltpu.VMEM((tokens, 1), F32),
        ],
        tokens * D * (6 * D + 10 * FF),
        "layer",
    )


def small_vectors(sums, db1, vec_len, devices):
    rows = [sums[0:1, :]] + [db1[:, at : at + D] for at in range(0, FF, D)]
    rows += [sums[i : i + 1, :] for i in range(1, 6)]
    out = 0.0
    for index, row in enumerate(rows):
        owner = div_mod(counted((1, D), 1) + index * D, vec_len)[0]
        spread = jnp.where(counted((devices, D), 0) == owner, row, 0.0).astype(BF)
        lane = div_mod(counted((D, 1), 0) + index * D, vec_len)[1]
        out = out + dot_nn(spread, jnp.where(counted((D, HALF), 1) == lane, 1.0, 0.0).astype(BF))
    return out


def grad_up_kernel(layout, place_ref, yr_ref, sums_ref, db1_ref, dur_ref, *rest):
    if not layout[0]:
        rest[0][...] = dot_tn(yr_ref[...], dur_ref[...]).astype(BF)
        return
    *grad_refs, small_ref, held, sems = rest
    step = pl.program_id(0)

    def up(index):
        slot = index % 2
        away = 1 - index // 2
        made = []
        for flip in range(2):
            x = place_ref[2] ^ flip
            for row in range(2 * layout[1]):
                at = pl.multiple_of((row * 2 + x) * 48, 16)
                target = piece_target(grad_refs, away, flip, row)
                for part in range(2):
                    source = held.at[slot, pl.ds(at, 48), pl.ds(part * HALF, HALF)]
                    used = sems.at[slot, part, flip * 2 * layout[1] + row]
                    made.append(pltpu.make_async_copy(source, target.at[pl.ds((slot * 2 + part) * 48, 48), :], used))
        return made

    steps = FF // D
    for index in range(steps):

        @pl.when(step == index)
        def _():
            if index == 0:
                rows = small_vectors(sums_ref, db1_ref, layout[2], 2 * SMALL_ROWS)
                device = lax.broadcasted_iota(jnp.int32, rows.shape, 0)
                for x in range(2):
                    kept = jnp.where((device // 2) % 2 == x, rows, 0.0)
                    source = lax.broadcasted_iota(jnp.int32, (SMALL_ROWS, rows.shape[0]), 1)
                    target = lax.broadcasted_iota(jnp.int32, (SMALL_ROWS, rows.shape[0]), 0)
                    take = (source == (target // 2) * 4 + x * 2 + target % 2).astype(F32)
                    small_ref[x] = dot_nn(take.astype(BF), kept.astype(BF))
            if index >= 2:
                finish_copies(up(index - 2))
            held[index % 2] = dot_tn(yr_ref[...], dur_ref[...]).astype(BF)
            run_copies(up(index))
            if index == steps - 1:
                finish_copies(up(index - 1))
                finish_copies(up(index))


def grad_up(place_vec, yr, sums, db1, dur, entries, z_size, vec_len, after):
    tokens = yr.shape[0]
    if entries:
        shapes = piece_shapes(z_size, 192) + [jax.ShapeDtypeStruct((2, SMALL_ROWS, HALF), F32)]
        specs = [ANY] * 3 + [whole((2, SMALL_ROWS, HALF))]

        def columns(g, p):
            return (0, (p[3] ^ (1 - g // 2)) * 2 + g % 2)
    else:
        shapes = [jax.ShapeDtypeStruct((D, FF), BF)]
        specs = [pl.BlockSpec((D, D), lambda g, p: (0, g))]

        def columns(g, p):
            return (0, g)

    return call(
        partial(grad_up_kernel, (entries, z_size, vec_len)),
        place_vec,
        (yr, sums, db1, dur),
        after,
        [whole((tokens, D)), whole((8, D)), whole((1, FF)), pl.BlockSpec((tokens, D), columns)],
        specs,
        shapes,
        (FF // D,),
        [pltpu.VMEM((2, D, D), BF), pltpu.SemaphoreType.DMA((2, 2, 4 * z_size))] if entries else [],
        2 * tokens * D * FF,
        "grad_up",
    )


def input_grad_kernel(place_ref, base_ref, weight_ref, *rest):
    *grads, out_ref, done_ref = rest
    done_ref[...] = jnp.zeros_like(done_ref)
    total = base_ref[...]
    for flip in range(2):
        col = pl.multiple_of(((place_ref[2] % 2) ^ flip) * HALF, 128)
        for j in range(3):
            total = total + dot_nt(grads[flip * 3 + j][...], weight_ref[j, :, pl.ds(col, HALF)])
    out_ref[...] = total


def input_grad(place_vec, base, near, far, weight, after):
    tokens = base.shape[0]
    tile = pl.BlockSpec((TILE, D), lambda t, p: (t, 0))
    half = pl.BlockSpec((TILE, HALF), lambda t, p: (t, 0))
    return call(
        input_grad_kernel,
        place_vec,
        (base, weight, *near, *far),
        after,
        [tile, whole((3, D, D))] + [half] * 6,
        [tile, whole((8, 128))],
        [jax.ShapeDtypeStruct((tokens, D), F32), jax.ShapeDtypeStruct((8, 128), F32)],
        (tokens // TILE,),
        [],
        6 * tokens * D * D,
        "input_grad",
    )


def split_vector(vec_values):
    split_points = [D, D + FF, 2 * D + FF, 3 * D + FF, 4 * D + FF, 5 * D + FF]
    return jnp.split(vec_values, split_points)


def squares_kernel(place_ref, *refs):
    *parts, small_ref, out_ref = refs
    total = 0.0
    for ref in parts:
        value = ref[...]
        total = total + jnp.sum(jnp.sum(value * value, axis=0, keepdims=True), axis=1, keepdims=True)
    small = small_ref[...]
    total = total + jnp.sum(small * small, axis=1, keepdims=True)
    out_ref[...] = jnp.broadcast_to(total[None], out_ref.shape)


def sum_squares(place, place_vec, parts, small):
    operands = (*parts, small)
    shape = jax.ShapeDtypeStruct((place.total, 8, 128), F32)
    own = call(
        squares_kernel, place_vec, operands, (), [whole(w.shape) for w in operands], whole(shape.shape), shape,
        (1,), [], 1000, "squares",
    )
    return lax.all_to_all(own, AXES, split_axis=0, concat_axis=0, tiled=True)


def final_kernel(vec_len, place_ref, got_ref, *refs):
    *parts, sum_ref, vec_ref, bias_ref, out_ref, held = refs
    total = 0.0
    for entry in range(got_ref.shape[0]):
        total = total + got_ref[entry].astype(F32)
    for j in range(3):
        sum_ref[j] = total[j * 48 : (j + 1) * 48]
    held[...] = total[144:]
    small = held[pl.ds((place_ref[0] * 2 + place_ref[1]) * 2 + place_ref[3], 1), :]
    vec_ref[...] = small[:, :vec_len]
    bias_ref[...] = small[:, vec_len : vec_len + bias_ref.shape[1]]
    squares = jnp.sum(small * small, axis=1, keepdims=True)
    for value in [total[:144]] + [ref[...] for ref in parts]:
        squares = squares + jnp.sum(jnp.sum(value * value, axis=0, keepdims=True), axis=1, keepdims=True)
    out_ref[...] = jnp.broadcast_to(squares[None], out_ref.shape)


def final_sums(place, place_vec, pieces, parts, vec_len, bias_len, after):
    got = lax.all_to_all(pieces, "rows", split_axis=0, concat_axis=0, tiled=True)
    operands = (got, *parts)
    shapes = [(3, 48, HALF), (1, vec_len), (1, bias_len), (place.total, 8, 128)]
    *sums, own = call(
        partial(final_kernel, vec_len), place_vec, operands, after, [whole(w.shape) for w in operands],
        [whole(shape) for shape in shapes], [jax.ShapeDtypeStruct(shape, F32) for shape in shapes],
        (1,), [pltpu.VMEM((SMALL_ROWS, HALF), F32)], 1000, "final", 16 * 1024 * 1024,
    )
    return *sums, lax.all_to_all(own, AXES, split_axis=0, concat_axis=0, tiled=True)


def adam_kernel(rates, place_ref, squares_ref, *refs):
    count = len(rates)
    norm = jnp.sqrt(jnp.sum(squares_ref[...], axis=0)[0:1, 0:1])
    refs[5 * count][...] = norm
    clip_limit = CLIP_RMS * math.sqrt(PARAMS)
    factor = clip_limit / jnp.maximum(norm, clip_limit)
    for index, rate in enumerate(rates):
        weight, first, second, average, gradient = (refs[index * 5 + i][...] for i in range(5))
        clipped = gradient * factor.reshape((1,) * gradient.ndim)
        first_new = BETA_ONE * first + (1.0 - BETA_ONE) * clipped
        second_new = BETA_TWO * second + (1.0 - BETA_TWO) * clipped * clipped
        first_hat = first_new / (1.0 - BETA_ONE**STEP)
        second_hat = second_new / (1.0 - BETA_TWO**STEP)
        weight_new = weight - rate * (first_hat / (jnp.sqrt(second_hat) + ADAM_EPS) + WEIGHT_DECAY * weight)
        outs = refs[5 * count + 1 + index * 4 : 5 * count + 5 + index * 4]
        outs[0][...] = weight_new
        outs[1][...] = first_new
        outs[2][...] = second_new
        outs[3][...] = AVERAGE_KEEP * average + (1.0 - AVERAGE_KEEP) * weight_new


def adam(place_vec, squares, groups, rates):
    flat = [value for group in groups for value in group]
    shapes = [jax.ShapeDtypeStruct((1, 1), F32)]
    shapes += [jax.ShapeDtypeStruct(group[0].shape, F32) for group in groups for _ in range(4)]
    return call(
        partial(adam_kernel, rates), place_vec, (squares, *flat), (),
        [whole(value.shape) for value in (squares, *flat)], [whole(value.shape) for value in shapes], shapes,
        (1,), [], 1000, "adam",
    )


def body(
    tokens,
    cotangent,
    bucket,
    lengths,
    in_weight,
    in_first,
    in_second,
    in_average,
    in_bias,
    bias_first,
    bias_second,
    bias_average,
    out_weight,
    out_first,
    out_second,
    out_average,
    up_weight,
    up_first,
    up_second,
    up_average,
    down_weight,
    down_first,
    down_second,
    down_average,
    vectors,
    vec_first,
    vec_second,
    vec_average,
):
    place = Place()
    n_rows, n_heads, total = place.n_rows, place.n_heads, place.total
    z_size = place.sizes["z"]
    share = cotangent.shape[0]
    row_index, head_index = lax.axis_index("rows"), lax.axis_index("heads")
    blocks = share // CAP_L
    own_kinds = lax.dynamic_slice_in_dim(bucket, head_index * blocks, blocks, 0)
    own_lengths = lax.dynamic_slice_in_dim(lengths, head_index * blocks, blocks, 0)
    own_blocks = jnp.concatenate([own_kinds[:, None], own_lengths], axis=1).reshape(-1)
    place_vec = jnp.concatenate([jnp.stack([place.z, place.y, place.x, place.c]), own_blocks]).astype(jnp.int32)
    in_rows, in_cols = in_weight.shape[1], in_weight.shape[2]
    out_rows, down_rows = out_weight.shape[0], down_weight.shape[0]
    bias_len, vec_len = in_bias.size, vectors.size
    pieces_fit = in_rows == 96 and in_cols == HALF // 2 and out_rows == 24 and n_heads == 4

    small = jnp.concatenate([vectors, in_bias.reshape(-1)])
    if pieces_fit:
        piece, ffn_piece = make_pieces(
            place, place_vec, in_weight, out_weight, up_weight, down_weight, small[None, :]
        )
        entries = gather_pieces(place, piece)
        ffn_all = lax.all_gather(ffn_piece, AXES, axis=0)
        buffers = [entry[0] for entry in entries]
        layout = [(None,) + entry[1:] for entry in entries]
        in_buffers, layer_buffers = buffers, buffers + [ffn_all]
    else:
        layout = ()
        all_in = lax.all_gather(in_weight.astype(BF), "rows", axis=1, tiled=True)
        all_in = lax.all_gather(all_in, "heads", axis=2, tiled=True)
        all_out, all_up, all_down = (
            lax.all_gather(w.astype(BF), AXES, axis=0, tiled=True)
            for w in (out_weight, up_weight, down_weight)
        )
        layer_buffers = [all_out, all_up, all_down]
        all_small = lax.all_gather(small.astype(BF), AXES, axis=0).astype(F32)
        bias_out, bias_up, bias_down, gain_one, shift_one, gain_two, shift_two = split_vector(
            all_small[:, :vec_len].reshape(-1)
        )
        bias_shape = (n_rows, n_heads) + in_bias.shape
        bias_all = all_small[:, vec_len:].reshape(bias_shape).transpose(2, 1, 3, 0, 4).reshape(2, D)
        bias_in = jnp.stack([bias_all[0], jnp.zeros_like(bias_all[0]), bias_all[1]])[:, None, :]
        vec_rows = jnp.stack([bias_out, bias_down, gain_one, shift_one, gain_two, shift_two, bias_out, bias_out])
        in_buffers = [all_in, bias_in]

    q, k, v, o, lse, *small_rows = attend(
        place_vec, tokens, share, layout, in_buffers, z_size, vec_len, n_rows
    )
    vec_rows, b1, all_in = small_rows if pieces_fit else (vec_rows, bias_up[None, :], all_in)
    layer_out, dr1, yr, dur, dor, sums, db1, *grads_down = layer(
        place_vec, o, tokens, cotangent, vec_rows, b1, layout, layer_buffers, z_size, n_heads
    )

    def back(vec, flip, *after):
        return attend_back(
            place_vec, q, k, v, dor, lse, tokens, vec, vec_len, z_size, pieces_fit, flip, after
        )

    if pieces_fit:
        down_near, down_far, down_far_first = grads_down
        parts = (slice(0, CUT_ROWS), slice(CUT_ROWS, None))
        down_c = place.send(down_far_first, "c")
        down_go = [low_sum(down_near[1, :, :, part], down_c[:, :, part]) for part in parts]
        got_first = [place.send(part, digit) for part, digit in zip(down_go, "xy")]
        down_c = place.send(down_far, "c")
        up_near, up_far, up_far_x, vec_small = grad_up(
            place_vec, yr, sums, db1, dur, layout, z_size, vec_len, tuple(down_go)
        )

        def down_terms(index, flip):
            part = parts[index]
            return down_near[0, flip, :, part], down_c[flip, :, part], got_first[index][flip]

        down_next = [low_sum(*down_terms(index, 1)) for index in range(2)]
        got_second = [place.send(part, digit) for part, digit in zip(down_next, "yx")]
        up_far_x = gate(place_vec, up_far_x, tuple(down_next))
        up_x = low_sum(up_near[1], place.send(up_far_x, "c"))
        got_up_x = place.send(up_x, "x")
        up_c = place.send(up_far, "c")
        down = jnp.concatenate([low_sum(*down_terms(index, 0), got_second[index]) for index in range(2)], axis=1)
        down_sums = trade(place, down, "z")
        other = back(vec_small, 1, up_x, down)

        far_c = place.send(other[4], "c")
        far_x = low_sum(other[3], far_c)
        got_far_x = place.send(far_x, "x")
        up = low_sum(up_near[0], up_c, got_up_x)
        up_sums = trade(place, up, "zy")
        mine = back(vec_small, 0, far_x, up, down_sums)

        near_c = place.send(mine[4], "c")
        near = low_sum(mine[3], near_c, got_far_x)
        token_grad, done = input_grad(place_vec, dr1, mine[:3], other[:3], all_in, (near,))

        in_sum, sum_vec, sum_bias, squares = final_sums(
            place, place_vec, near, (down_sums, up_sums), vec_len, bias_len, (done,)
        )
        sum_down = jnp.concatenate([down_sums[:96], down_sums[96:192]], axis=1)
        sum_up = jnp.concatenate([up_sums[at : at + 48] for at in range(0, 192, 48)], axis=1)
        sum_up = swap_halves(place, sum_up, 0, 1)
        sum_out = swap_halves(place, down_sums[192:], 0, 1)
        sum_in = swap_halves(place, in_sum, 2, 1)
        sum_bias = sum_bias.reshape(in_bias.shape)
    else:
        def spread(value):
            return lax.psum_scatter(value, AXES, scatter_dimension=0, tiled=True).astype(F32)

        def join(far, near, axis):
            return jnp.where(
                place.x == 0, jnp.concatenate([near, far], axis=axis), jnp.concatenate([far, near], axis=axis)
            )

        grads_up = grad_up(place_vec, yr, sums, db1, dur, layout, z_size, vec_len, ())
        unused = jnp.zeros((2, SMALL_ROWS, HALF), F32)
        grad_vec = jnp.concatenate([sums[0], db1[0], *(sums[i] for i in range(1, 6))])
        other, mine = back(unused, 1), back(unused, 0)
        token_grad, _ = input_grad(place_vec, dr1, mine[:3], other[:3], all_in, ())
        grad_in = join(other[3], mine[3], 2)
        sum_in = lax.psum_scatter(grad_in, "heads", scatter_dimension=2, tiled=True)
        sum_in = lax.psum_scatter(sum_in, "rows", scatter_dimension=1, tiled=True).astype(F32)
        sum_up, sum_out, sum_down = spread(grads_up[0]), spread(grads_down[1]), spread(grads_down[0])
        sum_vec = lax.psum_scatter(grad_vec, AXES, scatter_dimension=0, tiled=True)
        grad_bias = join(other[4], mine[4], 1).reshape(2, n_heads * in_bias.shape[1], -1)
        sum_bias = lax.psum_scatter(grad_bias, "heads", scatter_dimension=1, tiled=True)
        sum_bias = lax.psum_scatter(sum_bias, "rows", scatter_dimension=2, tiled=True)

        flat_small = jnp.concatenate([sum_vec, sum_bias.reshape(-1)])[None, :]
        parts = (sum_in.reshape(-1, in_cols), sum_out, sum_up, sum_down)
        squares = sum_squares(place, place_vec, parts, flat_small)
    row = (1, vec_len)
    grad_norm, *new = adam(
        place_vec,
        squares,
        (
            (in_weight, in_first, in_second, in_average, sum_in),
            tuple(v.transpose(1, 0, 2) for v in (in_bias, bias_first, bias_second, bias_average, sum_bias)),
            (out_weight, out_first, out_second, out_average, sum_out),
            (up_weight, up_first, up_second, up_average, sum_up),
            (down_weight, down_first, down_second, down_average, sum_down),
            tuple(value.reshape(row) for value in (vectors, vec_first, vec_second, vec_average, sum_vec)),
        ),
        (LEARN_RATE,) * 5 + (VECTOR_RATE,),
    )
    return (
        layer_out,
        token_grad,
        grad_norm[0, 0],
        *new[:4],
        *(value.transpose(1, 0, 2) for value in new[4:8]),
        *new[8:20],
        *(value.reshape(vec_len) for value in new[20:]),
    )


def solution(mesh):
    in_specs = (
        P("rows", None),
        P(("rows", "heads"), None),
        P("rows"),
        P("rows", None),
        P(None, "rows", "heads"),
        P(None, "rows", "heads"),
        P(None, "rows", "heads"),
        P(None, "rows", "heads"),
        P(None, "heads", "rows"),
        P(None, "heads", "rows"),
        P(None, "heads", "rows"),
        P(None, "heads", "rows"),
        P(("rows", "heads"), None),
        P(("rows", "heads"), None),
        P(("rows", "heads"), None),
        P(("rows", "heads"), None),
        P(("rows", "heads"), None),
        P(("rows", "heads"), None),
        P(("rows", "heads"), None),
        P(("rows", "heads"), None),
        P(("rows", "heads"), None),
        P(("rows", "heads"), None),
        P(("rows", "heads"), None),
        P(("rows", "heads"), None),
        P(("rows", "heads")),
        P(("rows", "heads")),
        P(("rows", "heads")),
        P(("rows", "heads")),
    )
    out_specs = (
        P(("rows", "heads"), None),
        P(("rows", "heads"), None),
        P(),
        P(None, "rows", "heads"),
        P(None, "rows", "heads"),
        P(None, "rows", "heads"),
        P(None, "rows", "heads"),
        P(None, "heads", "rows"),
        P(None, "heads", "rows"),
        P(None, "heads", "rows"),
        P(None, "heads", "rows"),
        P(("rows", "heads"), None),
        P(("rows", "heads"), None),
        P(("rows", "heads"), None),
        P(("rows", "heads"), None),
        P(("rows", "heads"), None),
        P(("rows", "heads"), None),
        P(("rows", "heads"), None),
        P(("rows", "heads"), None),
        P(("rows", "heads"), None),
        P(("rows", "heads"), None),
        P(("rows", "heads"), None),
        P(("rows", "heads"), None),
        P(("rows", "heads")),
        P(("rows", "heads")),
        P(("rows", "heads")),
        P(("rows", "heads")),
    )
    return jax.shard_map(body, mesh=mesh, in_specs=in_specs, out_specs=out_specs, check_vma=False)
```
